128 devices in a mesh: ctx: 64 (over y, x, z_lo, core), fsdp: 2 (over z_hi).
Axes of the slice: x: 4, y: 4, z: 4 (z_hi: 2, z_lo: 2; z = z_hi * 2 + z_lo), core: 2. Of those that a mesh axis runs over, the one named last changes fastest.
Arguments:
- tokens: bfloat16 [2, 8192, 1024], P('fsdp', 'ctx'), may hold values from -6 to 6
- doc_lengths: int32 [2, 3], P('fsdp'), may hold values from 1 to 8064, as said below
- query_weight: bfloat16 [1024, 2048], P('fsdp'), may hold values from -0.1875 to 0.1875
- key_weight: bfloat16 [1024, 1024], P('fsdp'), may hold values from -0.1875 to 0.1875
- value_weight: bfloat16 [1024, 1024], P('fsdp'), may hold values from -0.1875 to 0.1875
- out_weight: bfloat16 [2048, 1024], P('fsdp'), may hold values from -0.125 to 0.125
- gate_weight: bfloat16 [1024, 3072], P('fsdp'), may hold values from -0.1875 to 0.1875
- up_weight: bfloat16 [1024, 3072], P('fsdp'), may hold values from -0.1875 to 0.1875
- down_weight: bfloat16 [3072, 1024], P('fsdp'), may hold values from -0.109375 to 0.109375
- query_gain: bfloat16 [2048], P('fsdp'), may hold values from 0.25 to 1.75
- key_gain: bfloat16 [1024], P('fsdp'), may hold values from 0.25 to 1.75
- attn_gain: bfloat16 [1024], P('fsdp'), may hold values from 0.25 to 1.75
- ffn_gain: bfloat16 [1024], P('fsdp'), may hold values from 0.25 to 1.75
- cotangent: bfloat16 [2, 8192, 1024], P('fsdp', 'ctx'), may hold values from -6 to 6
Outputs:
- output: bfloat16 [2, 8192, 1024], P('fsdp', 'ctx')
- tokens_grad: float32 [2, 8192, 1024], P('fsdp', 'ctx')
- query_weight_grad: float32 [1024, 2048], P('fsdp')
- key_weight_grad: float32 [1024, 1024], P('fsdp')
- value_weight_grad: float32 [1024, 1024], P('fsdp')
- out_weight_grad: float32 [2048, 1024], P('fsdp')
- gate_weight_grad: float32 [1024, 3072], P('fsdp')
- up_weight_grad: float32 [1024, 3072], P('fsdp')
- down_weight_grad: float32 [3072, 1024], P('fsdp')
- query_gain_grad: float32 [2048], P('fsdp')
- key_gain_grad: float32 [1024], P('fsdp')
- attn_gain_grad: float32 [1024], P('fsdp')
- ffn_gain_grad: float32 [1024], P('fsdp')
The draws below stay inside these ranges and needn't reach their ends.
Inputs may be any that keep to these rules, and one draw needn't show every extreme that they name: `doc_lengths`: each row holds three document lengths in order; the middle one is 8064 and the outer two sum to 128.
All inputs are finite; a program needn't handle non-finite values.
Results may differ from the reference program's by a relative error of at most 0.035.
Values may be sent and summed in bfloat16 or wider, within the bound.
No kernel may reach another device: no remote copies, remote signals or barrier semaphores. Data moves between devices by JAX's collectives and lax.ppermute only.
A program may use at most 384 MiB of HBM per device.

```python
import math
import jax
import jax.numpy as jnp
from jax import lax

D = 1024
HEADS = 16
KVH = 8
HD = 128
FF = 3072
BLK = 128
HQ = 2048
HK = 1024
SEQ = 8192
SEQS = 2


def draw_doc_lengths(key, part):
    key = jax.random.fold_in(key, 7)
    leading = jax.random.randint(key, (SEQS,), 1, BLK, dtype=jnp.int32)
    middle = jnp.full((SEQS,), SEQ - BLK, jnp.int32)
    return jnp.stack([leading, middle, BLK - leading], axis=1)


def shard_levels(rng, dims, split, least, high):
    factor_of, own = 1.0, jax.random.fold_in(rng, 6)
    for position, shards_of in split:
        heights = jnp.exp(jax.random.uniform(jax.random.fold_in(own, position), (shards_of,), jnp.float32, least / len(split), high / len(split)))
        factor_of = factor_of * jnp.repeat(heights, dims[position] // shards_of).reshape([-1 if axis == position else 1 for axis in range(len(dims))])
    return factor_of


def gaussian(stream_key, shape, deviation, reach, cuts=(), held_as=jnp.bfloat16):
    entries = jax.random.normal(stream_key, shape, jnp.float32) * deviation
    if len(cuts) > 0:
        entries = shard_levels(stream_key, shape, cuts, -0.22, 0.18) * entries
    return jnp.clip(entries, min=-reach, max=reach).astype(held_as)


def setup_inputs(seed: int = 0) -> dict:
    keys = jax.random.split(jax.random.key(seed), 15)
    tokens = gaussian(keys[0], (SEQS, SEQ, D), 1.0, 6.0, ((0, 2), (1, 64)))
    doc_lengths = draw_doc_lengths(jax.random.fold_in(keys[14], 71), 0)
    query_weight = gaussian(keys[2], (D, HQ), D ** -0.5, 0.1875, ((0, 2),))
    key_weight = gaussian(keys[3], (D, HK), D ** -0.5, 0.1875, ((0, 2),))
    value_weight = gaussian(keys[4], (D, HK), D ** -0.5, 0.1875, ((0, 2),))
    out_weight = gaussian(keys[5], (HQ, D), HQ ** -0.5, 0.125, ((0, 2),))
    gate_weight = gaussian(keys[6], (D, FF), D ** -0.5, 0.1875, ((0, 2),))
    up_weight = gaussian(keys[7], (D, FF), D ** -0.5, 0.1875, ((0, 2),))
    down_weight = gaussian(keys[8], (FF, D), FF ** -0.5, 0.109375, ((0, 2),))
    query_gain = jnp.clip(1.0 + 0.15 * jax.random.normal(keys[9], (HQ,), jnp.float32), 0.25, 1.75).astype(jnp.bfloat16)
    key_gain = jnp.clip(1.0 + 0.15 * jax.random.normal(keys[10], (HK,), jnp.float32), 0.25, 1.75).astype(jnp.bfloat16)
    attn_gain = jnp.clip(1.0 + 0.15 * jax.random.normal(keys[11], (D,), jnp.float32), 0.25, 1.75).astype(jnp.bfloat16)
    ffn_gain = jnp.clip(1.0 + 0.15 * jax.random.normal(keys[12], (D,), jnp.float32), 0.25, 1.75).astype(jnp.bfloat16)
    cotangent = gaussian(keys[13], (SEQS, SEQ, D), 1.0, 6.0, ((0, 2), (1, 64)))
    return {"tokens": tokens, "doc_lengths": doc_lengths, "query_weight": query_weight, "key_weight": key_weight, "value_weight": value_weight, "out_weight": out_weight, "gate_weight": gate_weight, "up_weight": up_weight, "down_weight": down_weight, "query_gain": query_gain, "key_gain": key_gain, "attn_gain": attn_gain, "ffn_gain": ffn_gain, "cotangent": cotangent}


epsilon = 1e-06
rope_base = 1000000.0
masked_score = -1e+30

@jax.custom_vjp
def low(v):
    return lax.optimization_barrier(v.astype(jnp.bfloat16)).astype(jnp.float32)

@jax.custom_vjp
def low_back(v):
    return v

def low_keep(v):
    return (low(v), None)

def low_pass(kept, grad):
    return (grad,)

def back_keep(v):
    return (v, None)

def back_low(kept, grad):
    return (low(grad),)
low.defvjp(low_keep, low_pass)
low_back.defvjp(back_keep, back_low)

def matmul(left_op, right_op):
    return jnp.dot(left_op, right_op, precision=lax.Precision.HIGHEST, preferred_element_type=jnp.float32)

def rms_norm(tensor, gain_vec):
    return tensor * lax.rsqrt(lax.optimization_barrier(jnp.mean(tensor * tensor, axis=-1, keepdims=True)) + epsilon) * gain_vec

def rotate(tensor, cosine, sine_table):
    half_size = tensor.shape[-1] // 2
    first_half = tensor[..., :half_size]
    second = tensor[..., half_size:]
    return jnp.concatenate([first_half * cosine - second * sine_table, second * cosine + first_half * sine_table], axis=-1)

def stored_positions(stored, block_rows, total_rows):
    half_rows = block_rows // 2
    shard = stored // block_rows
    within = stored % block_rows
    return jnp.where(within < half_rows, shard * half_rows + within, total_rows - (shard + 2) * half_rows + within).astype(jnp.int32)

def sequence_layer(source, lengths, parameters):
    query_weight, key_weight, value_weight, out_weight, gate_weight, up_weight, down_weight, query_gain, key_gain, attn_gain, ffn_gain = parameters
    length = source.shape[0]
    group_size = HEADS // KVH
    positions = stored_positions(jnp.arange(length, dtype=jnp.int32), BLK, length)
    first_end = lengths[0]
    second_end = lengths[0] + lengths[1]
    doc_ids = (positions >= first_end).astype(jnp.int32) + (positions >= second_end).astype(jnp.int32)
    doc_start = jnp.where(doc_ids == 0, 0, jnp.where(doc_ids == 1, first_end, second_end))
    places = positions - doc_start
    half_size = HD // 2
    frequency = jnp.power(jnp.float32(rope_base), -jnp.arange(half_size, dtype=jnp.float32) * (2.0 / HD))
    angles = places.astype(jnp.float32)[:, None] * frequency[None, :]
    cosine = jnp.cos(angles)[:, None, :]
    sine_table = jnp.sin(angles)[:, None, :]
    query_raw = low_back(matmul(source, query_weight))
    key_raw = low_back(matmul(source, key_weight))
    value_raw = matmul(source, value_weight)
    queries = low(rotate(rms_norm(query_raw, query_gain).reshape(length, HEADS, HD), cosine, sine_table))
    queries = queries.reshape(length, KVH, group_size, HD)
    key_rows = low(rotate(rms_norm(key_raw, key_gain).reshape(length, KVH, HD), cosine, sine_table))
    values = low(low_back(value_raw)).reshape(length, KVH, HD)
    scaling = HD ** (-0.5)
    block_rows = math.gcd(length, 512)
    blocks = length // block_rows

    def one_block(inputs):
        query_block, query_pos, query_doc = inputs
        scores = low_back(jnp.einsum('qhgd,khd->qhgk', query_block, key_rows, precision=lax.Precision.HIGHEST) * scaling)
        allowed = ((query_doc[:, None] == doc_ids[None, :]) & (positions[None, :] <= query_pos[:, None]))[:, None, None, :]
        scores = jnp.where(allowed, scores, masked_score)
        maximum = lax.optimization_barrier(jnp.max(scores, axis=-1, keepdims=True))
        weights = jnp.where(allowed, jnp.exp(scores - maximum), 0.0)
        probabilities = weights / lax.optimization_barrier(jnp.sum(weights, axis=-1, keepdims=True))
        return jnp.einsum('qhgk,khd->qhgd', low(probabilities), values, precision=lax.Precision.HIGHEST)
    attended = lax.map(jax.checkpoint(one_block), (queries.reshape(blocks, block_rows, KVH, group_size, HD), positions.reshape(blocks, block_rows), doc_ids.reshape(blocks, block_rows)))
    attended = low(low_back(attended.reshape(length, HQ)))
    mixed_out = low_back(matmul(attended, out_weight))
    hidden = source + rms_norm(mixed_out, attn_gain)
    hidden_low = low(hidden)
    gate_act = low_back(matmul(hidden_low, gate_weight))
    up_act = low_back(matmul(hidden_low, up_weight))
    inner_act = low(jax.nn.silu(gate_act) * up_act)
    down_out = low_back(matmul(inner_act, down_weight))
    return hidden + rms_norm(down_out, ffn_gain)

def reference(tokens, doc_lengths, query_weight, key_weight, value_weight, out_weight, gate_weight, up_weight, down_weight, query_gain, key_gain, attn_gain, ffn_gain, cotangent):
    parameters = tuple((weight_arg.astype(jnp.float32) for weight_arg in (query_weight, key_weight, value_weight, out_weight, gate_weight, up_weight, down_weight, query_gain, key_gain, attn_gain, ffn_gain)))

    def forward(source_all, parameter_set):
        return lax.map(lambda sequence_item: sequence_layer(sequence_item[0], sequence_item[1], parameter_set), (source_all, doc_lengths))
    output, pullback = jax.vjp(forward, tokens.astype(jnp.float32), parameters)
    tokens_grad, parameter_grads = pullback(cotangent.astype(jnp.float32))
    return (output.astype(jnp.bfloat16), tokens_grad, parameter_grads[0], parameter_grads[1], parameter_grads[2], parameter_grads[3], parameter_grads[4], parameter_grads[5], parameter_grads[6], parameter_grads[7], parameter_grads[8], parameter_grads[9], parameter_grads[10])
```

```python
import functools
import math

import jax
import jax.numpy as jnp
from jax import lax
from jax.experimental import pallas as pl
from jax.experimental.pallas import tpu as pltpu
from jax.sharding import Mesh
from jax.sharding import PartitionSpec as P

D = 1024
HEADS = 16
KVH = 8
HD = 128
FF = 3072
BLK = 128
HQ = 2048
HK = 1024
SEQ = 8192

epsilon = 1e-06
rope_base = 1000000.0
masked_score = -1e30
score_scale = HD**-0.5
log2_scale = score_scale * math.log2(math.e)
half_blk = BLK // 2
group_rows = 8 * half_blk

bf16 = jnp.bfloat16
f32 = jnp.float32

TOKEN_AXES = ("y", "x", "zl", "co")
HEAD_AXES = ("x", "zl")
HEAD_LINKS = ("x0", "x1", "zA")

edge_a = [(0, 1), (1, 0), (2, 3), (3, 2)]
edge_b = [(1, 2), (2, 1), (3, 0), (0, 3)]
swap = [(0, 1), (1, 0)]
LINKS = {
    "x0": ("x", edge_a),
    "x1": ("x", edge_b),
    "y0": ("y", edge_a),
    "y1": ("y", edge_b),
    "zA": ("zl", swap),
    "zB": (("zl", "zh"), [(0, 3), (3, 0), (1, 2), (2, 1)]),
    "co": ("co", swap),
    "zh": ("zh", swap),
}


def link_bit(link):
    if link in ("x0", "y0"):
        place = lax.axis_index(link[0])
        return ((place == 1) | (place == 2)).astype(jnp.int32)
    if link in ("x1", "y1"):
        return (lax.axis_index(link[0]) >= 2).astype(jnp.int32)
    if link == "zA":
        return lax.axis_index("zl") ^ lax.axis_index("zh")
    if link == "zB":
        return lax.axis_index("zh")
    return lax.axis_index(link)


def across(array, link):
    axis, pairs = LINKS[link]
    return lax.ppermute(array, axis, pairs)


def dot_plain(left_op, right_op):
    return jnp.dot(left_op, right_op, preferred_element_type=f32)


def dot_second(left_op, right_op):
    return lax.dot_general(
        left_op, right_op, (((1,), (1,)), ((), ())), preferred_element_type=f32
    )


def dot_first(left_op, right_op):
    return lax.dot_general(
        left_op, right_op, (((0,), (0,)), ((), ())), preferred_element_type=f32
    )


def rms_forward(tensor, gain_vec):
    inverse = lax.rsqrt(jnp.mean(tensor * tensor, axis=-1, keepdims=True) + epsilon)
    normed = tensor * inverse
    return (normed * gain_vec.astype(f32), normed, inverse)


def rms_backward(upstream, gain_vec, normed, inverse):
    scaled = upstream * gain_vec.astype(f32)
    gain_grad = jnp.sum(upstream * normed, axis=0)
    tensor_grad = inverse * (scaled - normed * jnp.mean(scaled * normed, axis=-1, keepdims=True))
    return (tensor_grad, gain_grad)


def halve(array, link):
    rows = array.shape[0] // 2
    bit = link_bit(link)
    sent = lax.dynamic_slice_in_dim(array, (1 - bit) * rows, rows, 0)
    kept = lax.dynamic_slice_in_dim(array, bit * rows, rows, 0)
    got = across(sent, link)
    return (kept.astype(f32) + got.astype(f32)).astype(bf16)


def double(array, link):
    got = across(array, link)
    return jnp.where(
        link_bit(link) == 0, jnp.concatenate([array, got]), jnp.concatenate([got, array])
    )


def double_in_place(array, link, axis=0):
    got = across(array, link)
    bit = {
        "x0": lambda: lax.axis_index("x") % 2,
        "x1": lambda: lax.axis_index("x") // 2,
        "zA": lambda: lax.axis_index("zl"),
    }[link]()
    return jnp.where(
        bit == 0,
        jnp.concatenate([array, got], axis=axis),
        jnp.concatenate([got, array], axis=axis),
    )


def sum_over(array, links):
    for link in links:
        array = array + across(array, link)
    return array


def high_low(values):
    high = values.astype(bf16)
    return jnp.stack([high, (values - high.astype(f32)).astype(bf16)])


def rotate(tensor, cosine, sine_table):
    half_size = HD // 2
    first_half = tensor[..., :half_size]
    second = tensor[..., half_size:]
    return jnp.concatenate(
        [first_half * cosine - second * sine_table, second * cosine + first_half * sine_table],
        axis=-1,
    )


def half_positions(index, y, co, half):
    block = 16 * y + 2 * (index // half_blk) + co
    inner = index % half_blk
    return jnp.where(half == 0, block * half_blk + inner, SEQ - (block + 1) * half_blk + inner)


def query_masks(info_ref, half):
    y, co, first_end, second_end = info_ref[0], info_ref[1], info_ref[2], info_ref[3]
    index = lax.broadcasted_iota(jnp.int32, (1, group_rows), 1)
    position = half_positions(index, y, co, half)
    start = jnp.where(position >= second_end, second_end, 0)
    start = jnp.where((position >= first_end) & (position < second_end), first_end, start)
    return position, start, position >= second_end


def pair_mask(group, key_half, query_pos, query_start):
    index = lax.broadcasted_iota(jnp.int32, (group_rows, 1), 0)
    key_pos = half_positions(index, group // 2, group % 2, key_half)
    return (key_pos >= query_start) & (key_pos <= query_pos)


def open_steps(y, half):
    count = jnp.where(half == 0, jnp.maximum(2 * y - 2, 0), 6 + 6 - 2 * y)

    def chunk(step):
        late = step >= 6
        group = jnp.where(late, step - 6 + 2 * y + 2, step + 2)
        return group, jnp.where(late, 1, 0)

    return count, chunk


def masked_steps(y, half):
    count = jnp.where((half == 0) & (y == 0), 2, 4)

    def chunk(step):
        own = step >= 2
        group = jnp.where(own, 2 * y + step - 2, step)
        return group, jnp.where(own, half, 0)

    return count, chunk


def slot_of(group, key_half, y, co):
    other_y = group // 2
    beside = (other_y ^ 1) == y
    across_ring = (3 - other_y) == y
    first = jnp.where(key_half == 0, beside, across_ring)
    second = jnp.where(key_half == 0, across_ring, beside)
    ring = jnp.where(other_y == y, 0, jnp.where(first, 1, jnp.where(second, 2, 3)))
    return (group % 2) ^ co, key_half, ring


def load_chunks(pieces, kvs, sems):
    copies = []
    for number, piece in enumerate(pieces):
        core, rest = divmod(number, 4)
        half, pair = divmod(rest, 2)
        copies.append(
            pltpu.make_async_copy(piece, kvs.at[core, half, pl.ds(2 * pair, 2)], sems.at[number])
        )
    for copy in copies:
        copy.start()
    return copies


def forward_kernel(info_ref, query_ref, *refs):
    pieces, (low_ref, full_ref, total_ref), (kvs, sems, qt, top, denom, acc) = (
        refs[:8],
        refs[8:11],
        refs[11:],
    )
    y, co = info_ref[0], info_ref[1]
    for copy in load_chunks(pieces, kvs, sems):
        copy.wait()

    def half_body(half, carry):
        query_pos, query_start, last_doc = query_masks(info_ref, half)
        for head in range(2):
            lanes = slice(head * HD, (head + 1) * HD)
            qt[head] = query_ref[half, :, lanes].astype(f32).T.astype(bf16)
            top[head] = jnp.full((1, group_rows), masked_score, f32)
            denom[head] = jnp.zeros((1, group_rows), f32)
            acc[head] = jnp.zeros((HD, group_rows), f32)

        def step(group, key_half, masked):
            slot = slot_of(group, key_half, y, co)
            keys = kvs[(*slot, slice(None), slice(0, HD))]
            values = kvs[(*slot, slice(None), slice(HD, 2 * HD))]
            if masked:
                mask = pair_mask(group, key_half, query_pos, query_start)
            for head in range(2):
                scores = dot_plain(keys, qt[head])
                if masked:
                    scores = jnp.where(mask, scores, masked_score)
                old_top = top[head]
                new_top = jnp.maximum(old_top, jnp.max(scores, axis=0, keepdims=True))
                weights = jnp.exp2(scores - new_top)
                rescale = jnp.exp2(old_top - new_top)
                denom[head] = denom[head] * rescale + jnp.sum(weights, axis=0, keepdims=True)
                acc[head] = acc[head] * rescale + dot_first(values, weights.astype(bf16))
                top[head] = new_top

        count, chunk = open_steps(y, half)

        def open_body(number, inner):
            step(*chunk(number), False)
            return inner

        lax.fori_loop(0, count, open_body, 0)
        for head in range(2):
            top[head] = jnp.where(last_doc, masked_score, top[head])
            denom[head] = jnp.where(last_doc, 0.0, denom[head])
            acc[head] = jnp.where(last_doc, 0.0, acc[head])
        masked_count, masked_chunk = masked_steps(y, half)

        def masked_body(number, inner):
            step(*masked_chunk(number), True)
            return inner

        lax.fori_loop(0, masked_count, masked_body, 0)
        for head in range(2):
            lanes = slice(head * HD, (head + 1) * HD)
            attended = acc[head] / denom[head]
            full_ref[half, head] = attended
            total_ref[half, head] = top[head] + jnp.log2(denom[head])
            rows = attended.T.astype(bf16)
            for owner in range(8):
                low_ref[owner, half, :, lanes] = rows[owner * half_blk : (owner + 1) * half_blk]
        return carry

    lax.fori_loop(0, 2, half_body, 0)


def backward_kernel(info_ref, query_ref, grad_ref, full_ref, total_ref, *refs):
    pieces, (dq_ref, sent_ref, kept_ref), (kvs, sems, qt, gt, delta, dqt, dkv) = (
        refs[:8],
        refs[8:11],
        refs[11:],
    )
    y, co = info_ref[0], info_ref[1]
    copies = load_chunks(pieces, kvs, sems)
    dkv[...] = jnp.zeros_like(dkv)
    for copy in copies:
        copy.wait()

    def half_body(half, carry):
        query_pos, query_start, last_doc = query_masks(info_ref, half)
        for head in range(2):
            lanes = slice(head * HD, (head + 1) * HD)
            qt[head] = query_ref[half, :, lanes].astype(f32).T.astype(bf16)
            grad_t = grad_ref[half, :, lanes].astype(f32).T
            gt[head] = grad_t.astype(bf16)
            delta[head] = jnp.sum(grad_t * full_ref[half, head], axis=0, keepdims=True)
            dqt[head] = jnp.zeros((HD, group_rows), f32)

        def step(group, key_half, masked):
            slot = slot_of(group, key_half, y, co)
            key_lanes = (*slot, slice(None), slice(0, HD))
            value_lanes = (*slot, slice(None), slice(HD, 2 * HD))
            keys = kvs[key_lanes]
            values = kvs[value_lanes]
            if masked:
                mask = pair_mask(group, key_half, query_pos, query_start)
            key_total = dkv[key_lanes]
            value_total = dkv[value_lanes]
            for head in range(2):
                lanes = slice(head * HD, (head + 1) * HD)
                scores = dot_plain(keys, qt[head])
                total = total_ref[half, head]
                if masked:
                    scores = jnp.where(mask, scores, masked_score)
                else:
                    total = jnp.where(last_doc, -masked_score, total)
                probs = jnp.exp2(scores - total)
                value_total += dot_plain(probs.astype(bf16), grad_ref[half, :, lanes])
                prob_grad = dot_plain(values, gt[head])
                low = (probs * (prob_grad - delta[head])).astype(bf16)
                key_total += dot_plain(low, query_ref[half, :, lanes])
                dqt[head] += dot_first(keys, low)
            dkv[key_lanes] = key_total
            dkv[value_lanes] = value_total

        count, chunk = open_steps(y, half)

        def open_body(number, inner):
            step(*chunk(number), False)
            return inner

        lax.fori_loop(0, count, open_body, 0)
        masked_count, masked_chunk = masked_steps(y, half)

        def masked_body(number, inner):
            step(*masked_chunk(number), True)
            return inner

        lax.fori_loop(0, masked_count, masked_body, 0)
        for head in range(2):
            lanes = slice(head * HD, (head + 1) * HD)
            dq_ref[half, :, lanes] = dqt[head].T * score_scale
        return carry

    lax.fori_loop(0, 2, half_body, 0)

    def store_body(number, carry):
        half, ring = number // 4, number % 4
        for core, ref in enumerate((kept_ref, sent_ref)):
            ref[half, ring, :, :HD] = (dkv[core, half, ring, :, :HD] * math.log(2.0)).astype(bf16)
            ref[half, ring, :, HD:] = dkv[core, half, ring, :, HD:].astype(bf16)
        return carry

    lax.fori_loop(0, 8, store_body, 0)


smem = pl.BlockSpec(memory_space=pltpu.SMEM)
vmem = pl.BlockSpec(memory_space=pltpu.VMEM)
anywhere = pl.BlockSpec(memory_space=pl.ANY)
PAIRS = 4 * 2 * group_rows * 9 * group_rows
CHUNKS = (2, 2, 4, group_rows, 2 * HD)


def attention_forward(info, queries, pieces):
    return pl.pallas_call(
        forward_kernel,
        name="attention_forward",
        out_shape=(
            jax.ShapeDtypeStruct((8, 2, half_blk, 2 * HD), bf16),
            jax.ShapeDtypeStruct((2, 2, HD, group_rows), f32),
            jax.ShapeDtypeStruct((2, 2, 1, group_rows), f32),
        ),
        in_specs=[smem, vmem] + [anywhere] * 8,
        out_specs=[vmem] * 3,
        scratch_shapes=[
            pltpu.VMEM(CHUNKS, bf16),
            pltpu.SemaphoreType.DMA((8,)),
            pltpu.VMEM((2, HD, group_rows), bf16),
            pltpu.VMEM((2, 1, group_rows), f32),
            pltpu.VMEM((2, 1, group_rows), f32),
            pltpu.VMEM((2, HD, group_rows), f32),
        ],
        compiler_params=pltpu.CompilerParams(vmem_limit_bytes=40 << 20),
        cost_estimate=pl.CostEstimate(
            flops=2 * 2 * HD * PAIRS, bytes_accessed=8 << 20, transcendentals=PAIRS
        ),
    )(info, queries, *pieces)


def attention_backward(info, queries, pieces, grads, full, total):
    return pl.pallas_call(
        backward_kernel,
        name="attention_backward",
        out_shape=(
            jax.ShapeDtypeStruct((2, group_rows, 2 * HD), f32),
            jax.ShapeDtypeStruct(CHUNKS[1:], bf16),
            jax.ShapeDtypeStruct(CHUNKS[1:], bf16),
        ),
        in_specs=[smem] + [vmem] * 4 + [anywhere] * 8,
        out_specs=[vmem] * 3,
        scratch_shapes=[
            pltpu.VMEM(CHUNKS, bf16),
            pltpu.SemaphoreType.DMA((8,)),
            pltpu.VMEM((2, HD, group_rows), bf16),
            pltpu.VMEM((2, HD, group_rows), bf16),
            pltpu.VMEM((2, 1, group_rows), f32),
            pltpu.VMEM((2, HD, group_rows), f32),
            pltpu.VMEM(CHUNKS, f32),
        ],
        compiler_params=pltpu.CompilerParams(vmem_limit_bytes=56 << 20),
        cost_estimate=pl.CostEstimate(
            flops=5 * 2 * HD * PAIRS, bytes_accessed=12 << 20, transcendentals=PAIRS
        ),
    )(info, queries, grads, full, total, *pieces)


def gather_pieces(shard, order):
    rows = shard.shape[0]
    co, zh = lax.axis_index("co"), lax.axis_index("zh")
    chunk = rows // 16
    place = co
    for link in order[::-1]:
        place = place * 2 + link_bit(link)
    mine = across(lax.dynamic_slice_in_dim(shard, place * chunk, chunk, 0), "zB")
    for link in order:
        mine = double(mine, link)
    other = across(mine, "co")
    base = (1 - zh) * rows
    return (
        (shard, zh * rows),
        (mine, base + co * (rows // 2)),
        (other, base + (1 - co) * (rows // 2)),
    )


def dot_pieces(left_op, pieces):
    total = None
    for piece, start in pieces:
        part = dot_plain(lax.dynamic_slice_in_dim(left_op, start, piece.shape[0], 1), piece)
        total = part if total is None else total + part
    return total


def dot_pieces_t(left_op, pieces):
    out = jnp.zeros((left_op.shape[0], 2 * pieces[0][0].shape[0]), f32)
    for piece, start in pieces:
        out = lax.dynamic_update_slice(out, dot_second(left_op, piece), (0, start))
    return out


GATHERS = {
    "gate": ("x0", "y0", "x1"),
    "up": ("y0", "x1", "y1"),
    "down": ("x1", "y1", "x0"),
    "out": ("y1", "x0", "y0"),
}
ORDERS = {
    "gate": ("zB", "x0", "y0", "zA", "x1", "y1"),
    "up": ("x1", "zB", "zA", "y1", "y0", "x0"),
    "out": ("zA", "y1", "zB", "x0", "x1", "y0"),
    "down": ("y0", "x1", "zB", "y1", "zA", "x0"),
}


def scatter_weight_grad(left_op, right_op, order, extra=None):
    rows = left_op.shape[1]
    depth = max(order.index("zB") + 1, 2)
    near, far = order[:depth], order[depth:]
    size = rows // 4 // 2 ** (depth - 1)
    co = lax.axis_index("co")

    def columns(side, number):
        zh, place = 0, 0
        for step, link in enumerate(near):
            bit = link_bit(link) ^ ((number >> (depth - 1 - step)) & 1)
            if link == "zB":
                zh = bit
            else:
                place = place * 2 + bit
        start = zh * (rows // 2) + side * (rows // 4) + place * size
        return lax.dynamic_slice_in_dim(left_op, start, size, 1)

    def blocks(side, numbers):
        return jnp.concatenate([columns(side, number) for number in numbers], axis=1)

    count = 2**depth

    def with_extra(array):
        return array if extra is None else jnp.concatenate([array, high_low(extra).reshape(-1, D)])

    def take_extra(got, extra):
        if extra is None:
            return got, None
        body = got.shape[0] - 2 * extra.shape[0]
        more = got[body:].astype(f32).reshape(2, *extra.shape)
        return got[:body], extra + more[0] + more[1]

    got = across(
        with_extra(dot_first(blocks(1 - co, range(count)), right_op).astype(bf16)), "co"
    )
    got, extra = take_extra(got, extra)
    middle = got.shape[0] // 2
    sent = dot_first(blocks(co, range(count // 2, count)), right_op) + got[middle:].astype(f32)
    kept = dot_first(blocks(co, range(count // 2)), right_op) + got[:middle].astype(f32)
    more = across(with_extra(sent.astype(bf16)), near[0])
    more, extra = take_extra(more, extra)
    array = (kept + more.astype(f32)).astype(bf16)
    for link in near[1:]:
        middle = array.shape[0] // 2
        more = across(with_extra(array[middle:]), link)
        more, extra = take_extra(more, extra)
        array = (array[:middle].astype(f32) + more.astype(f32)).astype(bf16)
    for link in far:
        middle = array.shape[0] // 2
        bit = link_bit(link)
        sent = lax.dynamic_slice_in_dim(array, (1 - bit) * middle, middle, 0)
        kept = lax.dynamic_slice_in_dim(array, bit * middle, middle, 0)
        more = across(with_extra(sent), link)
        more, extra = take_extra(more, extra)
        array = (kept.astype(f32) + more.astype(f32)).astype(bf16)
    return array if extra is None else (array, extra)


def place_kernel(where_ref, *refs):
    pieces, out_ref = refs[:4], refs[4]
    for number, piece in enumerate(pieces):

        @pl.when(pl.program_id(0) // 2 == number)
        def _():
            out_ref[...] = piece[0].astype(f32)


def spread_rows(chunk, order):
    links = [link for link in order if link != "zB"]
    for link in links[:1:-1]:
        chunk = double(chunk, link)
    pair = jnp.stack([chunk, across(chunk, links[1])])
    pieces = [pair, across(pair, links[0])]
    pieces += [across(piece, "co") for piece in pieces]
    co, first, second = lax.axis_index("co"), link_bit(links[0]), link_bit(links[1])
    where = jnp.stack(
        [
            ((co ^ (number >> 2)) * 2 + (first ^ ((number >> 1) & 1))) * 2
            + (second ^ (number & 1))
            for number in range(8)
        ]
    ).astype(jnp.int32)
    rows, width = chunk.shape

    def piece_spec(number):
        return pl.BlockSpec(
            (1, rows, width), lambda step, where: (jnp.clip(step - 2 * number, 0, 1), 0, 0)
        )

    return pl.pallas_call(
        place_kernel,
        name="place_rows",
        out_shape=jax.ShapeDtypeStruct((8 * rows, width), f32),
        grid_spec=pltpu.PrefetchScalarGridSpec(
            num_scalar_prefetch=1,
            grid=(8,),
            in_specs=[piece_spec(number) for number in range(4)],
            out_specs=pl.BlockSpec((rows, width), lambda step, where: (where[step], 0)),
        ),
        compiler_params=pltpu.CompilerParams(vmem_limit_bytes=32 << 20),
        cost_estimate=pl.CostEstimate(
            flops=8 * rows * width, bytes_accessed=48 * rows * width, transcendentals=0
        ),
    )(where, *pieces)


def per_device(
    tokens,
    doc_lengths,
    query_weight,
    key_weight,
    value_weight,
    out_weight,
    gate_weight,
    up_weight,
    down_weight,
    query_gain,
    key_gain,
    attn_gain,
    ffn_gain,
    cotangent,
):
    y, x, zl, co, zh = (lax.axis_index(name) for name in ("y", "x", "zl", "co", "zh"))
    head = x * 2 + zl
    lengths = doc_lengths[0]
    first_end = lengths[0]
    second_end = lengths[0] + lengths[1]
    info = jnp.stack([y, co, first_end, second_end]).astype(jnp.int32)
    source = tokens[0]

    gains = jnp.concatenate([query_gain, key_gain, attn_gain, ffn_gain])
    other_gains = across(gains, "zh")

    def whole_gain(start, size):
        own = gains[start : start + size]
        got = other_gains[start : start + size]
        return jnp.where(zh == 0, jnp.concatenate([own, got]), jnp.concatenate([got, own]))

    query_scale = lax.dynamic_slice_in_dim(whole_gain(0, 1024), head * 2 * HD, 2 * HD).astype(f32)
    key_scale = lax.dynamic_slice_in_dim(whole_gain(1024, 512), head * HD, HD).astype(f32)
    attn_scale = whole_gain(1536, 512)
    ffn_scale = whole_gain(2048, 512)

    def head_slice(which):
        return jnp.concatenate(
            [
                lax.dynamic_slice_in_dim(query_weight, which * 2 * HD, 2 * HD, 1),
                lax.dynamic_slice_in_dim(key_weight, which * HD, HD, 1),
                lax.dynamic_slice_in_dim(value_weight, which * HD, HD, 1),
            ],
            axis=1,
        )

    own_slice = head_slice(head)
    got_slice = across(own_slice, "zh")
    head_weight = jnp.where(
        zh == 0,
        jnp.concatenate([own_slice, got_slice]),
        jnp.concatenate([got_slice, own_slice]),
    )
    left_cols, right_cols = source[None, :, : D // 2], source[None, :, D // 2 :]
    for link in ("x0", "x1"):
        left_cols = double_in_place(left_cols, link)
    left_cols = double_in_place(left_cols.reshape(4, 1, BLK, D // 2), "zA", axis=1)
    right_cols = double_in_place(right_cols, "zA")[None]
    for link in ("x0", "x1"):
        right_cols = double_in_place(right_cols, link)
    group_tokens = (
        jnp.concatenate([left_cols.reshape(8, BLK, -1), right_cols.reshape(8, BLK, -1)], axis=2)
        .reshape(8, 2, half_blk, D)
        .transpose(1, 0, 2, 3)
        .reshape(2 * group_rows, D)
    )
    out_pieces = gather_pieces(out_weight, GATHERS["out"])
    gate_pieces = gather_pieces(gate_weight, GATHERS["gate"])
    up_pieces = gather_pieces(up_weight, GATHERS["up"])
    down_pieces = gather_pieces(down_weight, GATHERS["down"])

    index = jnp.arange(group_rows, dtype=jnp.int32)
    positions = jnp.concatenate(
        [half_positions(index, y, co, 0), half_positions(index, y, co, 1)]
    )
    doc_start = jnp.where(
        positions >= second_end, second_end, jnp.where(positions >= first_end, first_end, 0)
    )
    frequency = jnp.power(
        f32(rope_base), -jnp.arange(HD // 2, dtype=f32) * (2.0 / HD)
    )
    angles = (positions - doc_start).astype(f32)[:, None] * frequency[None, :]
    cosine, sine_table = jnp.cos(angles), jnp.sin(angles)

    raw = dot_plain(group_tokens, head_weight)
    query_raw, key_raw, value_raw = raw[:, : 2 * HD], raw[:, 2 * HD : 3 * HD], raw[:, 3 * HD :]
    squares = sum_over(
        jnp.stack([jnp.sum(query_raw * query_raw, axis=-1), jnp.sum(key_raw * key_raw, axis=-1)]),
        HEAD_LINKS,
    )
    query_inverse = lax.rsqrt(squares[0][:, None] / HQ + epsilon)
    key_inverse = lax.rsqrt(squares[1][:, None] / HK + epsilon)
    query_normed = query_raw * query_inverse
    key_normed = key_raw * key_inverse
    query_out = query_normed * query_scale
    queries = (
        jnp.concatenate(
            [
                rotate(query_out[:, :HD], cosine, sine_table),
                rotate(query_out[:, HD:], cosine, sine_table),
            ],
            axis=1,
        )
        * log2_scale
    ).astype(bf16)
    keys = rotate(key_normed * key_scale, cosine, sine_table).astype(bf16)
    kv = jnp.concatenate([keys, value_raw.astype(bf16)], axis=1).reshape(2, group_rows, 2 * HD)
    pieces = []
    for half, (first, second) in enumerate((("y0", "y1"), ("y1", "y0"))):
        pair = jnp.stack([kv[half], across(kv[half], first)])
        pieces += [pair, across(pair, second)]
    pieces += [across(piece, "co") for piece in pieces]
    queries = queries.reshape(2, group_rows, 2 * HD)

    attended_low, attended_full, log_total = attention_forward(info, queries, pieces)
    attended_low = (
        lax.all_to_all(attended_low, HEAD_AXES, 0, 0, tiled=True)
        .transpose(1, 2, 0, 3)
        .reshape(BLK, HQ)
    )

    mixed_out = dot_pieces(attended_low, out_pieces)
    attn_out, attn_normed, attn_inverse = rms_forward(mixed_out, attn_scale)
    hidden = source.astype(f32) + attn_out
    hidden_low = hidden.astype(bf16)
    gate_act = dot_pieces(hidden_low, gate_pieces)
    up_act = dot_pieces(hidden_low, up_pieces)
    sigmoid = jax.nn.sigmoid(gate_act)
    swish_act = gate_act * sigmoid
    inner_low = (swish_act * up_act).astype(bf16)
    down_out = dot_pieces(inner_low, down_pieces)
    ffn_out, ffn_normed, ffn_inverse = rms_forward(down_out, ffn_scale)
    output = (hidden + ffn_out).astype(bf16)

    upstream = cotangent[0].astype(f32)
    down_grad, ffn_gain_grad = rms_backward(upstream, ffn_scale, ffn_normed, ffn_inverse)
    down_low = down_grad.astype(bf16)
    inner_grad = dot_pieces_t(down_low, down_pieces)
    gate_low = (inner_grad * up_act * sigmoid * (1.0 + gate_act * (1.0 - sigmoid))).astype(bf16)
    up_low = (inner_grad * swish_act).astype(bf16)
    hidden_grad = (
        upstream + dot_pieces_t(gate_low, gate_pieces) + dot_pieces_t(up_low, up_pieces)
    )
    mixed_grad, attn_gain_grad = rms_backward(hidden_grad, attn_scale, attn_normed, attn_inverse)
    mixed_low = mixed_grad.astype(bf16)
    attended_grad = dot_pieces_t(mixed_low, out_pieces).astype(bf16)

    grads = lax.all_to_all(
        attended_grad.reshape(2, half_blk, 8, 2 * HD).transpose(2, 0, 1, 3),
        HEAD_AXES,
        0,
        0,
        tiled=True,
    )
    grads = grads.transpose(1, 0, 2, 3).reshape(2, group_rows, 2 * HD)

    gate_chunk = scatter_weight_grad(hidden_low, gate_low, ORDERS["gate"])
    up_chunk = scatter_weight_grad(hidden_low, up_low, ORDERS["up"])
    down_chunk = scatter_weight_grad(inner_low, down_low, ORDERS["down"])
    norm_gain_grads = jnp.pad(jnp.stack([attn_gain_grad, ffn_gain_grad]), ((0, 6), (0, 0)))
    out_chunk, norm_gain_grads = scatter_weight_grad(
        attended_low, mixed_low, ORDERS["out"], norm_gain_grads
    )

    query_grad, sent, kept = attention_backward(
        info, queries, pieces, grads, attended_full, log_total
    )

    got = across(sent, "co")
    parts = []
    for half, (first, second) in enumerate((("y1", "y0"), ("y0", "y1"))):
        both = kept[half].astype(f32) + got[half].astype(f32)
        more = across(both[2:].astype(bf16), first)
        both = (both[:2] + more.astype(f32)).astype(bf16)
        more = across(both[1], second)
        parts.append(both[0].astype(f32) + more.astype(f32))
    kv_grad = jnp.concatenate(parts)
    key_grad, value_grad = kv_grad[:, :HD], kv_grad[:, HD:]
    query_grad = query_grad.reshape(2 * group_rows, 2 * HD)

    back_sine = -sine_table
    key_up = rotate(key_grad, cosine, back_sine)
    query_up = jnp.concatenate(
        [
            rotate(query_grad[:, :HD], cosine, back_sine),
            rotate(query_grad[:, HD:], cosine, back_sine),
        ],
        axis=1,
    )
    query_scaled = query_up * query_scale
    key_scaled = key_up * key_scale
    means = sum_over(
        jnp.stack(
            [
                jnp.sum(query_scaled * query_normed, axis=-1),
                jnp.sum(key_scaled * key_normed, axis=-1),
            ]
        ),
        HEAD_LINKS,
    )
    query_raw_grad = query_inverse * (query_scaled - query_normed * (means[0][:, None] / HQ))
    key_raw_grad = key_inverse * (key_scaled - key_normed * (means[1][:, None] / HK))
    query_gain_grad = jnp.sum(query_up * query_normed, axis=0)
    key_gain_grad = jnp.sum(key_up * key_normed, axis=0)
    raw_low = jnp.concatenate([query_raw_grad, key_raw_grad, value_grad], axis=1).astype(bf16)

    by_owner = (
        raw_low.reshape(2, 8, half_blk, 4 * HD).transpose(1, 0, 2, 3).reshape(8, BLK, 4 * HD)
    )
    x_high, x_low = x // 2, x % 2
    halves = []
    for part in range(2):
        columns = head_weight[part * (D // 2) : (part + 1) * (D // 2)]

        def product(rows):
            return dot_second(rows.reshape(4 * BLK, 4 * HD), columns)

        if part == 0:
            sent = lax.dynamic_slice_in_dim(by_owner, (1 - x_high) * 4, 4, 0)
            kept = lax.dynamic_slice_in_dim(by_owner, x_high * 4, 4, 0)
            got = across(product(sent).astype(bf16), "x1")
            both = (product(kept) + got.astype(f32)).astype(bf16).reshape(2, 2 * BLK, D // 2)
            sent = lax.dynamic_index_in_dim(both, 1 - x_low, 0, keepdims=False)
            kept = lax.dynamic_index_in_dim(both, x_low, 0, keepdims=False)
            got = across(sent, "x0")
            both = (kept.astype(f32) + got.astype(f32)).astype(bf16).reshape(2, BLK, D // 2)
            sent = lax.dynamic_index_in_dim(both, 1 - zl, 0, keepdims=False)
            kept = lax.dynamic_index_in_dim(both, zl, 0, keepdims=False)
            got = across(sent, "zA")
        else:
            by_side = by_owner.reshape(4, 2, BLK, 4 * HD)
            sent = lax.dynamic_index_in_dim(by_side, 1 - zl, 1, keepdims=False)
            kept = lax.dynamic_index_in_dim(by_side, zl, 1, keepdims=False)
            got = across(product(sent).astype(bf16), "zA")
            both = (product(kept) + got.astype(f32)).astype(bf16).reshape(2, 2 * BLK, D // 2)
            sent = lax.dynamic_index_in_dim(both, 1 - x_high, 0, keepdims=False)
            kept = lax.dynamic_index_in_dim(both, x_high, 0, keepdims=False)
            got = across(sent, "x1")
            both = (kept.astype(f32) + got.astype(f32)).astype(bf16).reshape(2, BLK, D // 2)
            sent = lax.dynamic_index_in_dim(both, 1 - x_low, 0, keepdims=False)
            kept = lax.dynamic_index_in_dim(both, x_low, 0, keepdims=False)
            got = across(sent, "x0")
        halves.append(kept.astype(f32) + got.astype(f32))
    tokens_grad = hidden_grad + jnp.concatenate(halves, axis=1)

    def token_columns(side):
        return jnp.concatenate(
            [
                lax.dynamic_slice_in_dim(group_tokens, part * 512 + side * 256, 256, 1)
                for part in range(2)
            ],
            axis=1,
        )

    gain_sums = jnp.pad(
        jnp.concatenate([query_gain_grad, key_gain_grad])[None], ((0, 7), (0, HD))
    )

    def with_gains(array, sums):
        return jnp.concatenate([array, high_low(sums).reshape(16, 4 * HD)])

    def take_gains(got, sums):
        more = got[-16:].astype(f32).reshape(2, 8, 4 * HD)
        return got[:-16].astype(f32), sums + more[0] + more[1]

    got = across(
        with_gains(dot_first(token_columns(1 - co), raw_low).astype(bf16), gain_sums), "co"
    )
    got, gain_sums = take_gains(got, gain_sums)
    head_chunk = (dot_first(token_columns(co), raw_low) + got).astype(bf16)
    for link in ("zh", "y1", "y0"):
        middle = head_chunk.shape[0] // 2
        bit = link_bit(link)
        sent = lax.dynamic_slice_in_dim(head_chunk, (1 - bit) * middle, middle, 0)
        kept = lax.dynamic_slice_in_dim(head_chunk, bit * middle, middle, 0)
        got, gain_sums = take_gains(across(with_gains(sent, gain_sums), link), gain_sums)
        head_chunk = (kept.astype(f32) + got).astype(bf16)
    gain_rows = high_low(gain_sums).reshape(1, 16, 4 * HD)
    query_part = head_chunk[None, :, : 2 * HD]
    rest_part = head_chunk[None, :, 2 * HD :]
    for link in ("y0", "y1"):
        query_part = double(query_part, link)
    query_part = query_part.reshape(1, 256, 2 * HD)
    query_part = jnp.concatenate([query_part, gain_rows[:, :, : 2 * HD]], axis=1)
    rest_part = jnp.concatenate([rest_part, gain_rows[:, :, 2 * HD :]], axis=1)[None]
    for link in ("x0", "x1"):
        query_part = double_in_place(query_part, link)
        rest_part = double_in_place(rest_part, link)
    query_part = double_in_place(query_part[:, None], "zA", axis=1).reshape(8, 272, 2 * HD)
    rest_part = double_in_place(rest_part.reshape(4, 1, 80, 2 * HD), "zA", axis=1)
    rest_part = rest_part.reshape(8, 80, 2 * HD)
    key_gain_grad = rest_part[:, 64, :HD].astype(f32) + rest_part[:, 72, :HD].astype(f32)
    query_gain_grad = query_part[:, 256].astype(f32) + query_part[:, 264].astype(f32)
    rest_part = rest_part[None, :, :64]
    for link in ("y0", "y1"):
        rest_part = double(rest_part, link)
    query_part = query_part[:, :256].transpose(1, 0, 2).reshape(256, HQ)
    rest_part = rest_part.reshape(4, 8, 64, 2 * HD).transpose(0, 2, 1, 3).reshape(256, HQ)

    def both_cores(array):
        other = across(array, "co")
        return jnp.where(
            co == 0, jnp.concatenate([array, other]), jnp.concatenate([other, array])
        ).astype(f32)

    query_weight_grad = both_cores(query_part)
    rest_part = both_cores(rest_part).reshape(512, 8, 2, HD)
    key_weight_grad = rest_part[:, :, 0].reshape(512, HK)
    value_weight_grad = rest_part[:, :, 1].reshape(512, HK)

    out_weight_grad = spread_rows(out_chunk, ORDERS["out"])
    gate_weight_grad = spread_rows(gate_chunk, ORDERS["gate"])
    up_weight_grad = spread_rows(up_chunk, ORDERS["up"])
    down_weight_grad = spread_rows(down_chunk, ORDERS["down"])

    def own_gain(gain_grad):
        size = gain_grad.shape[0] // 2
        return lax.dynamic_slice_in_dim(gain_grad, zh * size, size)

    return (
        output[None],
        tokens_grad[None],
        query_weight_grad,
        key_weight_grad,
        value_weight_grad,
        out_weight_grad,
        gate_weight_grad,
        up_weight_grad,
        down_weight_grad,
        own_gain(query_gain_grad.reshape(HQ)),
        own_gain(key_gain_grad.reshape(HK)),
        own_gain(norm_gain_grads[0]),
        own_gain(norm_gain_grads[1]),
    )


def solution(mesh):
    fine = Mesh(mesh.devices.reshape(4, 4, 2, 2, 2), ("y", "x", "zl", "co", "zh"))
    rows = P("zh", TOKEN_AXES, None)
    weight = P("zh", None)
    gain = P("zh")
    return jax.shard_map(
        per_device,
        mesh=fine,
        in_specs=(rows, weight) + (weight,) * 7 + (gain,) * 4 + (rows,),
        out_specs=(rows, rows) + (weight,) * 7 + (gain,) * 4,
        check_vma=False,
    )
```

```python
import functools
import math

import jax
import jax.numpy as jnp
from jax import lax
from jax.experimental import pallas as pl
from jax.experimental.pallas import tpu as pltpu
from jax.sharding import Mesh
from jax.sharding import PartitionSpec as P

D = 1024
HEADS = 16
KVH = 8
HD = 128
FF = 3072
BLK = 128
HQ = 2048
HK = 1024
SEQ = 8192

epsilon = 1e-06
rope_base = 1000000.0
masked_score = -1e30
score_scale = HD**-0.5
log2_scale = score_scale * math.log2(math.e)
half_blk = BLK // 2
group_rows = 8 * half_blk

bf16 = jnp.bfloat16
f32 = jnp.float32

TOKEN_AXES = ("y", "x", "zl", "co")
HEAD_AXES = ("x", "zl")

edge_a = [(0, 1), (1, 0), (2, 3), (3, 2)]
edge_b = [(1, 2), (2, 1), (3, 0), (0, 3)]
swap = [(0, 1), (1, 0)]
LINKS = {
    "x0": ("x", edge_a),
    "x1": ("x", edge_b),
    "y0": ("y", edge_a),
    "y1": ("y", edge_b),
    "zA": ("zl", swap),
    "zB": (("zl", "zh"), [(0, 3), (3, 0), (1, 2), (2, 1)]),
    "co": ("co", swap),
    "zh": ("zh", swap),
}


def link_bit(link):
    if link in ("x0", "y0"):
        place = lax.axis_index(link[0])
        return ((place == 1) | (place == 2)).astype(jnp.int32)
    if link in ("x1", "y1"):
        return (lax.axis_index(link[0]) >= 2).astype(jnp.int32)
    if link == "zA":
        return lax.axis_index("zl") ^ lax.axis_index("zh")
    if link == "zB":
        return lax.axis_index("zh")
    return lax.axis_index(link)


def across(array, link):
    axis, pairs = LINKS[link]
    return lax.ppermute(array, axis, pairs)


def dot_plain(left_op, right_op):
    return jnp.dot(left_op, right_op, preferred_element_type=f32)


def dot_second(left_op, right_op):
    return lax.dot_general(
        left_op, right_op, (((1,), (1,)), ((), ())), preferred_element_type=f32
    )


def dot_first(left_op, right_op):
    return lax.dot_general(
        left_op, right_op, (((0,), (0,)), ((), ())), preferred_element_type=f32
    )


def exchange(array, axes):
    return lax.all_to_all(array, axes, 0, 0, tiled=True)


def gather_all(array, axes, count):
    return exchange(jnp.broadcast_to(array[None], (count, *array.shape)), axes)


def high_low(values):
    high = values.astype(bf16)
    return jnp.stack([high, (values - high.astype(f32)).astype(bf16)])


def half_positions(index, y, co, half):
    block = 16 * y + 2 * (index // half_blk) + co
    inner = index % half_blk
    return jnp.where(half == 0, block * half_blk + inner, SEQ - (block + 1) * half_blk + inner)


def query_masks(info_ref, half):
    y, co, first_end, second_end = info_ref[0], info_ref[1], info_ref[2], info_ref[3]
    index = lax.broadcasted_iota(jnp.int32, (1, group_rows), 1)
    position = half_positions(index, y, co, half)
    start = jnp.where(position >= second_end, second_end, 0)
    start = jnp.where((position >= first_end) & (position < second_end), first_end, start)
    return position, start, position >= second_end


def pair_mask(group, key_half, query_pos, query_start):
    index = lax.broadcasted_iota(jnp.int32, (group_rows, 1), 0)
    key_pos = half_positions(index, group // 2, group % 2, key_half)
    return (key_pos >= query_start) & (key_pos <= query_pos)


def open_steps(y, half):
    count = jnp.where(half == 0, jnp.maximum(2 * y - 2, 0), 6 + 6 - 2 * y)

    def chunk(step):
        late = step >= 6
        group = jnp.where(late, step - 6 + 2 * y + 2, step + 2)
        return group, jnp.where(late, 1, 0)

    return count, chunk


def masked_steps(y, half):
    count = jnp.where((half == 0) & (y == 0), 2, 4)

    def chunk(step):
        own = step >= 2
        group = jnp.where(own, 2 * y + step - 2, step)
        return group, jnp.where(own, half, 0)

    return count, chunk


def slot_of(group, key_half, y, co):
    other_y = group // 2
    beside, over = other_y == (y ^ 1), other_y == 3 - y
    first = jnp.where(key_half == 0, beside, over)
    second = jnp.where(key_half == 0, over, beside)
    ring = jnp.where(other_y == y, 0, jnp.where(first, 1, jnp.where(second, 2, 3)))
    return (group % 2) ^ co, key_half, ring


def load_chunks(pieces, kvs, sems):
    copies = []
    for number, piece in enumerate(pieces):
        core, half, pair = number // 4, number // 2 % 2, number % 2
        target = kvs.at[core, half, pl.ds(2 * pair, 2)]
        copies.append(pltpu.make_async_copy(piece, target, sems.at[number]))
    for copy in copies:
        copy.start()
    return copies


def forward_kernel(info_ref, query_ref, *refs):
    pieces, (low_ref, full_ref, total_ref), (kvs, sems, qt, top, denom, acc) = (
        refs[:8],
        refs[8:11],
        refs[11:],
    )
    y, co = info_ref[0], info_ref[1]
    for copy in load_chunks(pieces, kvs, sems):
        copy.wait()

    def half_body(half, carry):
        query_pos, query_start, last_doc = query_masks(info_ref, half)
        for head in range(2):
            lanes = slice(head * HD, (head + 1) * HD)
            qt[head] = query_ref[half, :, lanes].astype(f32).T.astype(bf16)
            top[head] = jnp.full((1, group_rows), masked_score, f32)
            denom[head] = jnp.zeros((1, group_rows), f32)
            acc[head] = jnp.zeros((HD, group_rows), f32)

        def step(group, key_half, masked):
            slot = slot_of(group, key_half, y, co)
            keys = kvs[(*slot, slice(None), slice(0, HD))]
            values = kvs[(*slot, slice(None), slice(HD, 2 * HD))]
            if masked:
                mask = pair_mask(group, key_half, query_pos, query_start)
            for head in range(2):
                scores = dot_plain(keys, qt[head])
                if masked:
                    scores = jnp.where(mask, scores, masked_score)
                old_top = top[head]
                new_top = jnp.maximum(old_top, jnp.max(scores, axis=0, keepdims=True))
                weights = jnp.exp2(scores - new_top)
                rescale = jnp.exp2(old_top - new_top)
                denom[head] = denom[head] * rescale + jnp.sum(weights, axis=0, keepdims=True)
                acc[head] = acc[head] * rescale + dot_first(values, weights.astype(bf16))
                top[head] = new_top

        count, chunk = open_steps(y, half)

        def open_body(number, inner):
            step(*chunk(number), False)
            return inner

        lax.fori_loop(0, count, open_body, 0)
        for head in range(2):
            top[head] = jnp.where(last_doc, masked_score, top[head])
            denom[head] = jnp.where(last_doc, 0.0, denom[head])
            acc[head] = jnp.where(last_doc, 0.0, acc[head])
        masked_count, masked_chunk = masked_steps(y, half)

        def masked_body(number, inner):
            step(*masked_chunk(number), True)
            return inner

        lax.fori_loop(0, masked_count, masked_body, 0)
        for head in range(2):
            lanes = slice(head * HD, (head + 1) * HD)
            attended = acc[head] / denom[head]
            full_ref[half, head] = attended
            total_ref[half, head] = top[head] + jnp.log2(denom[head])
            rows = attended.T.astype(bf16)
            for owner in range(8):
                low_ref[owner, half, :, lanes] = rows[owner * half_blk : (owner + 1) * half_blk]
        return carry

    lax.fori_loop(0, 2, half_body, 0)


def backward_kernel(info_ref, query_ref, grad_ref, full_ref, total_ref, *refs):
    pieces, (dq_ref, sent_hbm, kept_hbm), (kvs, sems, qt, gt, delta, dqt, dkv) = (
        refs[:8],
        refs[8:11],
        refs[11:],
    )
    y, co = info_ref[0], info_ref[1]

    def grads_of(half, lanes):
        return grad_ref[:, half, :, lanes].reshape(group_rows, HD)

    copies = load_chunks(pieces, kvs, sems)
    dkv[...] = jnp.zeros_like(dkv)
    for copy in copies:
        copy.wait()

    def half_body(half, carry):
        query_pos, query_start, last_doc = query_masks(info_ref, half)
        for head in range(2):
            lanes = slice(head * HD, (head + 1) * HD)
            qt[head] = query_ref[half, :, lanes].astype(f32).T.astype(bf16)
            grad_t = grads_of(half, lanes).astype(f32).T
            gt[head] = grad_t.astype(bf16)
            delta[head] = jnp.sum(grad_t * full_ref[half, head], axis=0, keepdims=True)
            dqt[head] = jnp.zeros((HD, group_rows), f32)

        def step(group, key_half, masked):
            slot = slot_of(group, key_half, y, co)
            key_lanes = (*slot, slice(None), slice(0, HD))
            value_lanes = (*slot, slice(None), slice(HD, 2 * HD))
            keys = kvs[key_lanes]
            values = kvs[value_lanes]
            if masked:
                mask = pair_mask(group, key_half, query_pos, query_start)
            key_total = dkv[key_lanes]
            value_total = dkv[value_lanes]
            for head in range(2):
                lanes = slice(head * HD, (head + 1) * HD)
                scores = dot_plain(keys, qt[head])
                total = total_ref[half, head]
                if masked:
                    scores = jnp.where(mask, scores, masked_score)
                else:
                    total = jnp.where(last_doc, -masked_score, total)
                probs = jnp.exp2(scores - total)
                value_total += dot_plain(probs.astype(bf16), grads_of(half, lanes))
                prob_grad = dot_plain(values, gt[head])
                low = (probs * (prob_grad - delta[head])).astype(bf16)
                key_total += dot_plain(low, query_ref[half, :, lanes])
                dqt[head] += dot_first(keys, low)
            dkv[key_lanes] = key_total
            dkv[value_lanes] = value_total

        count, chunk = open_steps(y, half)

        def open_body(number, inner):
            step(*chunk(number), False)
            return inner

        lax.fori_loop(0, count, open_body, 0)
        masked_count, masked_chunk = masked_steps(y, half)

        def masked_body(number, inner):
            step(*masked_chunk(number), True)
            return inner

        lax.fori_loop(0, masked_count, masked_body, 0)
        for head in range(2):
            lanes = slice(head * HD, (head + 1) * HD)
            dq_ref[half, :, lanes] = dqt[head].T * score_scale
        return carry

    lax.fori_loop(0, 2, half_body, 0)

    def store(core):
        def store_body(number, carry):
            half, ring = number // 4, number % 4
            rows = (core, half, ring)
            kvs[(*rows, slice(None), slice(0, HD))] = (
                dkv[(*rows, slice(None), slice(0, HD))] * math.log(2.0)
            ).astype(bf16)
            kvs[(*rows, slice(None), slice(HD, 2 * HD))] = dkv[
                (*rows, slice(None), slice(HD, 2 * HD))
            ].astype(bf16)
            return carry

        lax.fori_loop(0, 8, store_body, 0)

    stores = [
        pltpu.make_async_copy(kvs.at[1], sent_hbm, sems.at[0]),
        pltpu.make_async_copy(kvs.at[0], kept_hbm, sems.at[1]),
    ]
    store(1)
    stores[0].start()
    store(0)
    stores[1].start()
    for copy in stores:
        copy.wait()


smem = pl.BlockSpec(memory_space=pltpu.SMEM)
vmem = pl.BlockSpec(memory_space=pltpu.VMEM)
hbm = pl.BlockSpec(memory_space=pltpu.HBM)


def in_hbm(*arrays):
    return [pltpu.with_memory_space_constraint(array, pltpu.HBM) for array in arrays]


PAIRS = 4 * 2 * group_rows * 9 * group_rows
CHUNKS = (2, 2, 4, group_rows, 2 * HD)


def attention_forward(info, queries, pieces):
    return pl.pallas_call(
        forward_kernel,
        name="attention_forward",
        out_shape=(
            jax.ShapeDtypeStruct((8, 2, half_blk, 2 * HD), bf16),
            jax.ShapeDtypeStruct((2, 2, HD, group_rows), f32),
            jax.ShapeDtypeStruct((2, 2, 1, group_rows), f32),
        ),
        in_specs=[smem, vmem] + [hbm] * 8,
        out_specs=[vmem] * 3,
        scratch_shapes=[
            pltpu.VMEM(CHUNKS, bf16),
            pltpu.SemaphoreType.DMA((8,)),
            pltpu.VMEM((2, HD, group_rows), bf16),
            pltpu.VMEM((2, 1, group_rows), f32),
            pltpu.VMEM((2, 1, group_rows), f32),
            pltpu.VMEM((2, HD, group_rows), f32),
        ],
        compiler_params=pltpu.CompilerParams(vmem_limit_bytes=24 << 20),
        cost_estimate=pl.CostEstimate(
            flops=2 * 2 * HD * PAIRS, bytes_accessed=8 << 20, transcendentals=PAIRS
        ),
    )(info, queries, *in_hbm(*pieces))


def attention_backward(info, queries, pieces, grads, full, total):
    return pl.pallas_call(
        backward_kernel,
        name="attention_backward",
        out_shape=(
            jax.ShapeDtypeStruct((2, group_rows, 2 * HD), f32),
            pltpu.HBM((2, 4, group_rows, 2 * HD), bf16),
            pltpu.HBM((2, 4, group_rows, 2 * HD), bf16),
        ),
        in_specs=[smem] + [vmem] * 4 + [hbm] * 8,
        out_specs=[vmem, hbm, hbm],
        scratch_shapes=[
            pltpu.VMEM(CHUNKS, bf16),
            pltpu.SemaphoreType.DMA((8,)),
            pltpu.VMEM((2, HD, group_rows), bf16),
            pltpu.VMEM((2, HD, group_rows), bf16),
            pltpu.VMEM((2, 1, group_rows), f32),
            pltpu.VMEM((2, HD, group_rows), f32),
            pltpu.VMEM(CHUNKS, f32),
        ],
        compiler_params=pltpu.CompilerParams(vmem_limit_bytes=36 << 20),
        cost_estimate=pl.CostEstimate(
            flops=5 * 2 * HD * PAIRS, bytes_accessed=12 << 20, transcendentals=PAIRS
        ),
    )(info, queries, grads, full, total, *in_hbm(*pieces))


OUT_ROWS, GATE_ROWS, DOWN_ROWS = HQ // 64, D // 64, FF // 64
BLOCKS = FF // D
GATE_AT = OUT_ROWS
UP_AT = GATE_AT + BLOCKS * GATE_ROWS
DOWN_AT = UP_AT + BLOCKS * GATE_ROWS
CHUNK_ROWS = DOWN_AT + DOWN_ROWS


def run_copies(copies):
    for copy in copies:
        copy.start()
    for copy in copies:
        copy.wait()


def collect_kernel(
    info_ref, query_ref, key_ref, value_ref, out_ref, gate_ref, up_ref, down_ref, gain_ref,
    own_ref, sent_ref, chunk_ref, sems,
):
    place = info_ref[0]
    numbers = iter(range(15))
    copies = []

    def copy(source, target):
        copies.append(pltpu.make_async_copy(source, target, sems.at[next(numbers)]))

    for target, head in ((sent_ref, info_ref[2]), (own_ref, info_ref[1])):
        lanes = pl.ds(pl.multiple_of(head * 2 * HD, 2 * HD), 2 * HD)
        copy(query_ref.at[:, lanes], target.at[:, pl.ds(0, 2 * HD)])
        lanes = pl.ds(pl.multiple_of(head * HD, HD), HD)
        copy(key_ref.at[:, lanes], target.at[:, pl.ds(2 * HD, HD)])
        copy(value_ref.at[:, lanes], target.at[:, pl.ds(3 * HD, HD)])
    copy(out_ref.at[place], chunk_ref.at[pl.ds(0, OUT_ROWS)])
    copy(down_ref.at[place], chunk_ref.at[pl.ds(DOWN_AT, DOWN_ROWS)])
    copy(gain_ref, chunk_ref.at[pl.ds(CHUNK_ROWS, 16)])
    for ref, start in ((gate_ref, GATE_AT), (up_ref, UP_AT)):
        for block in range(BLOCKS):
            copy(
                ref.at[place, :, pl.ds(block * D, D)],
                chunk_ref.at[pl.ds(start + block * GATE_ROWS, GATE_ROWS)],
            )
    run_copies(copies)


def collect(info, projections, shards, gains):
    gain_rows = jnp.pad(gains, (0, 16 * D - gains.shape[0])).reshape(16, D)
    return pl.pallas_call(
        collect_kernel,
        name="collect_chunk",
        out_shape=(
            jax.ShapeDtypeStruct((D // 2, 4 * HD), bf16),
            jax.ShapeDtypeStruct((D // 2, 4 * HD), bf16),
            jax.ShapeDtypeStruct((CHUNK_ROWS + 16, D), bf16),
        ),
        in_specs=[smem] + [hbm] * 8,
        out_specs=[vmem] * 3,
        scratch_shapes=[pltpu.SemaphoreType.DMA((15,))],
        compiler_params=pltpu.CompilerParams(vmem_limit_bytes=60 << 20),
    )(info, *in_hbm(*projections, *shards, gain_rows))


ROWS = 2 * group_rows


def as_lanes(column):
    return jnp.broadcast_to(column, (ROWS, HD)).T[0:1]


def as_rows(row):
    return jnp.broadcast_to(row, (HD, ROWS)).T


def turn(tensor, cosine, sine):
    return tensor * cosine + pltpu.roll(tensor, HD // 2, 1) * sine


def project_kernel(info_ref, tokens_ref, own_ref, got_ref, raw_ref, weight_ref, squares_ref):
    zh = info_ref[0]
    weight_ref[pl.ds(pl.multiple_of(zh * (D // 2), D // 2), D // 2)] = own_ref[...]
    weight_ref[pl.ds(pl.multiple_of((1 - zh) * (D // 2), D // 2), D // 2)] = got_ref[...]
    for owner in range(8):
        raw = dot_plain(tokens_ref[owner], weight_ref[...])
        for half in range(2):
            start = half * group_rows + owner * half_blk
            raw_ref[start : start + half_blk] = raw[half * half_blk : (half + 1) * half_blk]
    raw = raw_ref[:, : 3 * HD]
    squares = raw * raw
    query = jnp.sum(squares[:, :HD] + squares[:, HD : 2 * HD], axis=1, keepdims=True)
    key = jnp.sum(squares[:, 2 * HD :], axis=1, keepdims=True)
    sums = jnp.concatenate([as_lanes(query), as_lanes(key)])
    for owner in range(8):
        squares_ref[owner] = sums


def project(info, tokens, own_slice, got_slice):
    return pl.pallas_call(
        project_kernel,
        name="project",
        out_shape=(
            jax.ShapeDtypeStruct((ROWS, 4 * HD), f32),
            jax.ShapeDtypeStruct((D, 4 * HD), bf16),
            jax.ShapeDtypeStruct((8, 2, ROWS), f32),
        ),
        in_specs=[smem] + [vmem] * 3,
        out_specs=[vmem] * 3,
        compiler_params=pltpu.CompilerParams(vmem_limit_bytes=32 << 20),
        cost_estimate=pl.CostEstimate(
            flops=2 * ROWS * D * 4 * HD, bytes_accessed=6 << 20, transcendentals=0
        ),
    )(info, tokens, own_slice, got_slice)


def inverses(squares_ref):
    total = jnp.sum(squares_ref[...], axis=0)
    return (
        as_rows(lax.rsqrt(total[0:1] / HQ + epsilon)),
        as_rows(lax.rsqrt(total[1:2] / HK + epsilon)),
    )


def prepare_kernel(raw_ref, squares_ref, cos_ref, sin_ref, gain_ref, query_ref, kv_ref):
    query_inverse, key_inverse = inverses(squares_ref)
    cosine, sine = cos_ref[...], sin_ref[...]
    for head in range(3):
        lanes = slice(head * HD, (head + 1) * HD)
        inverse = query_inverse if head < 2 else key_inverse
        turned = turn(raw_ref[:, lanes] * inverse * gain_ref[:, lanes], cosine, sine)
        if head < 2:
            turned = (turned * log2_scale).astype(bf16)
            query_ref[0, :, lanes] = turned[:group_rows]
            query_ref[1, :, lanes] = turned[group_rows:]
        else:
            turned = turned.astype(bf16)
            values = raw_ref[:, 3 * HD :].astype(bf16)
            for half in range(2):
                rows = slice(half * group_rows, (half + 1) * group_rows)
                kv_ref[half, :, :HD] = turned[rows]
                kv_ref[half, :, HD:] = values[rows]


def prepare(raw, squares, tables, gain):
    return pl.pallas_call(
        prepare_kernel,
        name="prepare",
        out_shape=(
            jax.ShapeDtypeStruct((2, group_rows, 2 * HD), bf16),
            jax.ShapeDtypeStruct((2, group_rows, 2 * HD), bf16),
        ),
        in_specs=[vmem] * 5,
        out_specs=[vmem] * 2,
        compiler_params=pltpu.CompilerParams(vmem_limit_bytes=32 << 20),
        cost_estimate=pl.CostEstimate(flops=8 << 20, bytes_accessed=6 << 20, transcendentals=0),
    )(raw, squares, *tables, gain)


def turned_back(raw_ref, squares_ref, cos_ref, sin_ref, dq_ref, dkv_ref):
    query_inverse, key_inverse = inverses(squares_ref)
    cosine, sine = cos_ref[...], -sin_ref[...]
    for head in range(3):
        lanes = slice(head * HD, (head + 1) * HD)
        inverse = query_inverse if head < 2 else key_inverse
        grad = dq_ref[:, lanes] if head < 2 else dkv_ref[:, :HD]
        yield head, lanes, turn(grad, cosine, sine), raw_ref[:, lanes] * inverse, inverse


def means_kernel(raw_ref, squares_ref, cos_ref, sin_ref, gain_ref, dq_ref, dkv_ref, means_ref):
    products = []
    for _, lanes, upstream, normed, _ in turned_back(
        raw_ref, squares_ref, cos_ref, sin_ref, dq_ref, dkv_ref
    ):
        products.append(upstream * gain_ref[:, lanes] * normed)
    query = jnp.sum(products[0] + products[1], axis=1, keepdims=True)
    key = jnp.sum(products[2], axis=1, keepdims=True)
    means_ref[...] = jnp.concatenate([as_lanes(query), as_lanes(key)])


def raw_grad_kernel(
    raw_ref, squares_ref, cos_ref, sin_ref, gain_ref, dq_ref, dkv_ref, means_ref,
    low_ref, gain_grad_ref,
):
    means = (as_rows(means_ref[0:1]) / HQ, as_rows(means_ref[1:2]) / HK)

    def place(lanes, low):
        for owner in range(8):
            for half in range(2):
                start = half * group_rows + owner * half_blk
                low_ref[owner, half * half_blk : (half + 1) * half_blk, lanes] = low[
                    start : start + half_blk
                ]

    for head, lanes, upstream, normed, inverse in turned_back(
        raw_ref, squares_ref, cos_ref, sin_ref, dq_ref, dkv_ref
    ):
        mean = means[0] if head < 2 else means[1]
        place(lanes, (inverse * (upstream * gain_ref[:, lanes] - normed * mean)).astype(bf16))
        gain_grad_ref[:, lanes] = jnp.sum(upstream * normed, axis=0, keepdims=True)
    place(slice(3 * HD, 4 * HD), dkv_ref[:, HD:].astype(bf16))
    gain_grad_ref[:, 3 * HD :] = jnp.zeros((1, HD), f32)


def projection_means(*operands):
    return pl.pallas_call(
        means_kernel,
        name="projection_means",
        out_shape=jax.ShapeDtypeStruct((2, ROWS), f32),
        in_specs=[vmem] * 7,
        out_specs=vmem,
        compiler_params=pltpu.CompilerParams(vmem_limit_bytes=32 << 20),
        cost_estimate=pl.CostEstimate(flops=8 << 20, bytes_accessed=6 << 20, transcendentals=0),
    )(*operands)


def projection_grads(*operands):
    return pl.pallas_call(
        raw_grad_kernel,
        name="projection_grads",
        out_shape=(
            jax.ShapeDtypeStruct((8, BLK, 4 * HD), bf16),
            jax.ShapeDtypeStruct((1, 4 * HD), f32),
        ),
        in_specs=[vmem] * 8,
        out_specs=[vmem] * 2,
        compiler_params=pltpu.CompilerParams(vmem_limit_bytes=32 << 20),
        cost_estimate=pl.CostEstimate(flops=8 << 20, bytes_accessed=6 << 20, transcendentals=0),
    )(*operands)


INNER_AT = 0
DOWN_LOW_AT = INNER_AT + FF // 2
ATT_AT = DOWN_LOW_AT + D
HIDDEN_AT = ATT_AT + HQ // 2
GATE_LOW_AT = HIDDEN_AT + D
UP_LOW_AT = GATE_LOW_AT + FF // 2
MIXED_LOW_AT = UP_LOW_AT + FF // 2
PACK = MIXED_LOW_AT + D


def rows_kernel(
    info_ref, att_ref, tokens_ref, cot_ref, attn_gain_ref, ffn_gain_ref,
    out_own, gate_own, up_own, down_own, mine, other,
    output_ref, own_hbm, sent_hbm, att_grad_ref, hidden_grad_ref, gain_grad_ref,
    own_ref, sent_ref, out_v, gate_v, up_v, down_v, gate_act, up_act, inner_ref, hidden_ref, down_out, sems,
):
    zh, co = info_ref[0], info_ref[1]
    numbers = iter(range(22))

    def copy(source, target):
        return pltpu.make_async_copy(source, target, sems.at[next(numbers)])

    def pieces(own, rows_at, rows, scratch, blocks):
        copies = [copy(own, scratch.at[pl.ds(zh * 32, 32)])]
        for half, core in ((mine, co), (other, 1 - co)):
            at = (1 - zh) * 32 + core * 16
            for block in range(blocks):
                target = scratch.at[pl.ds(at, 16)]
                if blocks > 1:
                    target = scratch.at[pl.ds(at, 16), :, pl.ds(block * D, D)]
                copies.append(
                    copy(half.at[:, pl.ds(rows_at + block * rows, rows), :], target)
                )
        return copies

    out_copies = pieces(out_own, 0, OUT_ROWS, out_v, 1)
    gate_copies = pieces(gate_own, GATE_AT, GATE_ROWS, gate_v, BLOCKS)
    up_copies = pieces(up_own, UP_AT, GATE_ROWS, up_v, BLOCKS)
    down_copies = pieces(down_own, DOWN_AT, DOWN_ROWS, down_v, 1)
    for item in out_copies + gate_copies + up_copies + down_copies:
        item.start()

    def put(core, lanes, value):
        @pl.when(core == co)
        def _():
            own_ref[:, lanes] = value

        @pl.when(core != co)
        def _():
            sent_ref[:, lanes] = value

    def put_both(start, value):
        own_ref[:, start : start + D] = value
        sent_ref[:, start : start + D] = value

    for item in out_copies:
        item.wait()
    hidden_grad_ref[...] = jnp.zeros((BLK, D), f32)

    def mixed_body(head, carry):
        rows = att_ref[head].reshape(BLK, 2 * HD)
        column = (head // 4) * 2 + head % 2
        put((head // 2) % 2, pl.ds(pl.multiple_of(ATT_AT + column * 2 * HD, HD), 2 * HD), rows)
        hidden_grad_ref[...] += dot_plain(rows, out_v[pl.ds(head * 8, 8)].reshape(2 * HD, D))
        return carry

    lax.fori_loop(0, 8, mixed_body, 0)
    attn_gain = attn_gain_ref[...]
    mixed = hidden_grad_ref[...]
    attn_inverse = lax.rsqrt(jnp.mean(mixed * mixed, axis=-1, keepdims=True) + epsilon)
    hidden = tokens_ref[...].astype(f32) + mixed * attn_inverse * attn_gain
    hidden_ref[...] = hidden
    put_both(HIDDEN_AT, hidden.astype(bf16))
    for item in gate_copies + up_copies:
        item.wait()
    tile = 8 * DOWN_ROWS

    def act_body(step, carry):
        lanes = pl.ds(step * tile, tile)
        low = own_ref[:, HIDDEN_AT : HIDDEN_AT + D]
        gate = dot_plain(low, gate_v[:, :, lanes].reshape(D, tile))
        up = dot_plain(low, up_v[:, :, lanes].reshape(D, tile))
        gate_act[:, lanes] = gate
        up_act[:, lanes] = up
        inner = (gate * (1.0 / (1.0 + jnp.exp(-gate))) * up).astype(bf16)
        inner_ref[:, lanes] = inner
        column = (step // 4) * 2 + step % 2
        put((step // 2) % 2, pl.ds(pl.multiple_of(INNER_AT + column * tile, HD), tile), inner)
        return carry

    lax.fori_loop(0, FF // tile, act_body, 0)
    for item in down_copies:
        item.wait()
    down_out[...] = jnp.zeros((BLK, D), f32)

    def down_body(step, carry):
        rows = down_v[pl.ds(step * 8, 8)].reshape(tile, D)
        down_out[...] += dot_plain(inner_ref[:, pl.ds(step * tile, tile)], rows)
        return carry

    lax.fori_loop(0, FF // tile, down_body, 0)
    ffn_gain = ffn_gain_ref[...]
    down = down_out[...]
    ffn_inverse = lax.rsqrt(jnp.mean(down * down, axis=-1, keepdims=True) + epsilon)
    normed = down * ffn_inverse
    output_ref[...] = (hidden_ref[...] + normed * ffn_gain).astype(bf16)
    upstream = cot_ref[...].astype(f32)
    scaled = upstream * ffn_gain
    gain_grad_ref[1:2, :] = jnp.sum(upstream * normed, axis=0, keepdims=True)
    down_low = ffn_inverse * (scaled - normed * jnp.mean(scaled * normed, axis=-1, keepdims=True))
    put_both(DOWN_LOW_AT, down_low.astype(bf16))
    down_out[...] = upstream

    def back_body(step, carry):
        lanes = pl.ds(step * tile, tile)
        rows = down_v[pl.ds(step * 8, 8)].reshape(tile, D)
        inner_grad = dot_second(own_ref[:, DOWN_LOW_AT : DOWN_LOW_AT + D], rows)
        gate, up = gate_act[:, lanes], up_act[:, lanes]
        sigmoid = 1.0 / (1.0 + jnp.exp(-gate))
        gate_low = (inner_grad * up * sigmoid * (1.0 + gate * (1.0 - sigmoid))).astype(bf16)
        up_low = (inner_grad * (gate * sigmoid)).astype(bf16)
        column = (step % 4) * tile
        put(step // 4, pl.ds(pl.multiple_of(GATE_LOW_AT + column, HD), tile), gate_low)
        put(step // 4, pl.ds(pl.multiple_of(UP_LOW_AT + column, HD), tile), up_low)
        down_out[...] += dot_second(gate_low, gate_v[:, :, lanes].reshape(D, tile)) + dot_second(
            up_low, up_v[:, :, lanes].reshape(D, tile)
        )
        return carry

    lax.fori_loop(0, FF // tile, back_body, 0)
    mixed = hidden_grad_ref[...]
    attn_inverse = lax.rsqrt(jnp.mean(mixed * mixed, axis=-1, keepdims=True) + epsilon)
    normed = mixed * attn_inverse
    hidden_grad = down_out[...]
    scaled = hidden_grad * attn_gain_ref[...]
    gain_grad_ref[0:1, :] = jnp.sum(hidden_grad * normed, axis=0, keepdims=True)
    mixed_low = (
        attn_inverse * (scaled - normed * jnp.mean(scaled * normed, axis=-1, keepdims=True))
    ).astype(bf16)
    put_both(MIXED_LOW_AT, mixed_low)
    packs = [copy(sent_ref, sent_hbm), copy(own_ref, own_hbm)]
    for item in packs:
        item.start()
    hidden_grad_ref[...] = hidden_grad

    def grad_body(head, carry):
        rows = out_v[pl.ds(head * 8, 8)].reshape(2 * HD, D)
        mixed_low = own_ref[:, MIXED_LOW_AT : MIXED_LOW_AT + D]
        grad = dot_second(mixed_low, rows).astype(bf16)
        att_grad_ref[head] = grad.reshape(2, half_blk, 2 * HD)
        return carry

    lax.fori_loop(0, 8, grad_body, 0)
    for item in packs:
        item.wait()


def own_rows(info, attended, tokens, cotangent, attn_gain, ffn_gain, shards, mine, other):
    def shape(*dims, dtype=bf16):
        return jax.ShapeDtypeStruct(dims, dtype)

    return pl.pallas_call(
        rows_kernel,
        name="own_rows",
        out_shape=(
            shape(BLK, D),
            pltpu.HBM((BLK, PACK), bf16),
            pltpu.HBM((BLK, PACK), bf16),
            shape(8, 2, half_blk, 2 * HD),
            shape(BLK, D, dtype=f32),
            shape(2, D, dtype=f32),
        ),
        in_specs=[smem] + [vmem] * 5 + [hbm] * 6,
        out_specs=[vmem, hbm, hbm, vmem, vmem, vmem],
        scratch_shapes=[
            pltpu.VMEM((BLK, PACK), bf16),
            pltpu.VMEM((BLK, PACK), bf16),
            pltpu.VMEM((64, OUT_ROWS, D), bf16),
            pltpu.VMEM((64, GATE_ROWS, FF), bf16),
            pltpu.VMEM((64, GATE_ROWS, FF), bf16),
            pltpu.VMEM((64, DOWN_ROWS, D), bf16),
            pltpu.VMEM((BLK, FF), f32),
            pltpu.VMEM((BLK, FF), f32),
            pltpu.VMEM((BLK, FF), bf16),
            pltpu.VMEM((BLK, D), f32),
            pltpu.VMEM((BLK, D), f32),
            pltpu.SemaphoreType.DMA((22,)),
        ],
        compiler_params=pltpu.CompilerParams(vmem_limit_bytes=44 << 20),
        cost_estimate=pl.CostEstimate(
            flops=4 * BLK * (3 * D * FF + HQ * D),
            bytes_accessed=26 << 20,
            transcendentals=2 * BLK * FF,
        ),
    )(info, attended, tokens, cotangent, attn_gain, ffn_gain, *in_hbm(*shards, mine, other))


def wide_rows(array):
    return jnp.concatenate(
        [array[:, start : start + D] for start in range(0, array.shape[1], D)]
    )


def ring_place(bits):
    return bits[0] * 2 + (bits[0] ^ bits[1])


PRODUCTS = (
    (FF // 2, INNER_AT, D, DOWN_LOW_AT, "y", "01"),
    (D, HIDDEN_AT, FF // 2, GATE_LOW_AT, "x", "01"),
    (D, HIDDEN_AT, FF // 2, UP_LOW_AT, "x", "10"),
    (HQ // 2, ATT_AT, D, MIXED_LOW_AT, "y", "10"),
)


def products_kernel(places_ref, own_ref, got_ref, *refs):
    outs, (both, left, sems), scratch = refs[:8], refs[8:11], refs[11:]
    run_copies(
        [
            pltpu.make_async_copy(ref, both.at[pl.ds(core * BLK, BLK)], sems.at[8 + core])
            for core, ref in enumerate((own_ref, got_ref))
        ]
    )
    copies = [
        pltpu.make_async_copy(held, out, sems.at[number])
        for number, (held, out) in enumerate(zip(scratch, outs))
    ]
    held = None
    for number, (rows, left_at, width, right_at, _, _) in enumerate(PRODUCTS):
        if left_at != held:
            left[:rows] = both[:, left_at : left_at + rows].astype(f32).T.astype(bf16)
            held = left_at
        quarter = rows // 8
        for part in range(2):
            out = scratch[2 * number + part]

            def body(step, carry):
                place = places_ref[number * 4 + part * 2 + step // 2]
                start = pl.multiple_of(((step % 2) * 4 + place) * quarter, quarter)
                target = pl.ds(pl.multiple_of(step * quarter, quarter), quarter)
                out[target] = dot_plain(
                    left[pl.ds(start, quarter)], both[:, right_at : right_at + width]
                ).astype(bf16)
                return carry

            lax.fori_loop(0, 4, body, 0)
            copies[2 * number + part].start()
    for copy in copies:
        copy.wait()


def weight_products(own, got):
    places = []
    for _, _, _, _, axis, order in PRODUCTS:
        for first, second in ((1, 0), (1, 1), (0, 0), (0, 1)):
            bits = {name: link_bit(axis + name) for name in "01"}
            bits[order[0]] = bits[order[0]] ^ first
            bits[order[1]] = bits[order[1]] ^ second
            places.append(ring_place((bits["1"], bits["0"])))
    flops = sum(2 * 2 * BLK * rows * width for rows, _, width, _, _, _ in PRODUCTS)
    return pl.pallas_call(
        products_kernel,
        name="weight_products",
        out_shape=[
            pltpu.HBM((rows // 2, width), bf16)
            for rows, _, width, _, _, _ in PRODUCTS
            for _ in range(2)
        ],
        in_specs=[smem, hbm, hbm],
        out_specs=[hbm] * 8,
        scratch_shapes=[
            pltpu.VMEM((2 * BLK, PACK), bf16),
            pltpu.VMEM((FF // 2, 2 * BLK), bf16),
            pltpu.SemaphoreType.DMA((10,)),
        ]
        + [
            pltpu.VMEM((rows // 2, width), bf16)
            for rows, _, width, _, _, _ in PRODUCTS
            for _ in range(2)
        ],
        compiler_params=pltpu.CompilerParams(vmem_limit_bytes=40 << 20),
        cost_estimate=pl.CostEstimate(flops=flops, bytes_accessed=16 << 20, transcendentals=0),
    )(jnp.stack(places).astype(jnp.int32), *in_hbm(own, got))


def place_kernel(core_ref, chunk_ref, *refs):
    gate_ref, up_ref, down_ref, out_ref = refs[-4:]
    for y in range(4):
        for zl in range(2):
            chunk = chunk_ref[y, 0, zl]
            start = (2 * y + zl) * GATE_ROWS
            rows = slice(start, start + GATE_ROWS)
            gate_ref[rows, :D] = chunk[:16].astype(f32)
            gate_ref[rows, D:] = chunk[16:32, : D // 2].astype(f32)
            up_ref[rows, : D // 2] = chunk[16:32, D // 2 :].astype(f32)
            up_ref[rows, D // 2 :] = chunk[32:48].astype(f32)
            down_ref[y, 24 * zl : 24 * zl + 24] = chunk[48:72].astype(f32)
            out_ref[y, 16 * zl : 16 * zl + 16] = chunk[72:].astype(f32)


def place_rows(core, chunks, earlier):
    def columns(x, core):
        return (x, core[0])

    def rows(x, core):
        return (core[0], x, 0)

    return pl.pallas_call(
        place_kernel,
        name="place_rows",
        out_shape=(
            jax.ShapeDtypeStruct((D // 2, FF), f32),
            jax.ShapeDtypeStruct((D // 2, FF), f32),
            jax.ShapeDtypeStruct((8, 4 * 48, D), f32),
            jax.ShapeDtypeStruct((8, 4 * 32, D), f32),
        ),
        grid_spec=pltpu.PrefetchScalarGridSpec(
            num_scalar_prefetch=1,
            grid=(4,),
            in_specs=[pl.BlockSpec((4, 1, 2, 88, D), lambda x, core: (0, x, 0, 0, 0))]
            + [hbm] * len(earlier),
            out_specs=[
                pl.BlockSpec((D // 8, FF // 2), columns),
                pl.BlockSpec((D // 8, FF // 2), columns),
                pl.BlockSpec((4, 48, D), rows),
                pl.BlockSpec((4, 32, D), rows),
            ],
        ),
        input_output_aliases={2 + number: number for number in range(len(earlier))},
        compiler_params=pltpu.CompilerParams(vmem_limit_bytes=32 << 20),
        cost_estimate=pl.CostEstimate(flops=3 << 20, bytes_accessed=18 << 20, transcendentals=0),
    )(core, chunks, *earlier)


def place_heads_kernel(core_ref, chunk_ref, *refs):
    query_ref, key_ref, value_ref = refs[-3:]
    for owner in range(8):
        part = chunk_ref[0, owner, :64].astype(f32)
        query_ref[:, owner * 2 * HD : (owner + 1) * 2 * HD] = part[:, : 2 * HD]
        key_ref[:, owner * HD : (owner + 1) * HD] = part[:, 2 * HD : 3 * HD]
        value_ref[:, owner * HD : (owner + 1) * HD] = part[:, 3 * HD :]


def place_heads(core, chunks, earlier):
    def rows(y, core):
        return (core[0] * 4 + y, 0)

    return pl.pallas_call(
        place_heads_kernel,
        name="place_heads",
        out_shape=(
            jax.ShapeDtypeStruct((D // 2, HQ), f32),
            jax.ShapeDtypeStruct((D // 2, HK), f32),
            jax.ShapeDtypeStruct((D // 2, HK), f32),
        ),
        grid_spec=pltpu.PrefetchScalarGridSpec(
            num_scalar_prefetch=1,
            grid=(4,),
            in_specs=[pl.BlockSpec((1, 8, 80, 4 * HD), lambda y, core: (y, 0, 0, 0))]
            + [hbm] * len(earlier),
            out_specs=[
                pl.BlockSpec((64, HQ), rows),
                pl.BlockSpec((64, HK), rows),
                pl.BlockSpec((64, HK), rows),
            ],
        ),
        input_output_aliases={2 + number: number for number in range(len(earlier))},
        compiler_params=pltpu.CompilerParams(vmem_limit_bytes=32 << 20),
        cost_estimate=pl.CostEstimate(flops=1 << 20, bytes_accessed=6 << 20, transcendentals=0),
    )(core, chunks, *earlier)


def per_device(
    tokens,
    doc_lengths,
    query_weight,
    key_weight,
    value_weight,
    out_weight,
    gate_weight,
    up_weight,
    down_weight,
    query_gain,
    key_gain,
    attn_gain,
    ffn_gain,
    cotangent,
):
    y, x, zl, co, zh = (lax.axis_index(name) for name in ("y", "x", "zl", "co", "zh"))
    head = x * 2 + zl
    lengths = doc_lengths[0]
    first_end = lengths[0]
    second_end = lengths[0] + lengths[1]
    info = jnp.stack([y, co, first_end, second_end]).astype(jnp.int32)
    source = tokens[0]

    gains = jnp.concatenate([query_gain, key_gain, attn_gain, ffn_gain])
    shards = (
        out_weight.reshape(32, OUT_ROWS, D),
        gate_weight.reshape(32, GATE_ROWS, FF),
        up_weight.reshape(32, GATE_ROWS, FF),
        down_weight.reshape(32, DOWN_ROWS, D),
    )
    group_tokens = jnp.broadcast_to(source[None], (8, BLK, D))
    places = jnp.stack([co * 16 + y * 4 + x, head, x * 2 + 1 - zl]).astype(jnp.int32)
    group_tokens, places = lax.optimization_barrier((group_tokens, places))
    own_slice, sent_slice, weight_chunk = collect(
        places,
        (query_weight, key_weight, value_weight),
        shards,
        gains,
    )
    got_slice = across(sent_slice, "zB")
    weight_chunk = across(weight_chunk, "zB")
    group_tokens = exchange(group_tokens, HEAD_AXES)
    mine_weights = lax.all_gather(weight_chunk[:CHUNK_ROWS], ("y", "x"), axis=0, tiled=False)
    other_gains = weight_chunk[CHUNK_ROWS:].reshape(-1)[: gains.shape[0]]

    def whole_gain(start, size):
        own = gains[start : start + size]
        got = other_gains[start : start + size]
        return jnp.where(zh == 0, jnp.concatenate([own, got]), jnp.concatenate([got, own]))

    query_scale = lax.dynamic_slice_in_dim(whole_gain(0, 1024), head * 2 * HD, 2 * HD).astype(f32)
    key_scale = lax.dynamic_slice_in_dim(whole_gain(1024, 512), head * HD, HD).astype(f32)
    attn_scale = whole_gain(1536, 512)
    ffn_scale = whole_gain(2048, 512)

    head_gain = jnp.concatenate([query_scale, key_scale])[None]

    index = jnp.arange(group_rows, dtype=jnp.int32)
    positions = jnp.concatenate(
        [half_positions(index, y, co, 0), half_positions(index, y, co, 1)]
    )
    doc_start = jnp.where(
        positions >= second_end, second_end, jnp.where(positions >= first_end, first_end, 0)
    )
    frequency = jnp.power(
        f32(rope_base), -jnp.arange(HD // 2, dtype=f32) * (2.0 / HD)
    )
    angles = (positions - doc_start).astype(f32)[:, None] * frequency[None, :]
    cosine, sine_table = jnp.cos(angles), jnp.sin(angles)
    tables = (
        jnp.concatenate([cosine, cosine], axis=1),
        jnp.concatenate([-sine_table, sine_table], axis=1),
    )

    raw, head_weight, squares = project(
        zh[None].astype(jnp.int32), group_tokens, own_slice, got_slice
    )
    squares = exchange(squares, HEAD_AXES)
    queries, kv = prepare(raw, squares, tables, head_gain)
    pairs = [
        jnp.stack([kv[half], across(kv[half], first)]) for half, first in enumerate(("y0", "y1"))
    ]
    pieces = [
        piece
        for pair, second in zip(pairs, ("y1", "y0"))
        for piece in (pair, across(pair, second))
    ]
    pieces += [across(piece, "co") for piece in pieces]
    pieces, mine_weights = lax.optimization_barrier((pieces, mine_weights))
    other_weights = across(mine_weights, "co")

    attended_low, attended_full, log_total = attention_forward(info, queries, pieces)
    attended_low = exchange(attended_low, HEAD_AXES)
    (
        output,
        own_pack,
        sent_pack,
        attended_grad,
        hidden_grad,
        norm_gain_grads,
    ) = own_rows(
        jnp.stack([zh, co]).astype(jnp.int32),
        attended_low,
        source,
        cotangent[0],
        attn_scale.astype(f32)[None],
        ffn_scale.astype(f32)[None],
        shards,
        mine_weights,
        other_weights,
    )

    grads = exchange(attended_grad, HEAD_AXES)

    products = weight_products(own_pack, across(sent_pack, "co"))
    sent_parts, rest_parts = products[0::2], products[1::2]
    grads, sent_parts = lax.optimization_barrier((grads, sent_parts))
    got_parts = [
        across(sent, axis + order[0])
        for sent, (_, _, _, _, axis, order) in zip(sent_parts, PRODUCTS)
    ]

    query_grad, sent, kept = attention_backward(
        info, queries, pieces, grads, attended_full, log_total
    )
    stage = lax.optimization_barrier
    own_core, other_core = co[None].astype(jnp.int32), (1 - co)[None].astype(jnp.int32)

    sent, got_parts = stage((sent, got_parts))
    got = across(sent, "co")
    second_sent = [
        (rest[rest.shape[0] // 2 :].astype(f32) + part[rest.shape[0] // 2 :].astype(f32)).astype(
            bf16
        )
        for rest, part in zip(rest_parts, got_parts)
    ]
    got, second_sent = stage((got, second_sent))
    orders = (("y1", "y0"), ("y0", "y1"))
    kv_got = [
        across((kept[half, 2:].astype(f32) + got[half, 2:].astype(f32)).astype(bf16), first)
        for half, (first, _) in enumerate(orders)
    ]
    second_got = [
        across(part, axis + order[1])
        for part, (_, _, _, _, axis, order) in zip(second_sent, PRODUCTS)
    ]

    def second_sum(number):
        rest, part = rest_parts[number], got_parts[number]
        middle = rest.shape[0] // 2
        kept_part = rest[:middle].astype(f32) + part[:middle].astype(f32)
        return (kept_part + second_got[number].astype(f32)).astype(bf16)

    kv_got, second_got[1], second_got[2] = stage((kv_got, second_got[1], second_got[2]))
    kv_both = [
        kept[half, :2].astype(f32) + got[half, :2].astype(f32) + kv_got[half].astype(f32)
        for half in range(2)
    ]
    kv_got = [
        across(kv_both[half][1].astype(bf16), second) for half, (_, second) in enumerate(orders)
    ]
    act_part = exchange(
        jnp.concatenate([second_sum(1), second_sum(2)], axis=1).reshape(16, 16, FF),
        ("zh", "y", "zl"),
    )
    kv_got, act_part, second_got[0], second_got[3] = stage(
        (kv_got, act_part, second_got[0], second_got[3])
    )
    rest_part = exchange(
        jnp.concatenate(
            [second_sum(0).reshape(16, 24, D), second_sum(3).reshape(16, 16, D)], axis=1
        ),
        ("zh", "x", "zl"),
    )
    kv_grad = jnp.concatenate(
        [both[0] + more.astype(f32) for both, more in zip(kv_both, kv_got)]
    )
    operands = (
        raw, squares, *tables, head_gain, query_grad.reshape(ROWS, 2 * HD), kv_grad,
    )
    means = projection_means(*operands)
    for link in ("x0", "x1", "zA"):
        means = means + across(means, link)
    act_part = wide_rows(jnp.sum(act_part.astype(f32), axis=0).astype(bf16))
    means, rest_part = stage((means, rest_part))
    chunk = jnp.concatenate([act_part, jnp.sum(rest_part.astype(f32), axis=0).astype(bf16)])
    chunk_got = across(chunk, "zA")
    chunk = jnp.where(zl == 0, jnp.stack([chunk, chunk_got]), jnp.stack([chunk_got, chunk]))
    chunks = lax.all_gather(chunk, ("y", "x"), axis=0, tiled=False).reshape(4, 4, 2, 88, D)
    by_owner, head_gain_grad = projection_grads(*operands, means)
    raw_low = by_owner.reshape(ROWS, 4 * HD)
    group_tokens = group_tokens.reshape(ROWS, D)

    def token_columns(side):
        return jnp.concatenate(
            [
                lax.dynamic_slice_in_dim(group_tokens, part * 512 + side * 256, 256, 1)
                for part in range(2)
            ],
            axis=1,
        )

    gain_sums = jnp.concatenate(
        [
            head_gain_grad,
            norm_gain_grads.reshape(4, 4 * HD),
            jnp.zeros((3, 4 * HD), f32),
        ]
    )
    by_side = by_owner.reshape(4, 2, BLK, 4 * HD)
    x_high, x_low = x // 2, x % 2

    def product(rows, part):
        columns = head_weight[part * (D // 2) : (part + 1) * (D // 2)]
        return dot_second(rows.reshape(4 * BLK, 4 * HD), columns)

    def pick(array, number):
        return lax.dynamic_index_in_dim(array, number, 0, keepdims=False)

    def pass_on(both, link, number):
        return pick(both, number).astype(f32), across(pick(both, 1 - number), link)

    def halves(both):
        return both.astype(bf16).reshape(2, both.shape[0] // 2, D // 2)

    heads_got = across(
        jnp.concatenate(
            [
                dot_first(token_columns(1 - co), raw_low).astype(bf16),
                high_low(gain_sums).reshape(16, 4 * HD),
            ]
        ),
        "co",
    )
    left_sent = product(lax.dynamic_slice_in_dim(by_owner, (1 - x_high) * 4, 4, 0), 0)
    left_got = across(left_sent.astype(bf16), "x1")
    right_sent = product(lax.dynamic_index_in_dim(by_side, 1 - zl, 1, keepdims=False), 1)
    right_got = across(right_sent.astype(bf16), "zA")
    head_chunk = dot_first(token_columns(co), raw_low)
    left = product(lax.dynamic_slice_in_dim(by_owner, x_high * 4, 4, 0), 0)
    right = product(lax.dynamic_index_in_dim(by_side, zl, 1, keepdims=False), 1)
    heads_got, left_got, right_got, head_chunk, left, right = stage(
        (heads_got, left_got, right_got, head_chunk, left, right)
    )
    heads_got = heads_got.astype(f32)
    gain_sums = gain_sums + heads_got[512:520] + heads_got[520:]
    head_chunk = jnp.concatenate(
        [
            (head_chunk + heads_got[:512]).astype(bf16).reshape(8, 64, 4 * HD),
            jnp.broadcast_to(high_low(gain_sums).reshape(1, 16, 4 * HD), (8, 16, 4 * HD)),
        ],
        axis=1,
    )
    head_chunk = exchange(head_chunk, ("zh", "y"))
    left, left_got = pass_on(halves(left + left_got.astype(f32)), "x0", x_low)
    right, right_got = pass_on(halves(right + right_got.astype(f32)), "x1", x_high)
    head_chunk, left_got, right_got = stage((head_chunk, left_got, right_got))
    head_chunk = jnp.sum(head_chunk.astype(f32), axis=0)
    gain_sums = head_chunk[64:72] + head_chunk[72:]
    head_chunk = jnp.concatenate(
        [head_chunk[:64].astype(bf16), high_low(gain_sums).reshape(16, 4 * HD)]
    )
    mine = gather_all(head_chunk, ("y", "x", "zl"), 32)
    left, left_got = pass_on(halves(left + left_got.astype(f32)), "zA", zl)
    right, right_got = pass_on(halves(right + right_got.astype(f32)), "x0", x_low)
    mine, left_got, right_got = stage((mine, left_got, right_got))
    tokens_grad = hidden_grad + jnp.concatenate(
        [left + left_got.astype(f32), right + right_got.astype(f32)], axis=1
    )

    mine = mine.reshape(4, 8, 80, 4 * HD)
    other_heads = across(mine, "co")
    placed_heads = place_heads(own_core, mine, ())
    query_weight_grad, key_weight_grad, value_weight_grad = place_heads(
        other_core, other_heads, placed_heads
    )
    gain_sums = mine[0, :, 64:72].astype(f32) + mine[0, :, 72:].astype(f32)
    query_gain_grad = gain_sums[:, 0, : 2 * HD].reshape(HQ)
    key_gain_grad = gain_sums[:, 0, 2 * HD : 3 * HD].reshape(HK)
    norm_gain_grads = jnp.sum(gain_sums[:, 1:5], axis=0).reshape(2, D)
    chunks, query_weight_grad, tokens_grad = stage((chunks, query_weight_grad, tokens_grad))
    placed = place_rows(own_core, chunks, ())
    gate_weight_grad, up_weight_grad, down_weight_grad, out_weight_grad = place_rows(
        other_core, across(chunks, "co"), placed
    )
    down_weight_grad = down_weight_grad.reshape(FF // 2, D)
    out_weight_grad = out_weight_grad.reshape(HQ // 2, D)

    def own_gain(gain_grad):
        size = gain_grad.shape[0] // 2
        return lax.dynamic_slice_in_dim(gain_grad, zh * size, size)

    return (
        output[None],
        tokens_grad[None],
        query_weight_grad,
        key_weight_grad,
        value_weight_grad,
        out_weight_grad,
        gate_weight_grad,
        up_weight_grad,
        down_weight_grad,
        own_gain(query_gain_grad.reshape(HQ)),
        own_gain(key_gain_grad.reshape(HK)),
        own_gain(norm_gain_grads[0]),
        own_gain(norm_gain_grads[1]),
    )


def solution(mesh):
    fine = Mesh(mesh.devices.reshape(4, 4, 2, 2, 2), ("y", "x", "zl", "co", "zh"))
    rows = P("zh", TOKEN_AXES, None)
    weight = P("zh", None)
    gain = P("zh")
    return jax.shard_map(
        per_device,
        mesh=fine,
        in_specs=(rows, weight) + (weight,) * 7 + (gain,) * 4 + (rows,),
        out_specs=(rows, rows) + (weight,) * 7 + (gain,) * 4,
        check_vma=False,
    )
```

```python
import functools
import math

import jax
import jax.numpy as jnp
from jax import lax
from jax.experimental import pallas as pl
from jax.experimental.pallas import tpu as pltpu
from jax.sharding import Mesh
from jax.sharding import PartitionSpec as P

D = 1024
HEADS = 16
KVH = 8
HD = 128
FF = 3072
BLK = 128
HQ = 2048
HK = 1024
SEQ = 8192

epsilon = 1e-06
rope_base = 1000000.0
masked_score = -1e30
score_scale = HD**-0.5
log2_scale = score_scale * math.log2(math.e)
half_blk = BLK // 2
group_rows = 8 * half_blk

bf16 = jnp.bfloat16
f32 = jnp.float32

TOKEN_AXES = ("y", "x", "zl", "co")
HEAD_AXES = ("x", "zl")

edge_a = [(0, 1), (1, 0), (2, 3), (3, 2)]
edge_b = [(1, 2), (2, 1), (3, 0), (0, 3)]
swap = [(0, 1), (1, 0)]
LINKS = {
    "x0": ("x", edge_a),
    "x1": ("x", edge_b),
    "y0": ("y", edge_a),
    "y1": ("y", edge_b),
    "zA": ("zl", swap),
    "zB": (("zl", "zh"), [(0, 3), (3, 0), (1, 2), (2, 1)]),
    "zl": ("zl", swap),
    "co": ("co", swap),
    "zh": ("zh", swap),
}


def link_bit(link):
    if link in ("x0", "y0"):
        place = lax.axis_index(link[0])
        return ((place == 1) | (place == 2)).astype(jnp.int32)
    if link in ("x1", "y1"):
        return (lax.axis_index(link[0]) >= 2).astype(jnp.int32)
    if link == "zA":
        return lax.axis_index("zl") ^ lax.axis_index("zh")
    if link == "zB":
        return lax.axis_index("zh")
    return lax.axis_index(link)


def across(array, link):
    axis, pairs = LINKS[link]
    return lax.ppermute(array, axis, pairs)


def dot_plain(left_op, right_op):
    return jnp.dot(left_op, right_op, preferred_element_type=f32)


def dot_second(left_op, right_op):
    return lax.dot_general(
        left_op, right_op, (((1,), (1,)), ((), ())), preferred_element_type=f32
    )


def dot_first(left_op, right_op):
    return lax.dot_general(
        left_op, right_op, (((0,), (0,)), ((), ())), preferred_element_type=f32
    )


def exchange(array, axes):
    return lax.all_to_all(array, axes, 0, 0, tiled=True)


def gather_all(array, axes, count):
    return exchange(jnp.broadcast_to(array[None], (count, *array.shape)), axes)


def double(array, link):
    if link == "zA":
        bit = link_bit(link)
    else:
        place = lax.axis_index(LINKS[link][0])
        bit = place // 2 if link in ("x1", "y1") else place % 2
    got = across(array, link)
    return jnp.where(bit == 0, jnp.concatenate([array, got]), jnp.concatenate([got, array]))


def high_low(values):
    high = values.astype(bf16)
    return jnp.stack([high, (values - high.astype(f32)).astype(bf16)])


def half_positions(index, y, co, half):
    block = 16 * y + 2 * (index // half_blk) + co
    inner = index % half_blk
    return jnp.where(half == 0, block * half_blk + inner, SEQ - (block + 1) * half_blk + inner)


def query_masks(info_ref, half):
    y, co, first_end, second_end = info_ref[0], info_ref[1], info_ref[2], info_ref[3]
    index = lax.broadcasted_iota(jnp.int32, (1, group_rows), 1)
    position = half_positions(index, y, co, half)
    start = jnp.where(position >= second_end, second_end, 0)
    start = jnp.where((position >= first_end) & (position < second_end), first_end, start)
    return position, start, position >= second_end


def pair_mask(group, key_half, query_pos, query_start):
    index = lax.broadcasted_iota(jnp.int32, (group_rows, 1), 0)
    key_pos = half_positions(index, group // 2, group % 2, key_half)
    return (key_pos >= query_start) & (key_pos <= query_pos)


def open_steps(y, half):
    count = jnp.where(half == 0, jnp.maximum(2 * y - 2, 0), 6 + 6 - 2 * y)

    def chunk(step):
        late = step >= 6
        group = jnp.where(late, step - 6 + 2 * y + 2, step + 2)
        return group, jnp.where(late, 1, 0)

    return count, chunk


def masked_steps(y, half):
    count = jnp.where((half == 0) & (y == 0), 2, 4)

    def chunk(step):
        own = step >= 2
        group = jnp.where(own, 2 * y + step - 2, step)
        return group, jnp.where(own, half, 0)

    return count, chunk


def slot_of(group, key_half, y, co):
    other_y = group // 2
    beside, over = other_y == (y ^ 1), other_y == 3 - y
    first = jnp.where(key_half == 0, beside, over)
    second = jnp.where(key_half == 0, over, beside)
    ring = jnp.where(other_y == y, 0, jnp.where(first, 1, jnp.where(second, 2, 3)))
    return (group % 2) ^ co, key_half, ring


def load_chunks(pieces, kvs, sems):
    copies = []
    for number, piece in enumerate(pieces):
        core, half, pair = number // 4, number // 2 % 2, number % 2
        target = kvs.at[core, half, pl.ds(2 * pair, 2)]
        copies.append(pltpu.make_async_copy(piece, target, sems.at[number]))
    for copy in copies:
        copy.start()
    return copies


def forward_kernel(info_ref, query_ref, *refs):
    pieces, (low_ref, full_ref, total_ref), (kvs, sems, qt, top, denom, acc) = (
        refs[:8],
        refs[8:11],
        refs[11:],
    )
    y, co = info_ref[0], info_ref[1]
    for copy in load_chunks(pieces, kvs, sems):
        copy.wait()

    def half_body(half, carry):
        query_pos, query_start, last_doc = query_masks(info_ref, half)
        for head in range(2):
            lanes = slice(head * HD, (head + 1) * HD)
            qt[head] = query_ref[half, :, lanes].astype(f32).T.astype(bf16)
            top[head] = jnp.full((1, group_rows), masked_score, f32)
            denom[head] = jnp.zeros((1, group_rows), f32)
            acc[head] = jnp.zeros((HD, group_rows), f32)

        def step(chunks, masked):
            slots = [slot_of(*chunk, y, co) for chunk in chunks]
            keys = [kvs[(*slot, slice(None), slice(0, HD))] for slot in slots]
            values = [kvs[(*slot, slice(None), slice(HD, 2 * HD))] for slot in slots]
            if masked:
                masks = [pair_mask(*chunk, query_pos, query_start) for chunk in chunks]
            for head in range(2):
                scores = [dot_plain(part, qt[head]) for part in keys]
                if masked:
                    scores = [
                        jnp.where(mask, part, masked_score) for mask, part in zip(masks, scores)
                    ]
                old_top = top[head]
                new_top = old_top
                for part in scores:
                    new_top = jnp.maximum(new_top, jnp.max(part, axis=0, keepdims=True))
                weights = [jnp.exp2(part - new_top) for part in scores]
                rescale = jnp.exp2(old_top - new_top)
                total = denom[head] * rescale
                for part in weights:
                    total += jnp.sum(part, axis=0, keepdims=True)
                denom[head] = total
                acc[head] = (
                    acc[head] * rescale
                    + dot_first(values[0], weights[0].astype(bf16))
                    + dot_first(values[1], weights[1].astype(bf16))
                )
                top[head] = new_top

        count, chunk = open_steps(y, half)

        def open_body(number, inner):
            step((chunk(2 * number), chunk(2 * number + 1)), False)
            return inner

        lax.fori_loop(0, count // 2, open_body, 0)
        for head in range(2):
            top[head] = jnp.where(last_doc, masked_score, top[head])
            denom[head] = jnp.where(last_doc, 0.0, denom[head])
            acc[head] = jnp.where(last_doc, 0.0, acc[head])
        masked_count, masked_chunk = masked_steps(y, half)

        def masked_body(number, inner):
            step((masked_chunk(2 * number), masked_chunk(2 * number + 1)), True)
            return inner

        lax.fori_loop(0, masked_count // 2, masked_body, 0)
        for head in range(2):
            lanes = slice(head * HD, (head + 1) * HD)
            attended = acc[head] / denom[head]
            full_ref[half, head] = attended
            total_ref[half, head] = top[head] + jnp.log2(denom[head])
            rows = attended.T.astype(bf16)
            for owner in range(8):
                low_ref[owner, half, :, lanes] = rows[owner * half_blk : (owner + 1) * half_blk]
        return carry

    lax.fori_loop(0, 2, half_body, 0)


def backward_kernel(info_ref, query_ref, grad_ref, full_ref, total_ref, *refs):
    pieces, (dq_ref, sent_hbm, kept_hbm), (kvs, sems, qt, gt, delta, dqt, dkv) = (
        refs[:8],
        refs[8:11],
        refs[11:],
    )
    y, co = info_ref[0], info_ref[1]

    def grads_of(half, lanes):
        return grad_ref[:, half, :, lanes].reshape(group_rows, HD)

    copies = load_chunks(pieces, kvs, sems)
    dkv[...] = jnp.zeros_like(dkv)
    for copy in copies:
        copy.wait()

    def half_body(half, carry):
        query_pos, query_start, last_doc = query_masks(info_ref, half)
        for head in range(2):
            lanes = slice(head * HD, (head + 1) * HD)
            qt[head] = query_ref[half, :, lanes].astype(f32).T.astype(bf16)
            grad_t = grads_of(half, lanes).astype(f32).T
            gt[head] = grad_t.astype(bf16)
            delta[head] = jnp.sum(grad_t * full_ref[half, head], axis=0, keepdims=True)
            dqt[head] = jnp.zeros((HD, group_rows), f32)

        def step(chunks, masked):
            for head in range(2):
                lanes = slice(head * HD, (head + 1) * HD)
                total = total_ref[half, head]
                if not masked:
                    total = jnp.where(last_doc, -masked_score, total)
                query_total = dqt[head]
                for chunk in chunks:
                    slot = slot_of(*chunk, y, co)
                    key_lanes = (*slot, slice(None), slice(0, HD))
                    value_lanes = (*slot, slice(None), slice(HD, 2 * HD))
                    keys = kvs[key_lanes]
                    scores = dot_plain(keys, qt[head])
                    if masked:
                        mask = pair_mask(*chunk, query_pos, query_start)
                        scores = jnp.where(mask, scores, masked_score)
                    probs = jnp.exp2(scores - total)
                    dkv[value_lanes] += dot_plain(probs.astype(bf16), grads_of(half, lanes))
                    prob_grad = dot_plain(kvs[value_lanes], gt[head])
                    low = (probs * (prob_grad - delta[head])).astype(bf16)
                    dkv[key_lanes] += dot_plain(low, query_ref[half, :, lanes])
                    query_total += dot_first(keys, low)
                dqt[head] = query_total

        count, chunk = open_steps(y, half)

        def open_body(number, inner):
            step((chunk(2 * number), chunk(2 * number + 1)), False)
            return inner

        lax.fori_loop(0, count // 2, open_body, 0)
        masked_count, masked_chunk = masked_steps(y, half)

        def masked_body(number, inner):
            step((masked_chunk(2 * number), masked_chunk(2 * number + 1)), True)
            return inner

        lax.fori_loop(0, masked_count // 2, masked_body, 0)
        for head in range(2):
            lanes = slice(head * HD, (head + 1) * HD)
            dq_ref[half, :, lanes] = dqt[head].T * score_scale
        return carry

    lax.fori_loop(0, 2, half_body, 0)

    def store(core):
        def store_body(number, carry):
            half, ring = number // 4, number % 4
            rows = (core, half, ring)
            kvs[(*rows, slice(None), slice(0, HD))] = (
                dkv[(*rows, slice(None), slice(0, HD))] * math.log(2.0)
            ).astype(bf16)
            kvs[(*rows, slice(None), slice(HD, 2 * HD))] = dkv[
                (*rows, slice(None), slice(HD, 2 * HD))
            ].astype(bf16)
            return carry

        lax.fori_loop(0, 8, store_body, 0)

    stores = [
        pltpu.make_async_copy(kvs.at[1], sent_hbm, sems.at[0]),
        pltpu.make_async_copy(kvs.at[0], kept_hbm, sems.at[1]),
    ]
    store(1)
    stores[0].start()
    store(0)
    stores[1].start()
    for copy in stores:
        copy.wait()


smem = pl.BlockSpec(memory_space=pltpu.SMEM)
vmem = pl.BlockSpec(memory_space=pltpu.VMEM)
hbm = pl.BlockSpec(memory_space=pltpu.HBM)


def in_hbm(*arrays):
    return [pltpu.with_memory_space_constraint(array, pltpu.HBM) for array in arrays]


PAIRS = 4 * 2 * group_rows * 9 * group_rows
CHUNKS = (2, 2, 4, group_rows, 2 * HD)


def attention_forward(info, queries, pieces):
    return pl.pallas_call(
        forward_kernel,
        name="attention_forward",
        out_shape=(
            jax.ShapeDtypeStruct((8, 2, half_blk, 2 * HD), bf16),
            jax.ShapeDtypeStruct((2, 2, HD, group_rows), f32),
            jax.ShapeDtypeStruct((2, 2, 1, group_rows), f32),
        ),
        in_specs=[smem, vmem] + [hbm] * 8,
        out_specs=[vmem] * 3,
        scratch_shapes=[
            pltpu.VMEM(CHUNKS, bf16),
            pltpu.SemaphoreType.DMA((8,)),
            pltpu.VMEM((2, HD, group_rows), bf16),
            pltpu.VMEM((2, 1, group_rows), f32),
            pltpu.VMEM((2, 1, group_rows), f32),
            pltpu.VMEM((2, HD, group_rows), f32),
        ],
        compiler_params=pltpu.CompilerParams(vmem_limit_bytes=24 << 20),
        cost_estimate=pl.CostEstimate(
            flops=2 * 2 * HD * PAIRS, bytes_accessed=8 << 20, transcendentals=PAIRS
        ),
    )(info, queries, *in_hbm(*pieces))


def attention_backward(info, queries, pieces, grads, full, total):
    return pl.pallas_call(
        backward_kernel,
        name="attention_backward",
        out_shape=(
            jax.ShapeDtypeStruct((2, group_rows, 2 * HD), f32),
            pltpu.HBM((2, 4, group_rows, 2 * HD), bf16),
            pltpu.HBM((2, 4, group_rows, 2 * HD), bf16),
        ),
        in_specs=[smem] + [vmem] * 4 + [hbm] * 8,
        out_specs=[vmem, hbm, hbm],
        scratch_shapes=[
            pltpu.VMEM(CHUNKS, bf16),
            pltpu.SemaphoreType.DMA((8,)),
            pltpu.VMEM((2, HD, group_rows), bf16),
            pltpu.VMEM((2, HD, group_rows), bf16),
            pltpu.VMEM((2, 1, group_rows), f32),
            pltpu.VMEM((2, HD, group_rows), f32),
            pltpu.VMEM(CHUNKS, f32),
        ],
        compiler_params=pltpu.CompilerParams(vmem_limit_bytes=36 << 20),
        cost_estimate=pl.CostEstimate(
            flops=5 * 2 * HD * PAIRS, bytes_accessed=12 << 20, transcendentals=PAIRS
        ),
    )(info, queries, grads, full, total, *in_hbm(*pieces))


OUT_ROWS, GATE_ROWS, DOWN_ROWS = HQ // 64, D // 64, FF // 64
BLOCKS = FF // D
GATE_AT = OUT_ROWS
UP_AT = GATE_AT + BLOCKS * GATE_ROWS
DOWN_AT = UP_AT + BLOCKS * GATE_ROWS
CHUNK_ROWS = DOWN_AT + DOWN_ROWS


def run_copies(copies):
    for copy in copies:
        copy.start()
    for copy in copies:
        copy.wait()


def collect_kernel(
    info_ref, query_ref, key_ref, value_ref, out_ref, gate_ref, up_ref, down_ref, gain_ref,
    own_ref, sent_ref, chunk_ref, sems,
):
    place = info_ref[0]
    numbers = iter(range(15))
    copies = []

    def copy(source, target):
        copies.append(pltpu.make_async_copy(source, target, sems.at[next(numbers)]))

    for target, head in ((sent_ref, info_ref[2]), (own_ref, info_ref[1])):
        lanes = pl.ds(pl.multiple_of(head * 2 * HD, 2 * HD), 2 * HD)
        copy(query_ref.at[:, lanes], target.at[:, pl.ds(0, 2 * HD)])
        lanes = pl.ds(pl.multiple_of(head * HD, HD), HD)
        copy(key_ref.at[:, lanes], target.at[:, pl.ds(2 * HD, HD)])
        copy(value_ref.at[:, lanes], target.at[:, pl.ds(3 * HD, HD)])
    copy(out_ref.at[place], chunk_ref.at[pl.ds(0, OUT_ROWS)])
    copy(down_ref.at[place], chunk_ref.at[pl.ds(DOWN_AT, DOWN_ROWS)])
    copy(gain_ref, chunk_ref.at[pl.ds(CHUNK_ROWS, 16)])
    for ref, start in ((gate_ref, GATE_AT), (up_ref, UP_AT)):
        for block in range(BLOCKS):
            copy(
                ref.at[place, :, pl.ds(block * D, D)],
                chunk_ref.at[pl.ds(start + block * GATE_ROWS, GATE_ROWS)],
            )
    run_copies(copies)


def collect(info, projections, shards, gains):
    gain_rows = jnp.pad(gains, (0, 16 * D - gains.shape[0])).reshape(16, D)
    return pl.pallas_call(
        collect_kernel,
        name="collect_chunk",
        out_shape=(
            jax.ShapeDtypeStruct((D // 2, 4 * HD), bf16),
            jax.ShapeDtypeStruct((D // 2, 4 * HD), bf16),
            jax.ShapeDtypeStruct((CHUNK_ROWS + 16, D), bf16),
        ),
        in_specs=[smem] + [hbm] * 8,
        out_specs=[vmem] * 3,
        scratch_shapes=[pltpu.SemaphoreType.DMA((15,))],
        compiler_params=pltpu.CompilerParams(vmem_limit_bytes=60 << 20),
    )(info, *in_hbm(*projections, *shards, gain_rows))


ROWS = 2 * group_rows


def as_lanes(column):
    return jnp.broadcast_to(column, (ROWS, HD)).T[0:1]


def as_rows(row):
    return jnp.broadcast_to(row, (HD, ROWS)).T


def turn(tensor, cosine, sine):
    return tensor * cosine + pltpu.roll(tensor, HD // 2, 1) * sine


def project_kernel(info_ref, tokens_ref, own_ref, got_ref, raw_ref, weight_ref, squares_ref):
    zh = info_ref[0]
    weight_ref[pl.ds(pl.multiple_of(zh * (D // 2), D // 2), D // 2)] = own_ref[...]
    weight_ref[pl.ds(pl.multiple_of((1 - zh) * (D // 2), D // 2), D // 2)] = got_ref[...]
    for owner in range(8):
        raw = dot_plain(tokens_ref[owner], weight_ref[...])
        for half in range(2):
            start = half * group_rows + owner * half_blk
            raw_ref[start : start + half_blk] = raw[half * half_blk : (half + 1) * half_blk]
    raw = raw_ref[:, : 3 * HD]
    squares = raw * raw
    query = jnp.sum(squares[:, :HD] + squares[:, HD : 2 * HD], axis=1, keepdims=True)
    key = jnp.sum(squares[:, 2 * HD :], axis=1, keepdims=True)
    sums = jnp.concatenate([as_lanes(query), as_lanes(key)])
    for owner in range(8):
        squares_ref[owner] = sums


def project(info, tokens, own_slice, got_slice):
    return pl.pallas_call(
        project_kernel,
        name="project",
        out_shape=(
            jax.ShapeDtypeStruct((ROWS, 4 * HD), f32),
            jax.ShapeDtypeStruct((D, 4 * HD), bf16),
            jax.ShapeDtypeStruct((8, 2, ROWS), f32),
        ),
        in_specs=[smem] + [vmem] * 3,
        out_specs=[vmem] * 3,
        compiler_params=pltpu.CompilerParams(vmem_limit_bytes=32 << 20),
        cost_estimate=pl.CostEstimate(
            flops=2 * ROWS * D * 4 * HD, bytes_accessed=6 << 20, transcendentals=0
        ),
    )(info, tokens, own_slice, got_slice)


def inverses(squares_ref):
    total = jnp.sum(squares_ref[...], axis=0)
    return (
        as_rows(lax.rsqrt(total[0:1] / HQ + epsilon)),
        as_rows(lax.rsqrt(total[1:2] / HK + epsilon)),
    )


def prepare_kernel(raw_ref, squares_ref, cos_ref, sin_ref, gain_ref, query_ref, kv_ref):
    query_inverse, key_inverse = inverses(squares_ref)
    cosine, sine = cos_ref[...], sin_ref[...]
    for head in range(3):
        lanes = slice(head * HD, (head + 1) * HD)
        inverse = query_inverse if head < 2 else key_inverse
        turned = turn(raw_ref[:, lanes] * inverse * gain_ref[:, lanes], cosine, sine)
        if head < 2:
            turned = (turned * log2_scale).astype(bf16)
            query_ref[0, :, lanes] = turned[:group_rows]
            query_ref[1, :, lanes] = turned[group_rows:]
        else:
            turned = turned.astype(bf16)
            values = raw_ref[:, 3 * HD :].astype(bf16)
            for half in range(2):
                rows = slice(half * group_rows, (half + 1) * group_rows)
                kv_ref[half, :, :HD] = turned[rows]
                kv_ref[half, :, HD:] = values[rows]


def prepare(raw, squares, tables, gain):
    return pl.pallas_call(
        prepare_kernel,
        name="prepare",
        out_shape=(
            jax.ShapeDtypeStruct((2, group_rows, 2 * HD), bf16),
            jax.ShapeDtypeStruct((2, group_rows, 2 * HD), bf16),
        ),
        in_specs=[vmem] * 5,
        out_specs=[vmem] * 2,
        compiler_params=pltpu.CompilerParams(vmem_limit_bytes=32 << 20),
        cost_estimate=pl.CostEstimate(flops=8 << 20, bytes_accessed=6 << 20, transcendentals=0),
    )(raw, squares, *tables, gain)


def turned_back(raw_ref, squares_ref, cos_ref, sin_ref, dq_ref, dkv_ref):
    query_inverse, key_inverse = inverses(squares_ref)
    cosine, sine = cos_ref[...], -sin_ref[...]
    for head in range(3):
        lanes = slice(head * HD, (head + 1) * HD)
        inverse = query_inverse if head < 2 else key_inverse
        grad = dq_ref[:, lanes] if head < 2 else dkv_ref[:, :HD]
        yield head, lanes, turn(grad, cosine, sine), raw_ref[:, lanes] * inverse, inverse


def means_kernel(raw_ref, squares_ref, cos_ref, sin_ref, gain_ref, dq_ref, dkv_ref, means_ref):
    products = []
    for _, lanes, upstream, normed, _ in turned_back(
        raw_ref, squares_ref, cos_ref, sin_ref, dq_ref, dkv_ref
    ):
        products.append(upstream * gain_ref[:, lanes] * normed)
    query = jnp.sum(products[0] + products[1], axis=1, keepdims=True)
    key = jnp.sum(products[2], axis=1, keepdims=True)
    means_ref[...] = jnp.concatenate([as_lanes(query), as_lanes(key)])


def raw_grad_kernel(
    info_ref, raw_ref, squares_ref, cos_ref, sin_ref, gain_ref, dq_ref, dkv_ref, means_ref,
    tokens_ref, weight_ref, norm_gains_ref,
    heads_sent_ref, heads_kept_ref, gains_ref, left_sent_ref, left_kept_ref, right_sent_ref,
    right_kept_ref, low_ref,
):
    co, x_high, zl = info_ref[0], info_ref[1], info_ref[2]
    means = (as_rows(means_ref[0:1]) / HQ, as_rows(means_ref[1:2]) / HK)

    def place(lanes, low):
        for owner in range(8):
            for half in range(2):
                start = half * group_rows + owner * half_blk
                low_ref[owner, half * half_blk : (half + 1) * half_blk, lanes] = low[
                    start : start + half_blk
                ]

    gains_ref[...] = jnp.zeros((8, 4 * HD), f32)
    for head, lanes, upstream, normed, inverse in turned_back(
        raw_ref, squares_ref, cos_ref, sin_ref, dq_ref, dkv_ref
    ):
        mean = means[0] if head < 2 else means[1]
        place(lanes, (inverse * (upstream * gain_ref[:, lanes] - normed * mean)).astype(bf16))
        gains_ref[0:1, lanes] = jnp.sum(upstream * normed, axis=0, keepdims=True)
    place(slice(3 * HD, 4 * HD), dkv_ref[:, HD:].astype(bf16))
    for row in range(4):
        part = slice((row % 2) * 4 * HD, (row % 2 + 1) * 4 * HD)
        gains_ref[1 + row : 2 + row] = norm_gains_ref[row // 2 : row // 2 + 1, part]
    gains = gains_ref[...]
    high = gains.astype(bf16)
    heads_sent_ref[512:] = jnp.concatenate([high, (gains - high.astype(f32)).astype(bf16)])

    low = low_ref[...].reshape(ROWS, 4 * HD)
    for part in range(2):
        rows = slice(part * 256, (part + 1) * 256)
        for ref, side in ((heads_sent_ref, 1 - co), (heads_kept_ref, co)):
            lanes = pl.ds(pl.multiple_of(part * 512 + side * 256, 256), 256)
            tokens = tokens_ref[:, :, lanes].reshape(ROWS, 256)
            ref[rows] = dot_first(tokens, low).astype(ref.dtype)

    for number in range(4):
        for ref, side in ((left_sent_ref, 1 - x_high), (left_kept_ref, x_high)):
            rows = low_ref[side * 4 + number]
            ref[number] = dot_second(rows, weight_ref[: D // 2]).astype(bf16)
        for ref, side in ((right_sent_ref, 1 - zl), (right_kept_ref, zl)):
            rows = low_ref[2 * number + side]
            ref[number] = dot_second(rows, weight_ref[D // 2 :]).astype(bf16)


def projection_means(*operands):
    return pl.pallas_call(
        means_kernel,
        name="projection_means",
        out_shape=jax.ShapeDtypeStruct((2, ROWS), f32),
        in_specs=[vmem] * 7,
        out_specs=vmem,
        compiler_params=pltpu.CompilerParams(vmem_limit_bytes=32 << 20),
        cost_estimate=pl.CostEstimate(flops=8 << 20, bytes_accessed=6 << 20, transcendentals=0),
    )(*operands)


def projection_grads(info, *operands):
    part = jax.ShapeDtypeStruct((4, BLK, D // 2), bf16)
    return pl.pallas_call(
        raw_grad_kernel,
        name="projection_grads",
        out_shape=(
            jax.ShapeDtypeStruct((512 + 16, 4 * HD), bf16),
            jax.ShapeDtypeStruct((512, 4 * HD), f32),
            jax.ShapeDtypeStruct((8, 4 * HD), f32),
            part,
            part,
            part,
            part,
        ),
        in_specs=[smem] + [vmem] * 11,
        out_specs=[vmem] * 7,
        scratch_shapes=[pltpu.VMEM((8, BLK, 4 * HD), bf16)],
        compiler_params=pltpu.CompilerParams(vmem_limit_bytes=40 << 20),
        cost_estimate=pl.CostEstimate(flops=4 << 30, bytes_accessed=16 << 20, transcendentals=0),
    )(info, *operands)


INNER_AT = 0
DOWN_LOW_AT = INNER_AT + FF // 2
ATT_AT = DOWN_LOW_AT + D
HIDDEN_AT = ATT_AT + HQ // 2
GATE_LOW_AT = HIDDEN_AT + D
UP_LOW_AT = GATE_LOW_AT + FF // 2
MIXED_LOW_AT = UP_LOW_AT + FF // 2
PACK = MIXED_LOW_AT + D


def rows_kernel(
    info_ref, att_ref, tokens_ref, cot_ref, attn_gain_ref, ffn_gain_ref,
    out_own, gate_own, up_own, down_own, mine, other,
    output_ref, own_hbm, sent_hbm, att_grad_ref, hidden_grad_ref, gain_grad_ref,
    own_ref, sent_ref, out_v, gate_v, up_v, down_v, gate_act, up_act, inner_ref, up_low_ref, hidden_ref, sems,
):
    zh, co = info_ref[0], info_ref[1]
    numbers = iter(range(22))

    def copy(source, target):
        return pltpu.make_async_copy(source, target, sems.at[next(numbers)])

    def pieces(own, rows_at, rows, scratch, blocks):
        copies = [copy(own, scratch.at[pl.ds(zh * 32, 32)])]
        for half, core in ((mine, co), (other, 1 - co)):
            at = (1 - zh) * 32 + core * 16
            for block in range(blocks):
                target = scratch.at[pl.ds(at, 16)]
                if blocks > 1:
                    target = scratch.at[pl.ds(at, 16), :, pl.ds(block * D, D)]
                copies.append(
                    copy(half.at[:, pl.ds(rows_at + block * rows, rows), :], target)
                )
        return copies

    out_copies = pieces(out_own, 0, OUT_ROWS, out_v, 1)
    gate_copies = pieces(gate_own, GATE_AT, GATE_ROWS, gate_v, BLOCKS)
    up_copies = pieces(up_own, UP_AT, GATE_ROWS, up_v, BLOCKS)
    down_copies = pieces(down_own, DOWN_AT, DOWN_ROWS, down_v, 1)
    for item in out_copies:
        item.start()

    def put(core, lanes, value):
        @pl.when(core == co)
        def _():
            own_ref[:, lanes] = value

        @pl.when(core != co)
        def _():
            sent_ref[:, lanes] = value

    def put_both(start, value):
        own_ref[:, start : start + D] = value
        sent_ref[:, start : start + D] = value

    for head in range(8):
        rows = att_ref[head].reshape(BLK, 2 * HD)
        inner_ref[:, head * 2 * HD : (head + 1) * 2 * HD] = rows
        start = ATT_AT + ((head // 4) * 2 + head % 2) * 2 * HD
        put((head // 2) % 2, slice(start, start + 2 * HD), rows)
    for item in out_copies:
        item.wait()
    for item in gate_copies + up_copies:
        item.start()
    attn_gain = attn_gain_ref[...]
    mixed = dot_plain(inner_ref[:, :HQ], out_v[...].reshape(HQ, D))
    hidden_grad_ref[...] = mixed
    attn_inverse = lax.rsqrt(jnp.mean(mixed * mixed, axis=-1, keepdims=True) + epsilon)
    hidden = tokens_ref[...].astype(f32) + mixed * attn_inverse * attn_gain
    hidden_ref[...] = hidden
    put_both(HIDDEN_AT, hidden.astype(bf16))
    for item in gate_copies + up_copies:
        item.wait()
    for item in down_copies:
        item.start()
    tile = 8 * DOWN_ROWS

    def act_body(step, carry):
        lanes = pl.ds(step * tile, tile)
        low = own_ref[:, HIDDEN_AT : HIDDEN_AT + D]
        gate = dot_plain(low, gate_v[:, :, lanes].reshape(D, tile))
        up = dot_plain(low, up_v[:, :, lanes].reshape(D, tile))
        gate_act[:, lanes] = gate
        up_act[:, lanes] = up
        inner = (gate * (1.0 / (1.0 + jnp.exp(-gate))) * up).astype(bf16)
        inner_ref[:, lanes] = inner
        column = (step // 4) * 2 + step % 2
        put((step // 2) % 2, pl.ds(pl.multiple_of(INNER_AT + column * tile, HD), tile), inner)
        return carry

    lax.fori_loop(0, FF // tile, act_body, 0)
    for item in down_copies:
        item.wait()
    ffn_gain = ffn_gain_ref[...]
    down = dot_plain(inner_ref[...], down_v[...].reshape(FF, D))
    ffn_inverse = lax.rsqrt(jnp.mean(down * down, axis=-1, keepdims=True) + epsilon)
    normed = down * ffn_inverse
    output_ref[...] = (hidden_ref[...] + normed * ffn_gain).astype(bf16)
    upstream = cot_ref[...].astype(f32)
    scaled = upstream * ffn_gain
    gain_grad_ref[1:2, :] = jnp.sum(upstream * normed, axis=0, keepdims=True)
    down_low = ffn_inverse * (scaled - normed * jnp.mean(scaled * normed, axis=-1, keepdims=True))
    put_both(DOWN_LOW_AT, down_low.astype(bf16))
    def back_body(step, carry):
        lanes = pl.ds(step * tile, tile)
        rows = down_v[pl.ds(step * 8, 8)].reshape(tile, D)
        inner_grad = dot_second(own_ref[:, DOWN_LOW_AT : DOWN_LOW_AT + D], rows)
        gate, up = gate_act[:, lanes], up_act[:, lanes]
        sigmoid = 1.0 / (1.0 + jnp.exp(-gate))
        gate_low = (inner_grad * up * sigmoid * (1.0 + gate * (1.0 - sigmoid))).astype(bf16)
        up_low = (inner_grad * (gate * sigmoid)).astype(bf16)
        column = (step % 4) * tile
        put(step // 4, pl.ds(pl.multiple_of(GATE_LOW_AT + column, HD), tile), gate_low)
        put(step // 4, pl.ds(pl.multiple_of(UP_LOW_AT + column, HD), tile), up_low)
        inner_ref[:, lanes] = gate_low
        up_low_ref[:, lanes] = up_low
        return carry

    lax.fori_loop(0, FF // tile, back_body, 0)
    mixed = hidden_grad_ref[...]
    attn_inverse = lax.rsqrt(jnp.mean(mixed * mixed, axis=-1, keepdims=True) + epsilon)
    normed = mixed * attn_inverse
    hidden_grad = (
        cot_ref[...].astype(f32)
        + dot_second(inner_ref[...], gate_v[...].reshape(D, FF))
        + dot_second(up_low_ref[...], up_v[...].reshape(D, FF))
    )
    scaled = hidden_grad * attn_gain_ref[...]
    gain_grad_ref[0:1, :] = jnp.sum(hidden_grad * normed, axis=0, keepdims=True)
    mixed_low = (
        attn_inverse * (scaled - normed * jnp.mean(scaled * normed, axis=-1, keepdims=True))
    ).astype(bf16)
    put_both(MIXED_LOW_AT, mixed_low)
    packs = [copy(sent_ref, sent_hbm), copy(own_ref, own_hbm)]
    for item in packs:
        item.start()
    hidden_grad_ref[...] = hidden_grad

    def grad_body(head, carry):
        rows = out_v[pl.ds(head * 8, 8)].reshape(2 * HD, D)
        mixed_low = own_ref[:, MIXED_LOW_AT : MIXED_LOW_AT + D]
        grad = dot_second(mixed_low, rows).astype(bf16)
        att_grad_ref[head] = grad.reshape(2, half_blk, 2 * HD)
        return carry

    lax.fori_loop(0, 8, grad_body, 0)
    for item in packs:
        item.wait()


def own_rows(info, attended, tokens, cotangent, attn_gain, ffn_gain, shards, mine, other):
    def shape(*dims, dtype=bf16):
        return jax.ShapeDtypeStruct(dims, dtype)

    return pl.pallas_call(
        rows_kernel,
        name="own_rows",
        out_shape=(
            shape(BLK, D),
            pltpu.HBM((BLK, PACK), bf16),
            pltpu.HBM((BLK, PACK), bf16),
            shape(8, 2, half_blk, 2 * HD),
            shape(BLK, D, dtype=f32),
            shape(2, D, dtype=f32),
        ),
        in_specs=[smem] + [vmem] * 5 + [hbm] * 6,
        out_specs=[vmem, hbm, hbm, vmem, vmem, vmem],
        scratch_shapes=[
            pltpu.VMEM((BLK, PACK), bf16),
            pltpu.VMEM((BLK, PACK), bf16),
            pltpu.VMEM((64, OUT_ROWS, D), bf16),
            pltpu.VMEM((64, GATE_ROWS, FF), bf16),
            pltpu.VMEM((64, GATE_ROWS, FF), bf16),
            pltpu.VMEM((64, DOWN_ROWS, D), bf16),
            pltpu.VMEM((BLK, FF), f32),
            pltpu.VMEM((BLK, FF), f32),
            pltpu.VMEM((BLK, FF), bf16),
            pltpu.VMEM((BLK, FF), bf16),
            pltpu.VMEM((BLK, D), f32),
            pltpu.SemaphoreType.DMA((22,)),
        ],
        compiler_params=pltpu.CompilerParams(vmem_limit_bytes=44 << 20),
        cost_estimate=pl.CostEstimate(
            flops=4 * BLK * (3 * D * FF + HQ * D),
            bytes_accessed=26 << 20,
            transcendentals=2 * BLK * FF,
        ),
    )(info, attended, tokens, cotangent, attn_gain, ffn_gain, *in_hbm(*shards, mine, other))


def wide_rows(array):
    return jnp.concatenate(
        [array[:, start : start + D] for start in range(0, array.shape[1], D)]
    )


def ring_place(bits):
    return bits[0] * 2 + (bits[0] ^ bits[1])


PRODUCTS = (
    (FF // 2, INNER_AT, D, DOWN_LOW_AT, "zB", "zA"),
    (D, HIDDEN_AT, FF // 2, GATE_LOW_AT, "x0", "x1"),
    (D, HIDDEN_AT, FF // 2, UP_LOW_AT, "x1", "x0"),
    (HQ // 2, ATT_AT, D, MIXED_LOW_AT, "zA", "zB"),
)


def product_places():
    places = []
    for *_, first_link, second_link in PRODUCTS:
        for first, second in ((1, 0), (1, 1), (0, 0), (0, 1)):
            bits = {
                first_link: link_bit(first_link) ^ first,
                second_link: link_bit(second_link) ^ second,
            }
            for part in range(2):
                if "zA" in bits:
                    places.append((bits["zB"] * 2 + bits["zA"]) * 2 + part)
                else:
                    places.append(part * 4 + ring_place((bits["x1"], bits["x0"])))
    return jnp.stack(places).astype(jnp.int32)


def products_kernel(places_ref, own_ref, got_ref, *refs):
    outs, (both, sems), lefts, scratch = refs[:8], refs[8:10], refs[10:13], refs[13:]
    lefts = dict(zip((INNER_AT, HIDDEN_AT, ATT_AT), lefts))
    run_copies(
        [
            pltpu.make_async_copy(ref, both.at[pl.ds(core * BLK, BLK)], sems.at[8 + core])
            for core, ref in enumerate((own_ref, got_ref))
        ]
    )
    copies = [
        pltpu.make_async_copy(held, out, sems.at[number])
        for number, (held, out) in enumerate(zip(scratch, outs))
    ]
    for left_at, left in lefts.items():
        columns = slice(left_at, left_at + left.shape[0])
        left[...] = both[:, columns].astype(f32).T.astype(bf16)
    for number, (rows, left_at, width, right_at, *_) in enumerate(PRODUCTS):
        left = lefts[left_at]
        eighth = rows // 8
        for part in range(2):
            out = scratch[2 * number + part]

            starts = [
                pl.multiple_of(places_ref[number * 8 + part * 4 + step] * eighth, eighth)
                for step in range(4)
            ]
            picked = jnp.concatenate([left[pl.ds(start, eighth)] for start in starts])
            out[...] = dot_plain(picked, both[:, right_at : right_at + width]).astype(bf16)
            copies[2 * number + part].start()
    for copy in copies:
        copy.wait()


def weight_products(own, got):
    flops = sum(2 * 2 * BLK * rows * width for rows, _, width, *_ in PRODUCTS)
    return pl.pallas_call(
        products_kernel,
        name="weight_products",
        out_shape=[
            pltpu.HBM((rows // 2, width), bf16)
            for rows, _, width, *_ in PRODUCTS
            for _ in range(2)
        ],
        in_specs=[smem, hbm, hbm],
        out_specs=[hbm] * 8,
        scratch_shapes=[
            pltpu.VMEM((2 * BLK, PACK), bf16),
            pltpu.SemaphoreType.DMA((10,)),
            pltpu.VMEM((FF // 2, 2 * BLK), bf16),
            pltpu.VMEM((D, 2 * BLK), bf16),
            pltpu.VMEM((HQ // 2, 2 * BLK), bf16),
        ]
        + [
            pltpu.VMEM((rows // 2, width), bf16)
            for rows, _, width, *_ in PRODUCTS
            for _ in range(2)
        ],
        compiler_params=pltpu.CompilerParams(vmem_limit_bytes=40 << 20),
        cost_estimate=pl.CostEstimate(flops=flops, bytes_accessed=16 << 20, transcendentals=0),
    )(product_places(), *in_hbm(own, got))


def place_kernel(core_ref, chunk_ref, *refs):
    gate_ref, up_ref, down_ref, out_ref = refs[-4:]
    for y in range(4):
        for part in range(2):
            chunk = chunk_ref[y, 0, part]
            start = (2 * y + part) * GATE_ROWS
            rows = slice(start, start + GATE_ROWS)
            gate_ref[rows, :D] = chunk[:16].astype(f32)
            gate_ref[rows, D:] = chunk[16:32, : D // 2].astype(f32)
            up_ref[rows, : D // 2] = chunk[16:32, D // 2 :].astype(f32)
            up_ref[rows, D // 2 :] = chunk[32:48].astype(f32)
            down_ref[part, y] = chunk[48:72].astype(f32)
            out_ref[part, y] = chunk[72:].astype(f32)


def place_rows(core, chunks, earlier):
    def columns(x, core):
        return (x, core[0])

    def rows(x, core):
        return (core[0], 0, x, 0)

    return pl.pallas_call(
        place_kernel,
        name="place_rows",
        out_shape=(
            jax.ShapeDtypeStruct((D // 2, FF), f32),
            jax.ShapeDtypeStruct((D // 2, FF), f32),
            jax.ShapeDtypeStruct((4, 4, 4 * 24, D), f32),
            jax.ShapeDtypeStruct((4, 4, 4 * 16, D), f32),
        ),
        grid_spec=pltpu.PrefetchScalarGridSpec(
            num_scalar_prefetch=1,
            grid=(4,),
            in_specs=[pl.BlockSpec((4, 1, 2, 88, D), lambda x, core: (0, x, 0, 0, 0))]
            + [hbm] * len(earlier),
            out_specs=[
                pl.BlockSpec((D // 8, FF // 2), columns),
                pl.BlockSpec((D // 8, FF // 2), columns),
                pl.BlockSpec((2, 4, 24, D), rows),
                pl.BlockSpec((2, 4, 16, D), rows),
            ],
        ),
        input_output_aliases={2 + number: number for number in range(len(earlier))},
        compiler_params=pltpu.CompilerParams(vmem_limit_bytes=32 << 20),
        cost_estimate=pl.CostEstimate(flops=3 << 20, bytes_accessed=18 << 20, transcendentals=0),
    )(core, chunks, *earlier)


def place_heads_kernel(core_ref, chunk_ref, *refs):
    query_ref, key_ref, value_ref = refs[-3:]
    for owner in range(8):
        part = chunk_ref[0, owner, :64].astype(f32)
        query_ref[:, owner * 2 * HD : (owner + 1) * 2 * HD] = part[:, : 2 * HD]
        key_ref[:, owner * HD : (owner + 1) * HD] = part[:, 2 * HD : 3 * HD]
        value_ref[:, owner * HD : (owner + 1) * HD] = part[:, 3 * HD :]


def place_heads(core, chunks, earlier):
    def rows(y, core):
        return (core[0] * 4 + y, 0)

    return pl.pallas_call(
        place_heads_kernel,
        name="place_heads",
        out_shape=(
            jax.ShapeDtypeStruct((D // 2, HQ), f32),
            jax.ShapeDtypeStruct((D // 2, HK), f32),
            jax.ShapeDtypeStruct((D // 2, HK), f32),
        ),
        grid_spec=pltpu.PrefetchScalarGridSpec(
            num_scalar_prefetch=1,
            grid=(4,),
            in_specs=[pl.BlockSpec((1, 8, 80, 4 * HD), lambda y, core: (y, 0, 0, 0))]
            + [hbm] * len(earlier),
            out_specs=[
                pl.BlockSpec((64, HQ), rows),
                pl.BlockSpec((64, HK), rows),
                pl.BlockSpec((64, HK), rows),
            ],
        ),
        input_output_aliases={2 + number: number for number in range(len(earlier))},
        compiler_params=pltpu.CompilerParams(vmem_limit_bytes=32 << 20),
        cost_estimate=pl.CostEstimate(flops=1 << 20, bytes_accessed=6 << 20, transcendentals=0),
    )(core, chunks, *earlier)


def per_device(
    tokens,
    doc_lengths,
    query_weight,
    key_weight,
    value_weight,
    out_weight,
    gate_weight,
    up_weight,
    down_weight,
    query_gain,
    key_gain,
    attn_gain,
    ffn_gain,
    cotangent,
):
    y, x, zl, co, zh = (lax.axis_index(name) for name in ("y", "x", "zl", "co", "zh"))
    head = x * 2 + zl
    lengths = doc_lengths[0]
    first_end = lengths[0]
    second_end = lengths[0] + lengths[1]
    info = jnp.stack([y, co, first_end, second_end]).astype(jnp.int32)
    source = tokens[0]

    gains = jnp.concatenate([query_gain, key_gain, attn_gain, ffn_gain])
    shards = (
        out_weight.reshape(32, OUT_ROWS, D),
        gate_weight.reshape(32, GATE_ROWS, FF),
        up_weight.reshape(32, GATE_ROWS, FF),
        down_weight.reshape(32, DOWN_ROWS, D),
    )
    group_tokens = jnp.broadcast_to(source[None], (8, BLK, D))
    places = jnp.stack([co * 16 + y * 4 + x, head, x * 2 + 1 - zl]).astype(jnp.int32)
    group_tokens, places = lax.optimization_barrier((group_tokens, places))
    own_slice, sent_slice, weight_chunk = collect(
        places,
        (query_weight, key_weight, value_weight),
        shards,
        gains,
    )
    got_slice = across(sent_slice, "zB")
    weight_chunk = across(weight_chunk, "zB")
    group_tokens = exchange(group_tokens, HEAD_AXES)
    mine_weights = lax.all_gather(weight_chunk[:CHUNK_ROWS], ("y", "x"), axis=0, tiled=False)
    other_gains = weight_chunk[CHUNK_ROWS:].reshape(-1)[: gains.shape[0]]

    def whole_gain(start, size):
        own = gains[start : start + size]
        got = other_gains[start : start + size]
        return jnp.where(zh == 0, jnp.concatenate([own, got]), jnp.concatenate([got, own]))

    query_scale = lax.dynamic_slice_in_dim(whole_gain(0, 1024), head * 2 * HD, 2 * HD).astype(f32)
    key_scale = lax.dynamic_slice_in_dim(whole_gain(1024, 512), head * HD, HD).astype(f32)
    attn_scale = whole_gain(1536, 512)
    ffn_scale = whole_gain(2048, 512)

    head_gain = jnp.concatenate([query_scale, key_scale])[None]

    index = jnp.arange(group_rows, dtype=jnp.int32)
    positions = jnp.concatenate(
        [half_positions(index, y, co, 0), half_positions(index, y, co, 1)]
    )
    doc_start = jnp.where(
        positions >= second_end, second_end, jnp.where(positions >= first_end, first_end, 0)
    )
    frequency = jnp.power(
        f32(rope_base), -jnp.arange(HD // 2, dtype=f32) * (2.0 / HD)
    )
    angles = (positions - doc_start).astype(f32)[:, None] * frequency[None, :]
    cosine, sine_table = jnp.cos(angles), jnp.sin(angles)
    tables = (
        jnp.concatenate([cosine, cosine], axis=1),
        jnp.concatenate([-sine_table, sine_table], axis=1),
    )

    raw, head_weight, squares = project(
        zh[None].astype(jnp.int32), group_tokens, own_slice, got_slice
    )
    squares = exchange(squares, HEAD_AXES)
    queries, kv = prepare(raw, squares, tables, head_gain)
    pairs = [
        jnp.stack([kv[half], across(kv[half], first)]) for half, first in enumerate(("y0", "y1"))
    ]
    pieces = [
        piece
        for pair, second in zip(pairs, ("y1", "y0"))
        for piece in (pair, across(pair, second))
    ]
    pieces += [across(piece, "co") for piece in pieces]
    pieces, mine_weights = lax.optimization_barrier((pieces, mine_weights))
    other_weights = across(mine_weights, "co")

    attended_low, attended_full, log_total = attention_forward(info, queries, pieces)
    attended_low = exchange(attended_low, HEAD_AXES)
    (
        output,
        own_pack,
        sent_pack,
        attended_grad,
        hidden_grad,
        norm_gain_grads,
    ) = own_rows(
        jnp.stack([zh, co]).astype(jnp.int32),
        attended_low,
        source,
        cotangent[0],
        attn_scale.astype(f32)[None],
        ffn_scale.astype(f32)[None],
        shards,
        mine_weights,
        other_weights,
    )

    grads = exchange(attended_grad, HEAD_AXES)

    products = weight_products(own_pack, across(sent_pack, "co"))
    sent_parts, rest_parts = products[0::2], products[1::2]
    grads, sent_parts = lax.optimization_barrier((grads, sent_parts))
    got_parts = [
        across(sent, first_link)
        for sent, (*_, first_link, _) in zip(sent_parts, PRODUCTS)
    ]

    query_grad, sent, kept = attention_backward(
        info, queries, pieces, grads, attended_full, log_total
    )
    stage = lax.optimization_barrier
    own_core, other_core = co[None].astype(jnp.int32), (1 - co)[None].astype(jnp.int32)

    sent, got_parts = stage((sent, got_parts))
    got = across(sent, "co")
    second_sent = [
        (rest[rest.shape[0] // 2 :].astype(f32) + part[rest.shape[0] // 2 :].astype(f32)).astype(
            bf16
        )
        for rest, part in zip(rest_parts, got_parts)
    ]
    got, second_sent = stage((got, second_sent))
    orders = (("y1", "y0"), ("y0", "y1"))
    kv_got = [
        across((kept[half, 2:].astype(f32) + got[half, 2:].astype(f32)).astype(bf16), first)
        for half, (first, _) in enumerate(orders)
    ]
    second_got = [
        across(part, second_link) for part, (*_, second_link) in zip(second_sent, PRODUCTS)
    ]

    def second_sum(number, arrived):
        rest, part = rest_parts[number], got_parts[number]
        middle = rest.shape[0] // 2
        kept_part = rest[:middle].astype(f32) + part[:middle].astype(f32)
        return (kept_part + arrived.astype(f32)).astype(bf16)

    kv_got = stage(kv_got)
    kv_both = [
        kept[half, :2].astype(f32) + got[half, :2].astype(f32) + kv_got[half].astype(f32)
        for half in range(2)
    ]
    kv_got = [
        across(kv_both[half][1].astype(bf16), second) for half, (_, second) in enumerate(orders)
    ]
    kv_got, second_got = stage((kv_got, second_got))
    down_got, gate_got, up_got, out_got = second_got
    act_part = exchange(
        jnp.concatenate([second_sum(1, gate_got), second_sum(2, up_got)], axis=1).reshape(
            16, 16, FF
        ),
        ("zh", "y", "zl"),
    )
    kv_grad = jnp.concatenate(
        [both[0] + more.astype(f32) for both, more in zip(kv_both, kv_got)]
    )
    operands = (
        raw, squares, *tables, head_gain, query_grad.reshape(ROWS, 2 * HD), kv_grad,
    )
    means = projection_means(*operands)
    for link in ("x0", "x1", "zA"):
        means = means + across(means, link)
    means, act_part, down_got, out_got = stage((means, act_part, down_got, out_got))
    rest_part = exchange(
        jnp.concatenate(
            [second_sum(0, down_got).reshape(16, 24, D), second_sum(3, out_got).reshape(16, 16, D)],
            axis=1,
        ),
        ("y", "x"),
    )

    x_high, x_low = x // 2, x % 2
    heads_sent, heads_kept, gain_sums, left_sent, left, right_sent, right = projection_grads(
        jnp.stack([co, x_high, zl]).astype(jnp.int32),
        *operands,
        means,
        group_tokens,
        head_weight,
        norm_gain_grads,
    )

    def pick(array, number):
        return lax.dynamic_index_in_dim(array, number, 0, keepdims=False)

    def pass_on(both, link, number):
        return pick(both, number).astype(f32), across(pick(both, 1 - number), link)

    def halves(both):
        return both.astype(bf16).reshape(2, both.shape[0] // 2, *both.shape[1:])

    def take_gains(got, kept, sums):
        more = got[-16:].astype(f32)
        return (kept + got[:-16].astype(f32)).astype(bf16), sums + more[:8] + more[8:]

    def with_gains(array, sums):
        return jnp.concatenate([array, high_low(sums).reshape(16, 4 * HD)])

    def halve_heads(chunk, sums, link):
        bit = link_bit(link)
        chunk = chunk.reshape(2, chunk.shape[0] // 2, 4 * HD)
        kept = pick(chunk, bit).astype(f32)
        return kept, across(with_gains(pick(chunk, 1 - bit), sums), link)

    heads_got = across(heads_sent, "co")
    left_got = across(left_sent, "x1")
    right_got = across(right_sent, "zA")
    heads_got, left_got, right_got = stage((heads_got, left_got, right_got))
    rest_part, _ = stage((rest_part, heads_sent))
    chunk = jnp.concatenate(
        [
            wide_rows(jnp.sum(act_part.astype(f32), axis=0).astype(bf16)),
            jnp.sum(rest_part.astype(f32), axis=0).astype(bf16),
        ]
    )
    chunk_got = across(chunk, "zA")
    def beside(start, stop, bit):
        mine, other = chunk[start:stop], chunk_got[start:stop]
        return jnp.where(bit == 0, jnp.stack([mine, other]), jnp.stack([other, mine]))

    chunks = lax.all_gather(
        jnp.concatenate([beside(0, 48, zl), beside(48, 88, link_bit("zA"))], axis=1),
        ("y", "x"),
        axis=0,
        tiled=False,
    ).reshape(4, 4, 2, 88, D)
    heads, gain_sums = take_gains(heads_got, heads_kept, gain_sums)
    heads = jnp.concatenate(
        [
            heads.reshape(8, 64, 4 * HD),
            jnp.broadcast_to(high_low(gain_sums).reshape(1, 16, 4 * HD), (8, 16, 4 * HD)),
        ],
        axis=1,
    )
    heads = exchange(heads, ("zh", "y"))
    left, left_got = pass_on(halves(left.astype(f32) + left_got.astype(f32)), "x0", x_low)
    right, right_got = pass_on(halves(right.astype(f32) + right_got.astype(f32)), "x1", x_high)
    heads, left_got, right_got = stage((heads, left_got, right_got))

    heads = jnp.sum(heads.astype(f32), axis=0)
    gain_sums = heads[64:72] + heads[72:]
    heads = jnp.concatenate([heads[:64].astype(bf16), high_low(gain_sums).reshape(16, 4 * HD)])
    heads = gather_all(heads, ("y", "x", "zl"), 32).reshape(4, 8, 80, 4 * HD)
    left, left_got = pass_on(halves(left + left_got.astype(f32)), "zA", zl)
    right, right_got = pass_on(halves(right + right_got.astype(f32)), "x0", x_low)
    tokens_grad = hidden_grad + jnp.concatenate(
        [
            (left + left_got.astype(f32)).reshape(BLK, D // 2),
            (right + right_got.astype(f32)).reshape(BLK, D // 2),
        ],
        axis=1,
    )
    heads, tokens_grad = stage((heads, tokens_grad))
    other_heads = across(heads, "co")
    placed_heads = place_heads(own_core, heads, ())
    query_weight_grad, key_weight_grad, value_weight_grad = place_heads(
        other_core, other_heads, placed_heads
    )
    chunks, query_weight_grad = stage((chunks, query_weight_grad))
    other_chunks = across(chunks, "co")
    placed = place_rows(own_core, chunks, ())
    gate_weight_grad, up_weight_grad, down_weight_grad, out_weight_grad = place_rows(
        other_core, other_chunks, placed
    )
    down_weight_grad = down_weight_grad.reshape(FF // 2, D)
    out_weight_grad = out_weight_grad.reshape(HQ // 2, D)
    gain_sums = heads[0, :, 64:72].astype(f32) + heads[0, :, 72:].astype(f32)
    query_gain_grad = gain_sums[:, 0, : 2 * HD].reshape(HQ)
    key_gain_grad = gain_sums[:, 0, 2 * HD : 3 * HD].reshape(HK)
    norm_gain_grads = jnp.sum(gain_sums[:, 1:5], axis=0).reshape(2, D)

    def own_gain(gain_grad):
        size = gain_grad.shape[0] // 2
        return lax.dynamic_slice_in_dim(gain_grad, zh * size, size)

    return (
        output[None],
        tokens_grad[None],
        query_weight_grad,
        key_weight_grad,
        value_weight_grad,
        out_weight_grad,
        gate_weight_grad,
        up_weight_grad,
        down_weight_grad,
        own_gain(query_gain_grad.reshape(HQ)),
        own_gain(key_gain_grad.reshape(HK)),
        own_gain(norm_gain_grads[0]),
        own_gain(norm_gain_grads[1]),
    )


def solution(mesh):
    fine = Mesh(mesh.devices.reshape(4, 4, 2, 2, 2), ("y", "x", "zl", "co", "zh"))
    rows = P("zh", TOKEN_AXES, None)
    weight = P("zh", None)
    gain = P("zh")
    return jax.shard_map(
        per_device,
        mesh=fine,
        in_specs=(rows, weight) + (weight,) * 7 + (gain,) * 4 + (rows,),
        out_specs=(rows, rows) + (weight,) * 7 + (gain,) * 4,
        check_vma=False,
    )
```

```python
import functools
import math

import jax
import jax.numpy as jnp
from jax import lax
from jax.experimental import pallas as pl
from jax.experimental.pallas import tpu as pltpu
from jax.sharding import Mesh
from jax.sharding import PartitionSpec as P

D = 1024
HEADS = 16
KVH = 8
HD = 128
FF = 3072
BLK = 128
HQ = 2048
HK = 1024
SEQ = 8192

epsilon = 1e-06
rope_base = 1000000.0
masked_score = -1e30
score_scale = HD**-0.5
log2_scale = score_scale * math.log2(math.e)
half_blk = BLK // 2
group_rows = 8 * half_blk

bf16 = jnp.bfloat16
f32 = jnp.float32

TOKEN_AXES = ("y", "x", "zl", "co")
HEAD_AXES = ("x", "zl")

edge_a = [(0, 1), (1, 0), (2, 3), (3, 2)]
edge_b = [(1, 2), (2, 1), (3, 0), (0, 3)]
swap = [(0, 1), (1, 0)]
LINKS = {
    "x0": ("x", edge_a),
    "x1": ("x", edge_b),
    "y0": ("y", edge_a),
    "y1": ("y", edge_b),
    "zA": ("zl", swap),
    "zB": (("zl", "zh"), [(0, 3), (3, 0), (1, 2), (2, 1)]),
    "zl": ("zl", swap),
    "co": ("co", swap),
    "zh": ("zh", swap),
}


def link_bit(link):
    if link in ("x0", "y0"):
        place = lax.axis_index(link[0])
        return ((place == 1) | (place == 2)).astype(jnp.int32)
    if link in ("x1", "y1"):
        return (lax.axis_index(link[0]) >= 2).astype(jnp.int32)
    if link == "zA":
        return lax.axis_index("zl") ^ lax.axis_index("zh")
    if link == "zB":
        return lax.axis_index("zh")
    return lax.axis_index(link)


def across(array, link):
    axis, pairs = LINKS[link]
    return lax.ppermute(array, axis, pairs)


def dot_plain(left_op, right_op):
    return jnp.dot(left_op, right_op, preferred_element_type=f32)


def dot_second(left_op, right_op):
    return lax.dot_general(
        left_op, right_op, (((1,), (1,)), ((), ())), preferred_element_type=f32
    )


def dot_first(left_op, right_op):
    return lax.dot_general(
        left_op, right_op, (((0,), (0,)), ((), ())), preferred_element_type=f32
    )


def exchange(array, axes):
    return lax.all_to_all(array, axes, 0, 0, tiled=True)


def gather_all(array, axes, count):
    return exchange(jnp.broadcast_to(array[None], (count, *array.shape)), axes)


def double(array, link):
    if link == "zA":
        bit = link_bit(link)
    else:
        place = lax.axis_index(LINKS[link][0])
        bit = place // 2 if link in ("x1", "y1") else place % 2
    got = across(array, link)
    return jnp.where(bit == 0, jnp.concatenate([array, got]), jnp.concatenate([got, array]))


def high_low(values):
    high = values.astype(bf16)
    return jnp.stack([high, (values - high.astype(f32)).astype(bf16)])


def half_positions(index, y, co, half):
    block = 16 * y + 2 * (index // half_blk) + co
    inner = index % half_blk
    return jnp.where(half == 0, block * half_blk + inner, SEQ - (block + 1) * half_blk + inner)


def query_masks(info_ref, half):
    y, co, first_end, second_end = info_ref[0], info_ref[1], info_ref[2], info_ref[3]
    index = lax.broadcasted_iota(jnp.int32, (1, group_rows), 1)
    position = half_positions(index, y, co, half)
    start = jnp.where(position >= second_end, second_end, 0)
    start = jnp.where((position >= first_end) & (position < second_end), first_end, start)
    return position, start, position >= second_end


def pair_mask(group, key_half, query_pos, query_start):
    index = lax.broadcasted_iota(jnp.int32, (group_rows, 1), 0)
    key_pos = half_positions(index, group // 2, group % 2, key_half)
    return (key_pos >= query_start) & (key_pos <= query_pos)


def open_steps(y, half):
    count = jnp.where(half == 0, jnp.maximum(2 * y - 2, 0), 6 + 6 - 2 * y)

    def chunk(step):
        late = step >= 6
        group = jnp.where(late, step - 6 + 2 * y + 2, step + 2)
        return group, jnp.where(late, 1, 0)

    return count, chunk


def masked_steps(y, half):
    count = jnp.where((half == 0) & (y == 0), 2, 4)

    def chunk(step):
        own = step >= 2
        group = jnp.where(own, 2 * y + step - 2, step)
        return group, jnp.where(own, half, 0)

    return count, chunk


def slot_of(group, key_half, y, co):
    other_y = group // 2
    beside, over = other_y == (y ^ 1), other_y == 3 - y
    first = jnp.where(key_half == 0, beside, over)
    second = jnp.where(key_half == 0, over, beside)
    ring = jnp.where(other_y == y, 0, jnp.where(first, 1, jnp.where(second, 2, 3)))
    return (group % 2) ^ co, key_half, ring


def load_chunks(pieces, kvs, sems):
    copies = []
    for number, piece in enumerate(pieces):
        core, half, pair = number // 4, number // 2 % 2, number % 2
        target = kvs.at[core, half, pl.ds(2 * pair, 2)]
        copies.append(pltpu.make_async_copy(piece, target, sems.at[number]))
    for copy in copies:
        copy.start()
    return copies


def forward_kernel(info_ref, query_ref, *refs):
    pieces, (low_ref, full_ref, total_ref), (kvs, sems, qt, top, denom, acc) = (
        refs[:8],
        refs[8:11],
        refs[11:],
    )
    y, co = info_ref[0], info_ref[1]
    for copy in load_chunks(pieces, kvs, sems):
        copy.wait()

    def half_body(half, carry):
        query_pos, query_start, last_doc = query_masks(info_ref, half)
        for head in range(2):
            lanes = slice(head * HD, (head + 1) * HD)
            qt[head] = query_ref[half, :, lanes].astype(f32).T.astype(bf16)
            top[head] = jnp.full((1, group_rows), masked_score, f32)
            denom[head] = jnp.zeros((1, group_rows), f32)
            acc[head] = jnp.zeros((HD, group_rows), f32)

        def step(chunks, masked):
            slots = [slot_of(*chunk, y, co) for chunk in chunks]
            keys = [kvs[(*slot, slice(None), slice(0, HD))] for slot in slots]
            values = [kvs[(*slot, slice(None), slice(HD, 2 * HD))] for slot in slots]
            if masked:
                masks = [pair_mask(*chunk, query_pos, query_start) for chunk in chunks]
            for head in range(2):
                scores = [dot_plain(part, qt[head]) for part in keys]
                if masked:
                    scores = [
                        jnp.where(mask, part, masked_score) for mask, part in zip(masks, scores)
                    ]
                old_top = top[head]
                new_top = old_top
                for part in scores:
                    new_top = jnp.maximum(new_top, jnp.max(part, axis=0, keepdims=True))
                weights = [jnp.exp2(part - new_top) for part in scores]
                rescale = jnp.exp2(old_top - new_top)
                total = denom[head] * rescale
                for part in weights:
                    total += jnp.sum(part, axis=0, keepdims=True)
                denom[head] = total
                acc[head] = (
                    acc[head] * rescale
                    + dot_first(values[0], weights[0].astype(bf16))
                    + dot_first(values[1], weights[1].astype(bf16))
                )
                top[head] = new_top

        count, chunk = open_steps(y, half)

        def open_body(number, inner):
            step((chunk(2 * number), chunk(2 * number + 1)), False)
            return inner

        lax.fori_loop(0, count // 2, open_body, 0)
        for head in range(2):
            top[head] = jnp.where(last_doc, masked_score, top[head])
            denom[head] = jnp.where(last_doc, 0.0, denom[head])
            acc[head] = jnp.where(last_doc, 0.0, acc[head])
        masked_count, masked_chunk = masked_steps(y, half)

        def masked_body(number, inner):
            step((masked_chunk(2 * number), masked_chunk(2 * number + 1)), True)
            return inner

        lax.fori_loop(0, masked_count // 2, masked_body, 0)
        for head in range(2):
            lanes = slice(head * HD, (head + 1) * HD)
            attended = acc[head] / denom[head]
            full_ref[half, head] = attended
            total_ref[half, head] = top[head] + jnp.log2(denom[head])
            rows = attended.T.astype(bf16)
            for owner in range(8):
                low_ref[owner, half, :, lanes] = rows[owner * half_blk : (owner + 1) * half_blk]
        return carry

    lax.fori_loop(0, 2, half_body, 0)


def backward_kernel(info_ref, query_ref, grad_ref, full_ref, total_ref, *refs):
    pieces, (dq_ref, sent_hbm, kept_hbm), (kvs, sems, qt, gt, delta, dqt, dkv) = (
        refs[:8],
        refs[8:11],
        refs[11:],
    )
    y, co = info_ref[0], info_ref[1]

    def grads_of(half, lanes):
        return grad_ref[:, half, :, lanes].reshape(group_rows, HD)

    copies = load_chunks(pieces, kvs, sems)
    dkv[...] = jnp.zeros_like(dkv)
    for copy in copies:
        copy.wait()

    def half_body(half, carry):
        query_pos, query_start, last_doc = query_masks(info_ref, half)
        for head in range(2):
            lanes = slice(head * HD, (head + 1) * HD)
            qt[head] = query_ref[half, :, lanes].astype(f32).T.astype(bf16)
            grad_t = grads_of(half, lanes).astype(f32).T
            gt[head] = grad_t.astype(bf16)
            delta[head] = jnp.sum(grad_t * full_ref[half, head], axis=0, keepdims=True)
            dqt[head] = jnp.zeros((HD, group_rows), f32)

        def step(chunks, masked):
            for head in range(2):
                lanes = slice(head * HD, (head + 1) * HD)
                total = total_ref[half, head]
                if not masked:
                    total = jnp.where(last_doc, -masked_score, total)
                query_total = dqt[head]
                for chunk in chunks:
                    slot = slot_of(*chunk, y, co)
                    key_lanes = (*slot, slice(None), slice(0, HD))
                    value_lanes = (*slot, slice(None), slice(HD, 2 * HD))
                    keys = kvs[key_lanes]
                    scores = dot_plain(keys, qt[head])
                    if masked:
                        mask = pair_mask(*chunk, query_pos, query_start)
                        scores = jnp.where(mask, scores, masked_score)
                    probs = jnp.exp2(scores - total)
                    dkv[value_lanes] += dot_plain(probs.astype(bf16), grads_of(half, lanes))
                    prob_grad = dot_plain(kvs[value_lanes], gt[head])
                    low = (probs * (prob_grad - delta[head])).astype(bf16)
                    dkv[key_lanes] += dot_plain(low, query_ref[half, :, lanes])
                    query_total += dot_first(keys, low)
                dqt[head] = query_total

        count, chunk = open_steps(y, half)

        def open_body(number, inner):
            step((chunk(2 * number), chunk(2 * number + 1)), False)
            return inner

        lax.fori_loop(0, count // 2, open_body, 0)
        masked_count, masked_chunk = masked_steps(y, half)

        def masked_body(number, inner):
            step((masked_chunk(2 * number), masked_chunk(2 * number + 1)), True)
            return inner

        lax.fori_loop(0, masked_count // 2, masked_body, 0)
        for head in range(2):
            lanes = slice(head * HD, (head + 1) * HD)
            dq_ref[half, :, lanes] = dqt[head].T * score_scale
        return carry

    lax.fori_loop(0, 2, half_body, 0)

    def store(core):
        def store_body(number, carry):
            half, ring = number // 4, number % 4
            rows = (core, half, ring)
            kvs[(*rows, slice(None), slice(0, HD))] = (
                dkv[(*rows, slice(None), slice(0, HD))] * math.log(2.0)
            ).astype(bf16)
            kvs[(*rows, slice(None), slice(HD, 2 * HD))] = dkv[
                (*rows, slice(None), slice(HD, 2 * HD))
            ].astype(bf16)
            return carry

        lax.fori_loop(0, 8, store_body, 0)

    stores = [
        pltpu.make_async_copy(kvs.at[1], sent_hbm, sems.at[0]),
        pltpu.make_async_copy(kvs.at[0], kept_hbm, sems.at[1]),
    ]
    store(1)
    stores[0].start()
    store(0)
    stores[1].start()
    for copy in stores:
        copy.wait()


smem = pl.BlockSpec(memory_space=pltpu.SMEM)
vmem = pl.BlockSpec(memory_space=pltpu.VMEM)
hbm = pl.BlockSpec(memory_space=pltpu.HBM)


def in_hbm(*arrays):
    return [pltpu.with_memory_space_constraint(array, pltpu.HBM) for array in arrays]


PAIRS = 4 * 2 * group_rows * 9 * group_rows
CHUNKS = (2, 2, 4, group_rows, 2 * HD)


def attention_forward(info, queries, pieces):
    return pl.pallas_call(
        forward_kernel,
        name="attention_forward",
        out_shape=(
            jax.ShapeDtypeStruct((8, 2, half_blk, 2 * HD), bf16),
            jax.ShapeDtypeStruct((2, 2, HD, group_rows), f32),
            jax.ShapeDtypeStruct((2, 2, 1, group_rows), f32),
        ),
        in_specs=[smem, vmem] + [hbm] * 8,
        out_specs=[vmem] * 3,
        scratch_shapes=[
            pltpu.VMEM(CHUNKS, bf16),
            pltpu.SemaphoreType.DMA((8,)),
            pltpu.VMEM((2, HD, group_rows), bf16),
            pltpu.VMEM((2, 1, group_rows), f32),
            pltpu.VMEM((2, 1, group_rows), f32),
            pltpu.VMEM((2, HD, group_rows), f32),
        ],
        compiler_params=pltpu.CompilerParams(vmem_limit_bytes=24 << 20),
        cost_estimate=pl.CostEstimate(
            flops=2 * 2 * HD * PAIRS, bytes_accessed=8 << 20, transcendentals=PAIRS
        ),
    )(info, queries, *in_hbm(*pieces))


def attention_backward(info, queries, pieces, grads, full, total):
    return pl.pallas_call(
        backward_kernel,
        name="attention_backward",
        out_shape=(
            jax.ShapeDtypeStruct((2, group_rows, 2 * HD), f32),
            pltpu.HBM((2, 4, group_rows, 2 * HD), bf16),
            pltpu.HBM((2, 4, group_rows, 2 * HD), bf16),
        ),
        in_specs=[smem] + [vmem] * 4 + [hbm] * 8,
        out_specs=[vmem, hbm, hbm],
        scratch_shapes=[
            pltpu.VMEM(CHUNKS, bf16),
            pltpu.SemaphoreType.DMA((8,)),
            pltpu.VMEM((2, HD, group_rows), bf16),
            pltpu.VMEM((2, HD, group_rows), bf16),
            pltpu.VMEM((2, 1, group_rows), f32),
            pltpu.VMEM((2, HD, group_rows), f32),
            pltpu.VMEM(CHUNKS, f32),
        ],
        compiler_params=pltpu.CompilerParams(vmem_limit_bytes=36 << 20),
        cost_estimate=pl.CostEstimate(
            flops=5 * 2 * HD * PAIRS, bytes_accessed=12 << 20, transcendentals=PAIRS
        ),
    )(info, queries, grads, full, total, *in_hbm(*pieces))


OUT_ROWS, GATE_ROWS, DOWN_ROWS = HQ // 64, D // 64, FF // 64
BLOCKS = FF // D
GATE_AT = OUT_ROWS
UP_AT = GATE_AT + BLOCKS * GATE_ROWS
DOWN_AT = UP_AT + BLOCKS * GATE_ROWS
CHUNK_ROWS = DOWN_AT + DOWN_ROWS


def run_copies(copies):
    for copy in copies:
        copy.start()
    for copy in copies:
        copy.wait()


def collect_kernel(
    info_ref, query_ref, key_ref, value_ref, out_ref, gate_ref, up_ref, down_ref, gain_ref,
    own_ref, sent_ref, chunk_ref, sems,
):
    place = info_ref[0]
    numbers = iter(range(15))
    copies = []

    def copy(source, target):
        copies.append(pltpu.make_async_copy(source, target, sems.at[next(numbers)]))

    for target, head in ((sent_ref, info_ref[2]), (own_ref, info_ref[1])):
        lanes = pl.ds(pl.multiple_of(head * 2 * HD, 2 * HD), 2 * HD)
        copy(query_ref.at[:, lanes], target.at[:, pl.ds(0, 2 * HD)])
        lanes = pl.ds(pl.multiple_of(head * HD, HD), HD)
        copy(key_ref.at[:, lanes], target.at[:, pl.ds(2 * HD, HD)])
        copy(value_ref.at[:, lanes], target.at[:, pl.ds(3 * HD, HD)])
    copy(out_ref.at[place], chunk_ref.at[pl.ds(0, OUT_ROWS)])
    copy(down_ref.at[place], chunk_ref.at[pl.ds(DOWN_AT, DOWN_ROWS)])
    copy(gain_ref, chunk_ref.at[pl.ds(CHUNK_ROWS, 16)])
    for ref, start in ((gate_ref, GATE_AT), (up_ref, UP_AT)):
        for block in range(BLOCKS):
            copy(
                ref.at[place, :, pl.ds(block * D, D)],
                chunk_ref.at[pl.ds(start + block * GATE_ROWS, GATE_ROWS)],
            )
    run_copies(copies)


def collect(info, projections, shards, gains):
    gain_rows = jnp.pad(gains, (0, 16 * D - gains.shape[0])).reshape(16, D)
    return pl.pallas_call(
        collect_kernel,
        name="collect_chunk",
        out_shape=(
            jax.ShapeDtypeStruct((D // 2, 4 * HD), bf16),
            jax.ShapeDtypeStruct((D // 2, 4 * HD), bf16),
            jax.ShapeDtypeStruct((CHUNK_ROWS + 16, D), bf16),
        ),
        in_specs=[smem] + [hbm] * 8,
        out_specs=[vmem] * 3,
        scratch_shapes=[pltpu.SemaphoreType.DMA((15,))],
        compiler_params=pltpu.CompilerParams(vmem_limit_bytes=60 << 20),
    )(info, *in_hbm(*projections, *shards, gain_rows))


ROWS = 2 * group_rows


def as_lanes(column):
    return jnp.broadcast_to(column, (ROWS, HD)).T[0:1]


def as_rows(row):
    return jnp.broadcast_to(row, (HD, ROWS)).T


def turn(tensor, cosine, sine):
    return tensor * cosine + pltpu.roll(tensor, HD // 2, 1) * sine


def project_kernel(
    info_ref, tokens_hbm, own_ref, got_ref, raw_ref, weight_ref, squares_ref, tokens_ref, sems
):
    zh = info_ref[0]
    loads = [
        pltpu.make_async_copy(tokens_hbm.at[owner], tokens_ref.at[owner], sems.at[owner])
        for owner in range(8)
    ]
    for load in loads:
        load.start()
    weight_ref[pl.ds(pl.multiple_of(zh * (D // 2), D // 2), D // 2)] = own_ref[...]
    weight_ref[pl.ds(pl.multiple_of((1 - zh) * (D // 2), D // 2), D // 2)] = got_ref[...]
    for owner in range(8):
        loads[owner].wait()
        raw = dot_plain(tokens_ref[owner], weight_ref[...])
        for half in range(2):
            start = half * group_rows + owner * half_blk
            raw_ref[start : start + half_blk] = raw[half * half_blk : (half + 1) * half_blk]
    raw = raw_ref[:, : 3 * HD]
    squares = raw * raw
    query = jnp.sum(squares[:, :HD] + squares[:, HD : 2 * HD], axis=1, keepdims=True)
    key = jnp.sum(squares[:, 2 * HD :], axis=1, keepdims=True)
    sums = jnp.concatenate([as_lanes(query), as_lanes(key)])
    for owner in range(8):
        squares_ref[owner] = sums


def project(info, tokens, own_slice, got_slice):
    return pl.pallas_call(
        project_kernel,
        name="project",
        out_shape=(
            jax.ShapeDtypeStruct((ROWS, 4 * HD), f32),
            jax.ShapeDtypeStruct((D, 4 * HD), bf16),
            jax.ShapeDtypeStruct((8, 2, ROWS), f32),
        ),
        in_specs=[smem, hbm, vmem, vmem],
        out_specs=[vmem] * 3,
        scratch_shapes=[pltpu.VMEM((8, BLK, D), bf16), pltpu.SemaphoreType.DMA((8,))],
        compiler_params=pltpu.CompilerParams(vmem_limit_bytes=32 << 20),
        cost_estimate=pl.CostEstimate(
            flops=2 * ROWS * D * 4 * HD, bytes_accessed=6 << 20, transcendentals=0
        ),
    )(info, *in_hbm(tokens), own_slice, got_slice)


def inverses(squares_ref):
    total = jnp.sum(squares_ref[...], axis=0)
    return (
        as_rows(lax.rsqrt(total[0:1] / HQ + epsilon)),
        as_rows(lax.rsqrt(total[1:2] / HK + epsilon)),
    )


def prepare_kernel(raw_ref, squares_ref, cos_ref, sin_ref, gain_ref, query_ref, kv_ref):
    query_inverse, key_inverse = inverses(squares_ref)
    cosine, sine = cos_ref[...], sin_ref[...]
    for head in range(3):
        lanes = slice(head * HD, (head + 1) * HD)
        inverse = query_inverse if head < 2 else key_inverse
        turned = turn(raw_ref[:, lanes] * inverse * gain_ref[:, lanes], cosine, sine)
        if head < 2:
            turned = (turned * log2_scale).astype(bf16)
            query_ref[0, :, lanes] = turned[:group_rows]
            query_ref[1, :, lanes] = turned[group_rows:]
        else:
            turned = turned.astype(bf16)
            values = raw_ref[:, 3 * HD :].astype(bf16)
            for half in range(2):
                rows = slice(half * group_rows, (half + 1) * group_rows)
                kv_ref[half, :, :HD] = turned[rows]
                kv_ref[half, :, HD:] = values[rows]


def prepare(raw, squares, tables, gain):
    return pl.pallas_call(
        prepare_kernel,
        name="prepare",
        out_shape=(
            jax.ShapeDtypeStruct((2, group_rows, 2 * HD), bf16),
            jax.ShapeDtypeStruct((2, group_rows, 2 * HD), bf16),
        ),
        in_specs=[vmem] * 5,
        out_specs=[vmem] * 2,
        compiler_params=pltpu.CompilerParams(vmem_limit_bytes=32 << 20),
        cost_estimate=pl.CostEstimate(flops=8 << 20, bytes_accessed=6 << 20, transcendentals=0),
    )(raw, squares, *tables, gain)


def turned_back(raw_ref, squares_ref, cos_ref, sin_ref, dq_ref, dkv_ref):
    query_inverse, key_inverse = inverses(squares_ref)
    cosine, sine = cos_ref[...], -sin_ref[...]
    for head in range(3):
        lanes = slice(head * HD, (head + 1) * HD)
        inverse = query_inverse if head < 2 else key_inverse
        grad = dq_ref[:, lanes] if head < 2 else dkv_ref[:, :HD]
        yield head, lanes, turn(grad, cosine, sine), raw_ref[:, lanes] * inverse, inverse


def means_kernel(raw_ref, squares_ref, cos_ref, sin_ref, gain_ref, dq_ref, dkv_ref, means_ref):
    products = []
    for _, lanes, upstream, normed, _ in turned_back(
        raw_ref, squares_ref, cos_ref, sin_ref, dq_ref, dkv_ref
    ):
        products.append(upstream * gain_ref[:, lanes] * normed)
    query = jnp.sum(products[0] + products[1], axis=1, keepdims=True)
    key = jnp.sum(products[2], axis=1, keepdims=True)
    means_ref[...] = jnp.concatenate([as_lanes(query), as_lanes(key)])


def raw_grad_kernel(
    info_ref, squares_ref, gain_ref, dkv_ref, means_ref, norm_gains_ref,
    raw_hbm, cos_hbm, sin_hbm, dq_hbm, tokens_hbm, weight_hbm,
    gains_ref, *refs,
):
    outs, held, (raw_ref, cos_ref, sin_ref, dq_ref, tokens_ref, weight_ref, low_ref, sems) = (
        refs[:6],
        refs[6:12],
        refs[12:],
    )
    loads = [
        pltpu.make_async_copy(source, target, sems.at[number])
        for number, (source, target) in enumerate(
            (
                (raw_hbm, raw_ref),
                (cos_hbm, cos_ref),
                (sin_hbm, sin_ref),
                (dq_hbm, dq_ref),
                (tokens_hbm, tokens_ref),
                (weight_hbm, weight_ref),
            )
        )
    ]
    for load in loads:
        load.start()
    stores = [
        pltpu.make_async_copy(source, target, sems.at[6 + number])
        for number, (source, target) in enumerate(zip(held, outs))
    ]
    heads_sent_ref, heads_kept_ref = held[:2]
    left_sent_ref, left_kept_ref, right_sent_ref, right_kept_ref = held[2:]
    for load in loads[:4]:
        load.wait()
    co, x_high, zl = info_ref[0], info_ref[1], info_ref[2]
    means = (as_rows(means_ref[0:1]) / HQ, as_rows(means_ref[1:2]) / HK)

    def place(lanes, low):
        for owner in range(8):
            for half in range(2):
                start = half * group_rows + owner * half_blk
                low_ref[owner, half * half_blk : (half + 1) * half_blk, lanes] = low[
                    start : start + half_blk
                ]

    gains_ref[...] = jnp.zeros((8, 4 * HD), f32)
    for head, lanes, upstream, normed, inverse in turned_back(
        raw_ref, squares_ref, cos_ref, sin_ref, dq_ref, dkv_ref
    ):
        mean = means[0] if head < 2 else means[1]
        place(lanes, (inverse * (upstream * gain_ref[:, lanes] - normed * mean)).astype(bf16))
        gains_ref[0:1, lanes] = jnp.sum(upstream * normed, axis=0, keepdims=True)
    place(slice(3 * HD, 4 * HD), dkv_ref[:, HD:].astype(bf16))
    for row in range(4):
        part = slice((row % 2) * 4 * HD, (row % 2 + 1) * 4 * HD)
        gains_ref[1 + row : 2 + row] = norm_gains_ref[row // 2 : row // 2 + 1, part]
    gains = gains_ref[...]
    high = gains.astype(bf16)
    heads_sent_ref[512:] = jnp.concatenate([high, (gains - high.astype(f32)).astype(bf16)])

    for load in loads[4:]:
        load.wait()
    low = low_ref[...].reshape(ROWS, 4 * HD)
    for part in range(2):
        rows = slice(part * 256, (part + 1) * 256)
        for ref, side in ((heads_sent_ref, 1 - co), (heads_kept_ref, co)):
            lanes = pl.ds(pl.multiple_of(part * 512 + side * 256, 256), 256)
            tokens = tokens_ref[:, :, lanes].reshape(ROWS, 256)
            ref[rows] = dot_first(tokens, low).astype(ref.dtype)
    stores[0].start()
    stores[1].start()

    for number in range(4):
        for ref, side in ((left_sent_ref, 1 - x_high), (left_kept_ref, x_high)):
            rows = low_ref[side * 4 + number]
            ref[number] = dot_second(rows, weight_ref[: D // 2]).astype(bf16)
        for ref, side in ((right_sent_ref, 1 - zl), (right_kept_ref, zl)):
            rows = low_ref[2 * number + side]
            ref[number] = dot_second(rows, weight_ref[D // 2 :]).astype(bf16)
    for store in stores[2:]:
        store.start()
    for store in stores:
        store.wait()


def projection_means(*operands):
    return pl.pallas_call(
        means_kernel,
        name="projection_means",
        out_shape=jax.ShapeDtypeStruct((2, ROWS), f32),
        in_specs=[vmem] * 7,
        out_specs=vmem,
        compiler_params=pltpu.CompilerParams(vmem_limit_bytes=32 << 20),
        cost_estimate=pl.CostEstimate(flops=8 << 20, bytes_accessed=6 << 20, transcendentals=0),
    )(*operands)


def projection_grads(
    info, raw, squares, cosine, sine, gain, dq, dkv, means, tokens, weight, norm_gains
):
    shapes = [((512 + 16, 4 * HD), bf16), ((512, 4 * HD), f32)] + [((4, BLK, D // 2), bf16)] * 4
    large = (raw, cosine, sine, dq, tokens, weight)
    return pl.pallas_call(
        raw_grad_kernel,
        name="projection_grads",
        out_shape=[jax.ShapeDtypeStruct((8, 4 * HD), f32)]
        + [pltpu.HBM(shape, dtype) for shape, dtype in shapes],
        in_specs=[smem] + [vmem] * 5 + [hbm] * 6,
        out_specs=[vmem] + [hbm] * 6,
        scratch_shapes=[pltpu.VMEM(shape, dtype) for shape, dtype in shapes]
        + [pltpu.VMEM(array.shape, array.dtype) for array in large]
        + [pltpu.VMEM((8, BLK, 4 * HD), bf16), pltpu.SemaphoreType.DMA((12,))],
        compiler_params=pltpu.CompilerParams(vmem_limit_bytes=40 << 20),
        cost_estimate=pl.CostEstimate(flops=4 << 30, bytes_accessed=16 << 20, transcendentals=0),
    )(info, squares, gain, dkv, means, norm_gains, *in_hbm(*large))


INNER_AT = 0
DOWN_LOW_AT = INNER_AT + FF // 2
ATT_AT = DOWN_LOW_AT + D
HIDDEN_AT = ATT_AT + HQ // 2
GATE_LOW_AT = HIDDEN_AT + D
UP_LOW_AT = GATE_LOW_AT + FF // 2
MIXED_LOW_AT = UP_LOW_AT + FF // 2
PACK = MIXED_LOW_AT + D


def rows_kernel(
    info_ref, att_ref, tokens_ref, cot_ref, attn_gain_ref, ffn_gain_ref,
    out_own, gate_own, up_own, down_own, mine, other,
    output_ref, own_hbm, sent_hbm, att_grad_ref, hidden_grad_ref, gain_grad_ref,
    own_ref, sent_ref, out_v, gate_v, up_v, down_v, gate_act, up_act, inner_ref, up_low_ref, hidden_ref, sems,
):
    zh, co = info_ref[0], info_ref[1]
    numbers = iter(range(22))

    def copy(source, target):
        return pltpu.make_async_copy(source, target, sems.at[next(numbers)])

    def pieces(own, rows_at, rows, scratch, blocks):
        copies = [copy(own, scratch.at[pl.ds(zh * 32, 32)])]
        for half, core in ((mine, co), (other, 1 - co)):
            at = (1 - zh) * 32 + core * 16
            for block in range(blocks):
                target = scratch.at[pl.ds(at, 16)]
                if blocks > 1:
                    target = scratch.at[pl.ds(at, 16), :, pl.ds(block * D, D)]
                copies.append(
                    copy(half.at[:, pl.ds(rows_at + block * rows, rows), :], target)
                )
        return copies

    out_copies = pieces(out_own, 0, OUT_ROWS, out_v, 1)
    gate_copies = pieces(gate_own, GATE_AT, GATE_ROWS, gate_v, BLOCKS)
    up_copies = pieces(up_own, UP_AT, GATE_ROWS, up_v, BLOCKS)
    down_copies = pieces(down_own, DOWN_AT, DOWN_ROWS, down_v, 1)
    for item in out_copies:
        item.start()

    def put(core, lanes, value):
        @pl.when(core == co)
        def _():
            own_ref[:, lanes] = value

        @pl.when(core != co)
        def _():
            sent_ref[:, lanes] = value

    def put_both(start, value):
        own_ref[:, start : start + D] = value
        sent_ref[:, start : start + D] = value

    for head in range(8):
        rows = att_ref[head].reshape(BLK, 2 * HD)
        inner_ref[:, head * 2 * HD : (head + 1) * 2 * HD] = rows
        start = ATT_AT + ((head // 4) * 2 + head % 2) * 2 * HD
        put((head // 2) % 2, slice(start, start + 2 * HD), rows)
    for item in out_copies:
        item.wait()
    for item in gate_copies + up_copies:
        item.start()
    attn_gain = attn_gain_ref[...]
    mixed = dot_plain(inner_ref[:, :HQ], out_v[...].reshape(HQ, D))
    hidden_grad_ref[...] = mixed
    attn_inverse = lax.rsqrt(jnp.mean(mixed * mixed, axis=-1, keepdims=True) + epsilon)
    hidden = tokens_ref[...].astype(f32) + mixed * attn_inverse * attn_gain
    hidden_ref[...] = hidden
    put_both(HIDDEN_AT, hidden.astype(bf16))
    for item in gate_copies + up_copies:
        item.wait()
    for item in down_copies:
        item.start()
    tile = 8 * DOWN_ROWS

    def act_body(step, carry):
        lanes = pl.ds(step * tile, tile)
        low = own_ref[:, HIDDEN_AT : HIDDEN_AT + D]
        gate = dot_plain(low, gate_v[:, :, lanes].reshape(D, tile))
        up = dot_plain(low, up_v[:, :, lanes].reshape(D, tile))
        gate_act[:, lanes] = gate
        up_act[:, lanes] = up
        inner = (gate * (1.0 / (1.0 + jnp.exp(-gate))) * up).astype(bf16)
        inner_ref[:, lanes] = inner
        column = (step // 4) * 2 + step % 2
        put((step // 2) % 2, pl.ds(pl.multiple_of(INNER_AT + column * tile, HD), tile), inner)
        return carry

    lax.fori_loop(0, FF // tile, act_body, 0)
    for item in down_copies:
        item.wait()
    ffn_gain = ffn_gain_ref[...]
    down = dot_plain(inner_ref[...], down_v[...].reshape(FF, D))
    ffn_inverse = lax.rsqrt(jnp.mean(down * down, axis=-1, keepdims=True) + epsilon)
    normed = down * ffn_inverse
    output_ref[...] = (hidden_ref[...] + normed * ffn_gain).astype(bf16)
    upstream = cot_ref[...].astype(f32)
    scaled = upstream * ffn_gain
    gain_grad_ref[1:2, :] = jnp.sum(upstream * normed, axis=0, keepdims=True)
    down_low = ffn_inverse * (scaled - normed * jnp.mean(scaled * normed, axis=-1, keepdims=True))
    put_both(DOWN_LOW_AT, down_low.astype(bf16))
    def back_body(step, carry):
        lanes = pl.ds(step * tile, tile)
        rows = down_v[pl.ds(step * 8, 8)].reshape(tile, D)
        inner_grad = dot_second(own_ref[:, DOWN_LOW_AT : DOWN_LOW_AT + D], rows)
        gate, up = gate_act[:, lanes], up_act[:, lanes]
        sigmoid = 1.0 / (1.0 + jnp.exp(-gate))
        gate_low = (inner_grad * up * sigmoid * (1.0 + gate * (1.0 - sigmoid))).astype(bf16)
        up_low = (inner_grad * (gate * sigmoid)).astype(bf16)
        column = (step % 4) * tile
        put(step // 4, pl.ds(pl.multiple_of(GATE_LOW_AT + column, HD), tile), gate_low)
        put(step // 4, pl.ds(pl.multiple_of(UP_LOW_AT + column, HD), tile), up_low)
        inner_ref[:, lanes] = gate_low
        up_low_ref[:, lanes] = up_low
        return carry

    lax.fori_loop(0, FF // tile, back_body, 0)
    mixed = hidden_grad_ref[...]
    attn_inverse = lax.rsqrt(jnp.mean(mixed * mixed, axis=-1, keepdims=True) + epsilon)
    normed = mixed * attn_inverse
    hidden_grad = (
        cot_ref[...].astype(f32)
        + dot_second(inner_ref[...], gate_v[...].reshape(D, FF))
        + dot_second(up_low_ref[...], up_v[...].reshape(D, FF))
    )
    scaled = hidden_grad * attn_gain_ref[...]
    gain_grad_ref[0:1, :] = jnp.sum(hidden_grad * normed, axis=0, keepdims=True)
    mixed_low = (
        attn_inverse * (scaled - normed * jnp.mean(scaled * normed, axis=-1, keepdims=True))
    ).astype(bf16)
    put_both(MIXED_LOW_AT, mixed_low)
    packs = [copy(sent_ref, sent_hbm), copy(own_ref, own_hbm)]
    for item in packs:
        item.start()
    hidden_grad_ref[...] = hidden_grad

    def grad_body(head, carry):
        rows = out_v[pl.ds(head * 8, 8)].reshape(2 * HD, D)
        mixed_low = own_ref[:, MIXED_LOW_AT : MIXED_LOW_AT + D]
        grad = dot_second(mixed_low, rows).astype(bf16)
        att_grad_ref[head] = grad.reshape(2, half_blk, 2 * HD)
        return carry

    lax.fori_loop(0, 8, grad_body, 0)
    for item in packs:
        item.wait()


def own_rows(info, attended, tokens, cotangent, attn_gain, ffn_gain, shards, mine, other):
    def shape(*dims, dtype=bf16):
        return jax.ShapeDtypeStruct(dims, dtype)

    return pl.pallas_call(
        rows_kernel,
        name="own_rows",
        out_shape=(
            shape(BLK, D),
            pltpu.HBM((BLK, PACK), bf16),
            pltpu.HBM((BLK, PACK), bf16),
            shape(8, 2, half_blk, 2 * HD),
            shape(BLK, D, dtype=f32),
            shape(2, D, dtype=f32),
        ),
        in_specs=[smem] + [vmem] * 5 + [hbm] * 6,
        out_specs=[vmem, hbm, hbm, vmem, vmem, vmem],
        scratch_shapes=[
            pltpu.VMEM((BLK, PACK), bf16),
            pltpu.VMEM((BLK, PACK), bf16),
            pltpu.VMEM((64, OUT_ROWS, D), bf16),
            pltpu.VMEM((64, GATE_ROWS, FF), bf16),
            pltpu.VMEM((64, GATE_ROWS, FF), bf16),
            pltpu.VMEM((64, DOWN_ROWS, D), bf16),
            pltpu.VMEM((BLK, FF), f32),
            pltpu.VMEM((BLK, FF), f32),
            pltpu.VMEM((BLK, FF), bf16),
            pltpu.VMEM((BLK, FF), bf16),
            pltpu.VMEM((BLK, D), f32),
            pltpu.SemaphoreType.DMA((22,)),
        ],
        compiler_params=pltpu.CompilerParams(vmem_limit_bytes=44 << 20),
        cost_estimate=pl.CostEstimate(
            flops=4 * BLK * (3 * D * FF + HQ * D),
            bytes_accessed=26 << 20,
            transcendentals=2 * BLK * FF,
        ),
    )(info, attended, tokens, cotangent, attn_gain, ffn_gain, *in_hbm(*shards, mine, other))


def wide_rows(array):
    return jnp.concatenate(
        [array[:, start : start + D] for start in range(0, array.shape[1], D)]
    )


def ring_place(bits):
    return bits[0] * 2 + (bits[0] ^ bits[1])


PRODUCTS = (
    (FF // 2, INNER_AT, D, DOWN_LOW_AT, "zB", "zA"),
    (D, HIDDEN_AT, FF // 2, GATE_LOW_AT, "x0", "x1"),
    (D, HIDDEN_AT, FF // 2, UP_LOW_AT, "x1", "x0"),
    (HQ // 2, ATT_AT, D, MIXED_LOW_AT, "zA", "zB"),
)


def product_places():
    places = []
    for *_, first_link, second_link in PRODUCTS:
        for first, second in ((1, 0), (1, 1), (0, 0), (0, 1)):
            bits = {
                first_link: link_bit(first_link) ^ first,
                second_link: link_bit(second_link) ^ second,
            }
            for part in range(2):
                if "zA" in bits:
                    places.append((bits["zB"] * 2 + bits["zA"]) * 2 + part)
                else:
                    places.append(part * 4 + ring_place((bits["x1"], bits["x0"])))
    return jnp.stack(places).astype(jnp.int32)


def products_kernel(places_ref, own_ref, got_ref, *refs):
    outs, (both, sems), lefts, scratch = refs[:8], refs[8:10], refs[10:13], refs[13:]
    lefts = dict(zip((INNER_AT, HIDDEN_AT, ATT_AT), lefts))
    run_copies(
        [
            pltpu.make_async_copy(ref, both.at[pl.ds(core * BLK, BLK)], sems.at[8 + core])
            for core, ref in enumerate((own_ref, got_ref))
        ]
    )
    copies = [
        pltpu.make_async_copy(held, out, sems.at[number])
        for number, (held, out) in enumerate(zip(scratch, outs))
    ]
    for left_at, left in lefts.items():
        columns = slice(left_at, left_at + left.shape[0])
        left[...] = both[:, columns].astype(f32).T.astype(bf16)
    for number, (rows, left_at, width, right_at, *_) in enumerate(PRODUCTS):
        left = lefts[left_at]
        eighth = rows // 8
        for part in range(2):
            out = scratch[2 * number + part]

            starts = [
                pl.multiple_of(places_ref[number * 8 + part * 4 + step] * eighth, eighth)
                for step in range(4)
            ]
            picked = jnp.concatenate([left[pl.ds(start, eighth)] for start in starts])
            out[...] = dot_plain(picked, both[:, right_at : right_at + width]).astype(bf16)
            copies[2 * number + part].start()
    for copy in copies:
        copy.wait()


def weight_products(own, got):
    flops = sum(2 * 2 * BLK * rows * width for rows, _, width, *_ in PRODUCTS)
    return pl.pallas_call(
        products_kernel,
        name="weight_products",
        out_shape=[
            pltpu.HBM((rows // 2, width), bf16)
            for rows, _, width, *_ in PRODUCTS
            for _ in range(2)
        ],
        in_specs=[smem, hbm, hbm],
        out_specs=[hbm] * 8,
        scratch_shapes=[
            pltpu.VMEM((2 * BLK, PACK), bf16),
            pltpu.SemaphoreType.DMA((10,)),
            pltpu.VMEM((FF // 2, 2 * BLK), bf16),
            pltpu.VMEM((D, 2 * BLK), bf16),
            pltpu.VMEM((HQ // 2, 2 * BLK), bf16),
        ]
        + [
            pltpu.VMEM((rows // 2, width), bf16)
            for rows, _, width, *_ in PRODUCTS
            for _ in range(2)
        ],
        compiler_params=pltpu.CompilerParams(vmem_limit_bytes=40 << 20),
        cost_estimate=pl.CostEstimate(flops=flops, bytes_accessed=16 << 20, transcendentals=0),
    )(product_places(), *in_hbm(own, got))


def place_kernel(core_ref, chunk_ref, *refs):
    gate_ref, up_ref, down_ref, out_ref = refs[-4:]
    for y in range(4):
        for part in range(2):
            chunk = chunk_ref[y, 0, part]
            start = (2 * y + part) * GATE_ROWS
            rows = slice(start, start + GATE_ROWS)
            gate_ref[rows, :D] = chunk[:16].astype(f32)
            gate_ref[rows, D:] = chunk[16:32, : D // 2].astype(f32)
            up_ref[rows, : D // 2] = chunk[16:32, D // 2 :].astype(f32)
            up_ref[rows, D // 2 :] = chunk[32:48].astype(f32)
            down_ref[part, y] = chunk[48:72].astype(f32)
            out_ref[part, y] = chunk[72:].astype(f32)


def place_rows(core, chunks, earlier):
    def columns(x, core):
        return (x, core[0])

    def rows(x, core):
        return (core[0], 0, x, 0)

    return pl.pallas_call(
        place_kernel,
        name="place_rows",
        out_shape=(
            jax.ShapeDtypeStruct((D // 2, FF), f32),
            jax.ShapeDtypeStruct((D // 2, FF), f32),
            jax.ShapeDtypeStruct((4, 4, 4 * 24, D), f32),
            jax.ShapeDtypeStruct((4, 4, 4 * 16, D), f32),
        ),
        grid_spec=pltpu.PrefetchScalarGridSpec(
            num_scalar_prefetch=1,
            grid=(4,),
            in_specs=[pl.BlockSpec((4, 1, 2, 88, D), lambda x, core: (0, x, 0, 0, 0))]
            + [hbm] * len(earlier),
            out_specs=[
                pl.BlockSpec((D // 8, FF // 2), columns),
                pl.BlockSpec((D // 8, FF // 2), columns),
                pl.BlockSpec((2, 4, 24, D), rows),
                pl.BlockSpec((2, 4, 16, D), rows),
            ],
        ),
        input_output_aliases={2 + number: number for number in range(len(earlier))},
        compiler_params=pltpu.CompilerParams(vmem_limit_bytes=32 << 20),
        cost_estimate=pl.CostEstimate(flops=3 << 20, bytes_accessed=18 << 20, transcendentals=0),
    )(core, chunks, *earlier)


def place_heads_kernel(core_ref, query_chunk_ref, rest_chunk_ref, *refs):
    query_ref, key_ref, value_ref = refs[-3:]
    for owner in range(8):
        query = query_chunk_ref[owner // 2, 0, owner % 2, :64].astype(f32)
        rest = rest_chunk_ref[0, owner // 2, owner % 2, :64].astype(f32)
        query_ref[:, owner * 2 * HD : (owner + 1) * 2 * HD] = query
        key_ref[:, owner * HD : (owner + 1) * HD] = rest[:, :HD]
        value_ref[:, owner * HD : (owner + 1) * HD] = rest[:, HD:]


def place_heads(core, query, rest, earlier):
    def rows(y, core):
        return (core[0] * 4 + y, 0)

    return pl.pallas_call(
        place_heads_kernel,
        name="place_heads",
        out_shape=(
            jax.ShapeDtypeStruct((D // 2, HQ), f32),
            jax.ShapeDtypeStruct((D // 2, HK), f32),
            jax.ShapeDtypeStruct((D // 2, HK), f32),
        ),
        grid_spec=pltpu.PrefetchScalarGridSpec(
            num_scalar_prefetch=1,
            grid=(4,),
            in_specs=[
                pl.BlockSpec((4, 1, 2, 80, 2 * HD), lambda y, core: (0, y, 0, 0, 0)),
                pl.BlockSpec((1, 4, 2, 80, 2 * HD), lambda y, core: (y, 0, 0, 0, 0)),
            ]
            + [hbm] * len(earlier),
            out_specs=[
                pl.BlockSpec((64, HQ), rows),
                pl.BlockSpec((64, HK), rows),
                pl.BlockSpec((64, HK), rows),
            ],
        ),
        input_output_aliases={3 + number: number for number in range(len(earlier))},
        compiler_params=pltpu.CompilerParams(vmem_limit_bytes=32 << 20),
        cost_estimate=pl.CostEstimate(flops=1 << 20, bytes_accessed=6 << 20, transcendentals=0),
    )(core, query, rest, *earlier)


def per_device(
    tokens,
    doc_lengths,
    query_weight,
    key_weight,
    value_weight,
    out_weight,
    gate_weight,
    up_weight,
    down_weight,
    query_gain,
    key_gain,
    attn_gain,
    ffn_gain,
    cotangent,
):
    y, x, zl, co, zh = (lax.axis_index(name) for name in ("y", "x", "zl", "co", "zh"))
    head = x * 2 + zl
    lengths = doc_lengths[0]
    first_end = lengths[0]
    second_end = lengths[0] + lengths[1]
    info = jnp.stack([y, co, first_end, second_end]).astype(jnp.int32)
    source = tokens[0]

    gains = jnp.concatenate([query_gain, key_gain, attn_gain, ffn_gain])
    shards = (
        out_weight.reshape(32, OUT_ROWS, D),
        gate_weight.reshape(32, GATE_ROWS, FF),
        up_weight.reshape(32, GATE_ROWS, FF),
        down_weight.reshape(32, DOWN_ROWS, D),
    )
    group_tokens = jnp.broadcast_to(source[None], (8, BLK, D))
    places = jnp.stack([co * 16 + y * 4 + x, head, x * 2 + 1 - zl]).astype(jnp.int32)
    group_tokens, places = lax.optimization_barrier((group_tokens, places))
    own_slice, sent_slice, weight_chunk = collect(
        places,
        (query_weight, key_weight, value_weight),
        shards,
        gains,
    )
    got_slice = across(sent_slice, "zB")
    weight_chunk = across(weight_chunk, "zB")
    group_tokens = exchange(group_tokens, HEAD_AXES)
    mine_weights = lax.all_gather(weight_chunk[:CHUNK_ROWS], ("y", "x"), axis=0, tiled=False)
    other_gains = weight_chunk[CHUNK_ROWS:].reshape(-1)[: gains.shape[0]]

    def whole_gain(start, size):
        own = gains[start : start + size]
        got = other_gains[start : start + size]
        return jnp.where(zh == 0, jnp.concatenate([own, got]), jnp.concatenate([got, own]))

    query_scale = lax.dynamic_slice_in_dim(whole_gain(0, 1024), head * 2 * HD, 2 * HD).astype(f32)
    key_scale = lax.dynamic_slice_in_dim(whole_gain(1024, 512), head * HD, HD).astype(f32)
    attn_scale = whole_gain(1536, 512)
    ffn_scale = whole_gain(2048, 512)

    head_gain = jnp.concatenate([query_scale, key_scale])[None]

    index = jnp.arange(group_rows, dtype=jnp.int32)
    positions = jnp.concatenate(
        [half_positions(index, y, co, 0), half_positions(index, y, co, 1)]
    )
    doc_start = jnp.where(
        positions >= second_end, second_end, jnp.where(positions >= first_end, first_end, 0)
    )
    frequency = jnp.power(
        f32(rope_base), -jnp.arange(HD // 2, dtype=f32) * (2.0 / HD)
    )
    angles = (positions - doc_start).astype(f32)[:, None] * frequency[None, :]
    cosine, sine_table = jnp.cos(angles), jnp.sin(angles)
    tables = (
        jnp.concatenate([cosine, cosine], axis=1),
        jnp.concatenate([-sine_table, sine_table], axis=1),
    )

    raw, head_weight, squares = project(
        zh[None].astype(jnp.int32), group_tokens, own_slice, got_slice
    )
    squares = exchange(squares, HEAD_AXES)
    queries, kv = prepare(raw, squares, tables, head_gain)
    pairs = [
        jnp.stack([kv[half], across(kv[half], first)]) for half, first in enumerate(("y0", "y1"))
    ]
    pieces = [
        piece
        for pair, second in zip(pairs, ("y1", "y0"))
        for piece in (pair, across(pair, second))
    ]
    pieces += [across(piece, "co") for piece in pieces]
    pieces, mine_weights = lax.optimization_barrier((pieces, mine_weights))
    other_weights = across(mine_weights, "co")

    attended_low, attended_full, log_total = attention_forward(info, queries, pieces)
    attended_low = exchange(attended_low, HEAD_AXES)
    (
        output,
        own_pack,
        sent_pack,
        attended_grad,
        hidden_grad,
        norm_gain_grads,
    ) = own_rows(
        jnp.stack([zh, co]).astype(jnp.int32),
        attended_low,
        source,
        cotangent[0],
        attn_scale.astype(f32)[None],
        ffn_scale.astype(f32)[None],
        shards,
        mine_weights,
        other_weights,
    )

    grads = exchange(attended_grad, HEAD_AXES)

    products = weight_products(own_pack, across(sent_pack, "co"))
    sent_parts, rest_parts = products[0::2], products[1::2]
    grads, sent_parts = lax.optimization_barrier((grads, sent_parts))
    got_parts = [
        across(sent, first_link)
        for sent, (*_, first_link, _) in zip(sent_parts, PRODUCTS)
    ]

    query_grad, sent, kept = attention_backward(
        info, queries, pieces, grads, attended_full, log_total
    )
    stage = lax.optimization_barrier
    own_core, other_core = co[None].astype(jnp.int32), (1 - co)[None].astype(jnp.int32)

    sent, got_parts = stage((sent, got_parts))
    got = across(sent, "co")
    second_sent = [
        (rest[rest.shape[0] // 2 :].astype(f32) + part[rest.shape[0] // 2 :].astype(f32)).astype(
            bf16
        )
        for rest, part in zip(rest_parts, got_parts)
    ]
    got, second_sent = stage((got, second_sent))
    orders = (("y1", "y0"), ("y0", "y1"))
    kv_got = [
        across((kept[half, 2:].astype(f32) + got[half, 2:].astype(f32)).astype(bf16), first)
        for half, (first, _) in enumerate(orders)
    ]
    second_got = [
        across(part, second_link) for part, (*_, second_link) in zip(second_sent, PRODUCTS)
    ]

    def second_sum(number, arrived):
        rest, part = rest_parts[number], got_parts[number]
        middle = rest.shape[0] // 2
        kept_part = rest[:middle].astype(f32) + part[:middle].astype(f32)
        return (kept_part + arrived.astype(f32)).astype(bf16)

    kv_got = stage(kv_got)
    kv_both = [
        kept[half, :2].astype(f32) + got[half, :2].astype(f32) + kv_got[half].astype(f32)
        for half in range(2)
    ]
    kv_got = [
        across(kv_both[half][1].astype(bf16), second) for half, (_, second) in enumerate(orders)
    ]
    kv_grad = jnp.concatenate(
        [both[0] + more.astype(f32) for both, more in zip(kv_both, kv_got)]
    )
    operands = (
        raw, squares, *tables, head_gain, query_grad.reshape(ROWS, 2 * HD), kv_grad,
    )
    means = projection_means(*operands)
    second_got, _ = stage((second_got, means))
    down_got, gate_got, up_got, out_got = second_got
    act_part = exchange(
        jnp.concatenate([second_sum(1, gate_got), second_sum(2, up_got)], axis=1).reshape(
            16, 16, FF
        ),
        ("zh", "y", "zl"),
    )
    for link in ("x0", "x1", "zA"):
        means = means + across(means, link)
    means, act_part, down_got, out_got = stage((means, act_part, down_got, out_got))
    rest_part = exchange(
        jnp.concatenate(
            [second_sum(0, down_got).reshape(16, 24, D), second_sum(3, out_got).reshape(16, 16, D)],
            axis=1,
        ),
        ("y", "x"),
    )

    x_high, x_low = x // 2, x % 2
    gain_sums, heads_sent, heads_kept, left_sent, left, right_sent, right = projection_grads(
        jnp.stack([co, x_high, zl]).astype(jnp.int32),
        *operands,
        means,
        group_tokens,
        head_weight,
        norm_gain_grads,
    )

    def pick(array, number):
        return lax.dynamic_index_in_dim(array, number, 0, keepdims=False)

    def pass_on(both, link, number):
        return pick(both, number).astype(f32), across(pick(both, 1 - number), link)

    def halves(both):
        return both.astype(bf16).reshape(2, both.shape[0] // 2, *both.shape[1:])

    def take_gains(got, kept, sums):
        more = got[-16:].astype(f32)
        return (kept + got[:-16].astype(f32)).astype(bf16), sums + more[:8] + more[8:]

    def with_gains(array, sums):
        return jnp.concatenate([array, high_low(sums).reshape(16, 4 * HD)])

    def halve_heads(chunk, sums, link):
        bit = link_bit(link)
        chunk = chunk.reshape(2, chunk.shape[0] // 2, 4 * HD)
        kept = pick(chunk, bit).astype(f32)
        return kept, across(with_gains(pick(chunk, 1 - bit), sums), link)

    heads_got = across(heads_sent, "co")
    left_got = across(left_sent, "x1")
    right_got = across(right_sent, "zA")
    rest_part, heads_got = stage((rest_part, heads_got))
    chunk = jnp.concatenate(
        [
            wide_rows(jnp.sum(act_part.astype(f32), axis=0).astype(bf16)),
            jnp.sum(rest_part.astype(f32), axis=0).astype(bf16),
        ]
    )
    chunk_got = across(chunk, "zA")
    def beside(start, stop, bit):
        mine, other = chunk[start:stop], chunk_got[start:stop]
        return jnp.where(bit == 0, jnp.stack([mine, other]), jnp.stack([other, mine]))

    chunks = lax.all_gather(
        jnp.concatenate([beside(0, 48, zl), beside(48, 88, link_bit("zA"))], axis=1),
        ("y", "x"),
        axis=0,
        tiled=False,
    ).reshape(4, 4, 2, 88, D)
    heads, gain_sums = take_gains(heads_got, heads_kept, gain_sums)
    heads = jnp.concatenate(
        [
            heads.reshape(8, 64, 4 * HD),
            jnp.broadcast_to(high_low(gain_sums).reshape(1, 16, 4 * HD), (8, 16, 4 * HD)),
        ],
        axis=1,
    )
    heads = exchange(heads, ("zh", "y"))
    left, left_got = pass_on(halves(left.astype(f32) + left_got.astype(f32)), "x0", x_low)
    right, right_got = pass_on(halves(right.astype(f32) + right_got.astype(f32)), "x1", x_high)
    heads, left_got, right_got = stage((heads, left_got, right_got))
    heads = jnp.sum(heads.astype(f32), axis=0)
    gain_sums = heads[64:72] + heads[72:]
    heads = jnp.concatenate([heads[:64].astype(bf16), high_low(gain_sums).reshape(16, 4 * HD)])
    heads = double(heads[None], "zl")
    head_query, head_rest = heads[:, :, : 2 * HD], heads[:, :, 2 * HD :]
    for query_link, rest_link in (("y0", "x0"), ("y1", "x1"), ("x0", "y0"), ("x1", "y1")):
        head_query, head_rest = double(head_query, query_link), double(head_rest, rest_link)
    head_query = head_query.reshape(4, 4, 2, 80, 2 * HD)
    head_rest = head_rest.reshape(4, 4, 2, 80, 2 * HD)
    left, left_got = pass_on(halves(left + left_got.astype(f32)), "zA", zl)
    right, right_got = pass_on(halves(right + right_got.astype(f32)), "x0", x_low)
    tokens_grad = hidden_grad + jnp.concatenate(
        [
            (left + left_got.astype(f32)).reshape(BLK, D // 2),
            (right + right_got.astype(f32)).reshape(BLK, D // 2),
        ],
        axis=1,
    )
    head_query, head_rest, tokens_grad, chunks = stage(
        (head_query, head_rest, tokens_grad, chunks)
    )
    other_chunks = across(chunks, "co")
    other_heads = across(head_query, "co"), across(head_rest, "co")
    placed = place_rows(own_core, chunks, ())
    placed_heads = place_heads(own_core, head_query, head_rest, ())
    gate_weight_grad, up_weight_grad, down_weight_grad, out_weight_grad = place_rows(
        other_core, other_chunks, placed
    )
    query_weight_grad, key_weight_grad, value_weight_grad = place_heads(
        other_core, *other_heads, placed_heads
    )
    down_weight_grad = down_weight_grad.reshape(FF // 2, D)
    out_weight_grad = out_weight_grad.reshape(HQ // 2, D)
    def gain_of(rows):
        return rows[..., 64, :].astype(f32) + rows[..., 72, :].astype(f32)

    query_gain_grad = gain_of(head_query[:, 0]).reshape(HQ)
    key_gain_grad = gain_of(head_rest[0])[..., :HD].reshape(HK)

    def norm_gains(rows):
        return jnp.sum(
            rows[:, :, 65:69].astype(f32) + rows[:, :, 73:77].astype(f32), axis=(0, 1)
        )

    norm_gain_grads = jnp.concatenate(
        [norm_gains(head_query[:, 0]), norm_gains(head_rest[0])], axis=1
    ).reshape(2, D)

    def own_gain(gain_grad):
        size = gain_grad.shape[0] // 2
        return lax.dynamic_slice_in_dim(gain_grad, zh * size, size)

    return (
        output[None],
        tokens_grad[None],
        query_weight_grad,
        key_weight_grad,
        value_weight_grad,
        out_weight_grad,
        gate_weight_grad,
        up_weight_grad,
        down_weight_grad,
        own_gain(query_gain_grad.reshape(HQ)),
        own_gain(key_gain_grad.reshape(HK)),
        own_gain(norm_gain_grads[0]),
        own_gain(norm_gain_grads[1]),
    )


def solution(mesh):
    fine = Mesh(mesh.devices.reshape(4, 4, 2, 2, 2), ("y", "x", "zl", "co", "zh"))
    rows = P("zh", TOKEN_AXES, None)
    weight = P("zh", None)
    gain = P("zh")
    return jax.shard_map(
        per_device,
        mesh=fine,
        in_specs=(rows, weight) + (weight,) * 7 + (gain,) * 4 + (rows,),
        out_specs=(rows, rows) + (weight,) * 7 + (gain,) * 4,
        check_vma=False,
    )
```

```python
import functools
import math

import jax
import jax.numpy as jnp
from jax import lax
from jax.experimental import pallas as pl
from jax.experimental.pallas import tpu as pltpu
from jax.sharding import Mesh
from jax.sharding import PartitionSpec as P

D = 1024
HEADS = 16
KVH = 8
HD = 128
FF = 3072
BLK = 128
HQ = 2048
HK = 1024
SEQ = 8192

epsilon = 1e-06
rope_base = 1000000.0
masked_score = -1e30
score_scale = HD**-0.5
log2_scale = score_scale * math.log2(math.e)
half_blk = BLK // 2
group_rows = 8 * half_blk

bf16 = jnp.bfloat16
f32 = jnp.float32

TOKEN_AXES = ("y", "x", "zl", "co")
HEAD_AXES = ("x", "zl")

edge_a = [(0, 1), (1, 0), (2, 3), (3, 2)]
edge_b = [(1, 2), (2, 1), (3, 0), (0, 3)]
swap = [(0, 1), (1, 0)]
LINKS = {
    "x0": ("x", edge_a),
    "x1": ("x", edge_b),
    "y0": ("y", edge_a),
    "y1": ("y", edge_b),
    "zA": ("zl", swap),
    "zB": (("zl", "zh"), [(0, 3), (3, 0), (1, 2), (2, 1)]),
    "zl": ("zl", swap),
    "co": ("co", swap),
    "zh": ("zh", swap),
}


def link_bit(link):
    if link in ("x0", "y0"):
        place = lax.axis_index(link[0])
        return ((place == 1) | (place == 2)).astype(jnp.int32)
    if link in ("x1", "y1"):
        return (lax.axis_index(link[0]) >= 2).astype(jnp.int32)
    if link == "zA":
        return lax.axis_index("zl") ^ lax.axis_index("zh")
    if link == "zB":
        return lax.axis_index("zh")
    return lax.axis_index(link)


def across(array, link):
    axis, pairs = LINKS[link]
    return lax.ppermute(array, axis, pairs)


def dot_plain(left_op, right_op):
    return jnp.dot(left_op, right_op, preferred_element_type=f32)


def dot_second(left_op, right_op):
    return lax.dot_general(
        left_op, right_op, (((1,), (1,)), ((), ())), preferred_element_type=f32
    )


def dot_first(left_op, right_op):
    return lax.dot_general(
        left_op, right_op, (((0,), (0,)), ((), ())), preferred_element_type=f32
    )


def exchange(array, axes):
    return lax.all_to_all(array, axes, 0, 0, tiled=True)


def gather_all(array, axes, count):
    return exchange(jnp.broadcast_to(array[None], (count, *array.shape)), axes)


def double(array, link):
    if link == "zA":
        bit = link_bit(link)
    else:
        place = lax.axis_index(LINKS[link][0])
        bit = place // 2 if link in ("x1", "y1") else place % 2
    got = across(array, link)
    return jnp.where(bit == 0, jnp.concatenate([array, got]), jnp.concatenate([got, array]))


def high_low(values):
    high = values.astype(bf16)
    return jnp.stack([high, (values - high.astype(f32)).astype(bf16)])


def half_positions(index, y, co, half):
    block = 16 * y + 2 * (index // half_blk) + co
    inner = index % half_blk
    return jnp.where(half == 0, block * half_blk + inner, SEQ - (block + 1) * half_blk + inner)


def query_masks(info_ref, half):
    y, co, first_end, second_end = info_ref[0], info_ref[1], info_ref[2], info_ref[3]
    index = lax.broadcasted_iota(jnp.int32, (1, group_rows), 1)
    position = half_positions(index, y, co, half)
    start = jnp.where(position >= second_end, second_end, 0)
    start = jnp.where((position >= first_end) & (position < second_end), first_end, start)
    return position, start, position >= second_end


def pair_mask(group, key_half, query_pos, query_start):
    index = lax.broadcasted_iota(jnp.int32, (group_rows, 1), 0)
    key_pos = half_positions(index, group // 2, group % 2, key_half)
    return (key_pos >= query_start) & (key_pos <= query_pos)


def open_steps(y, half):
    count = jnp.where(half == 0, jnp.maximum(2 * y - 2, 0), 6 + 6 - 2 * y)

    def chunk(step):
        late = step >= 6
        group = jnp.where(late, step - 6 + 2 * y + 2, step + 2)
        return group, jnp.where(late, 1, 0)

    return count, chunk


def masked_steps(y, half):
    count = jnp.where((half == 0) & (y == 0), 2, 4)

    def chunk(step):
        own = step >= 2
        group = jnp.where(own, 2 * y + step - 2, step)
        return group, jnp.where(own, half, 0)

    return count, chunk


def slot_of(group, key_half, y, co):
    other_y = group // 2
    beside, over = other_y == (y ^ 1), other_y == 3 - y
    first = jnp.where(key_half == 0, beside, over)
    second = jnp.where(key_half == 0, over, beside)
    ring = jnp.where(other_y == y, 0, jnp.where(first, 1, jnp.where(second, 2, 3)))
    return (group % 2) ^ co, key_half, ring


def load_chunks(pieces, kvs, sems):
    copies = []
    for number, piece in enumerate(pieces):
        core, half, pair = number // 4, number // 2 % 2, number % 2
        target = kvs.at[core, half, pl.ds(2 * pair, 2)]
        copies.append(pltpu.make_async_copy(piece, target, sems.at[number]))
    for copy in copies:
        copy.start()
    return copies


def forward_kernel(info_ref, query_ref, *refs):
    pieces, (low_ref, full_ref, total_ref), (kvs, sems, qt, top, denom, acc) = (
        refs[:8],
        refs[8:11],
        refs[11:],
    )
    y, co = info_ref[0], info_ref[1]
    for copy in load_chunks(pieces, kvs, sems):
        copy.wait()

    def half_body(half, carry):
        query_pos, query_start, last_doc = query_masks(info_ref, half)
        for head in range(2):
            lanes = slice(head * HD, (head + 1) * HD)
            qt[head] = query_ref[half, :, lanes].astype(f32).T.astype(bf16)
            top[head] = jnp.full((1, group_rows), masked_score, f32)
            denom[head] = jnp.zeros((1, group_rows), f32)
            acc[head] = jnp.zeros((HD, group_rows), f32)

        def step(chunks, masked):
            slots = [slot_of(*chunk, y, co) for chunk in chunks]
            keys = [kvs[(*slot, slice(None), slice(0, HD))] for slot in slots]
            values = [kvs[(*slot, slice(None), slice(HD, 2 * HD))] for slot in slots]
            if masked:
                masks = [pair_mask(*chunk, query_pos, query_start) for chunk in chunks]
            for head in range(2):
                scores = [dot_plain(part, qt[head]) for part in keys]
                if masked:
                    scores = [
                        jnp.where(mask, part, masked_score) for mask, part in zip(masks, scores)
                    ]
                old_top = top[head]
                new_top = old_top
                for part in scores:
                    new_top = jnp.maximum(new_top, jnp.max(part, axis=0, keepdims=True))
                weights = [jnp.exp2(part - new_top) for part in scores]
                rescale = jnp.exp2(old_top - new_top)
                total = denom[head] * rescale
                for part in weights:
                    total += jnp.sum(part, axis=0, keepdims=True)
                denom[head] = total
                acc[head] = (
                    acc[head] * rescale
                    + dot_first(values[0], weights[0].astype(bf16))
                    + dot_first(values[1], weights[1].astype(bf16))
                )
                top[head] = new_top

        count, chunk = open_steps(y, half)

        def open_body(number, inner):
            step((chunk(2 * number), chunk(2 * number + 1)), False)
            return inner

        lax.fori_loop(0, count // 2, open_body, 0)
        for head in range(2):
            top[head] = jnp.where(last_doc, masked_score, top[head])
            denom[head] = jnp.where(last_doc, 0.0, denom[head])
            acc[head] = jnp.where(last_doc, 0.0, acc[head])
        masked_count, masked_chunk = masked_steps(y, half)

        def masked_body(number, inner):
            step((masked_chunk(2 * number), masked_chunk(2 * number + 1)), True)
            return inner

        lax.fori_loop(0, masked_count // 2, masked_body, 0)
        for head in range(2):
            lanes = slice(head * HD, (head + 1) * HD)
            attended = acc[head] / denom[head]
            full_ref[half, head] = attended
            total_ref[half, head] = top[head] + jnp.log2(denom[head])
            rows = attended.T.astype(bf16)
            for owner in range(8):
                low_ref[owner, half, :, lanes] = rows[owner * half_blk : (owner + 1) * half_blk]
        return carry

    lax.fori_loop(0, 2, half_body, 0)


def backward_kernel(info_ref, query_ref, grad_ref, full_ref, total_ref, *refs):
    pieces, (dq_ref, sent_hbm, kept_hbm), (kvs, sems, qt, gt, delta, dqt, dkv) = (
        refs[:8],
        refs[8:11],
        refs[11:],
    )
    y, co = info_ref[0], info_ref[1]

    def grads_of(half, lanes):
        return grad_ref[:, half, :, lanes].reshape(group_rows, HD)

    copies = load_chunks(pieces, kvs, sems)
    dkv[...] = jnp.zeros_like(dkv)
    for copy in copies:
        copy.wait()

    def half_body(half, carry):
        query_pos, query_start, last_doc = query_masks(info_ref, half)
        for head in range(2):
            lanes = slice(head * HD, (head + 1) * HD)
            qt[head] = query_ref[half, :, lanes].astype(f32).T.astype(bf16)
            grad_t = grads_of(half, lanes).astype(f32).T
            gt[head] = grad_t.astype(bf16)
            delta[head] = jnp.sum(grad_t * full_ref[half, head], axis=0, keepdims=True)
            dqt[head] = jnp.zeros((HD, group_rows), f32)

        def step(chunks, masked):
            masks = [pair_mask(*chunk, query_pos, query_start) if masked else None for chunk in chunks]
            for head in range(2):
                lanes = slice(head * HD, (head + 1) * HD)
                total = total_ref[half, head]
                if not masked:
                    total = jnp.where(last_doc, -masked_score, total)
                query_total = dqt[head]
                for chunk, mask in zip(chunks, masks):
                    slot = slot_of(*chunk, y, co)
                    key_lanes = (*slot, slice(None), slice(0, HD))
                    value_lanes = (*slot, slice(None), slice(HD, 2 * HD))
                    keys = kvs[key_lanes]
                    scores = dot_plain(keys, qt[head])
                    if masked:
                        scores = jnp.where(mask, scores, masked_score)
                    probs = jnp.exp2(scores - total)
                    dkv[value_lanes] += dot_plain(probs.astype(bf16), grads_of(half, lanes))
                    prob_grad = dot_plain(kvs[value_lanes], gt[head])
                    low = (probs * (prob_grad - delta[head])).astype(bf16)
                    dkv[key_lanes] += dot_plain(low, query_ref[half, :, lanes])
                    query_total += dot_first(keys, low)
                dqt[head] = query_total

        count, chunk = open_steps(y, half)

        def open_body(number, inner):
            step((chunk(2 * number), chunk(2 * number + 1)), False)
            return inner

        lax.fori_loop(0, count // 2, open_body, 0)
        masked_count, masked_chunk = masked_steps(y, half)

        def masked_body(number, inner):
            step((masked_chunk(2 * number), masked_chunk(2 * number + 1)), True)
            return inner

        lax.fori_loop(0, masked_count // 2, masked_body, 0)
        for head in range(2):
            lanes = slice(head * HD, (head + 1) * HD)
            dq_ref[half, :, lanes] = dqt[head].T * score_scale
        return carry

    lax.fori_loop(0, 2, half_body, 0)

    def store(core):
        def store_body(number, carry):
            half, ring = number // 4, number % 4
            rows = (core, half, ring)
            kvs[(*rows, slice(None), slice(0, HD))] = (
                dkv[(*rows, slice(None), slice(0, HD))] * math.log(2.0)
            ).astype(bf16)
            kvs[(*rows, slice(None), slice(HD, 2 * HD))] = dkv[
                (*rows, slice(None), slice(HD, 2 * HD))
            ].astype(bf16)
            return carry

        lax.fori_loop(0, 8, store_body, 0)

    stores = [
        pltpu.make_async_copy(kvs.at[1], sent_hbm, sems.at[0]),
        pltpu.make_async_copy(kvs.at[0], kept_hbm, sems.at[1]),
    ]
    store(1)
    stores[0].start()
    store(0)
    stores[1].start()
    for copy in stores:
        copy.wait()


smem = pl.BlockSpec(memory_space=pltpu.SMEM)
vmem = pl.BlockSpec(memory_space=pltpu.VMEM)
hbm = pl.BlockSpec(memory_space=pltpu.HBM)


def in_hbm(*arrays):
    return [pltpu.with_memory_space_constraint(array, pltpu.HBM) for array in arrays]


PAIRS = 4 * 2 * group_rows * 9 * group_rows
CHUNKS = (2, 2, 4, group_rows, 2 * HD)


def attention_forward(info, queries, pieces):
    return pl.pallas_call(
        forward_kernel,
        name="attention_forward",
        out_shape=(
            jax.ShapeDtypeStruct((8, 2, half_blk, 2 * HD), bf16),
            jax.ShapeDtypeStruct((2, 2, HD, group_rows), f32),
            jax.ShapeDtypeStruct((2, 2, 1, group_rows), f32),
        ),
        in_specs=[smem, vmem] + [hbm] * 8,
        out_specs=[vmem] * 3,
        scratch_shapes=[
            pltpu.VMEM(CHUNKS, bf16),
            pltpu.SemaphoreType.DMA((8,)),
            pltpu.VMEM((2, HD, group_rows), bf16),
            pltpu.VMEM((2, 1, group_rows), f32),
            pltpu.VMEM((2, 1, group_rows), f32),
            pltpu.VMEM((2, HD, group_rows), f32),
        ],
        compiler_params=pltpu.CompilerParams(vmem_limit_bytes=24 << 20),
        cost_estimate=pl.CostEstimate(
            flops=2 * 2 * HD * PAIRS, bytes_accessed=8 << 20, transcendentals=PAIRS
        ),
    )(info, queries, *in_hbm(*pieces))


def attention_backward(info, queries, pieces, grads, full, total):
    return pl.pallas_call(
        backward_kernel,
        name="attention_backward",
        out_shape=(
            jax.ShapeDtypeStruct((2, group_rows, 2 * HD), f32),
            pltpu.HBM((2, 4, group_rows, 2 * HD), bf16),
            pltpu.HBM((2, 4, group_rows, 2 * HD), bf16),
        ),
        in_specs=[smem] + [vmem] * 4 + [hbm] * 8,
        out_specs=[vmem, hbm, hbm],
        scratch_shapes=[
            pltpu.VMEM(CHUNKS, bf16),
            pltpu.SemaphoreType.DMA((8,)),
            pltpu.VMEM((2, HD, group_rows), bf16),
            pltpu.VMEM((2, HD, group_rows), bf16),
            pltpu.VMEM((2, 1, group_rows), f32),
            pltpu.VMEM((2, HD, group_rows), f32),
            pltpu.VMEM(CHUNKS, f32),
        ],
        compiler_params=pltpu.CompilerParams(vmem_limit_bytes=36 << 20),
        cost_estimate=pl.CostEstimate(
            flops=5 * 2 * HD * PAIRS, bytes_accessed=12 << 20, transcendentals=PAIRS
        ),
    )(info, queries, grads, full, total, *in_hbm(*pieces))


OUT_ROWS, GATE_ROWS, DOWN_ROWS = HQ // 64, D // 64, FF // 64
BLOCKS = FF // D
GATE_AT = OUT_ROWS
UP_AT = GATE_AT + BLOCKS * GATE_ROWS
DOWN_AT = UP_AT + BLOCKS * GATE_ROWS
CHUNK_ROWS = DOWN_AT + DOWN_ROWS


def run_copies(copies):
    for copy in copies:
        copy.start()
    for copy in copies:
        copy.wait()


def collect_kernel(
    info_ref, query_ref, key_ref, value_ref, out_ref, gate_ref, up_ref, down_ref, gain_ref,
    own_ref, sent_ref, chunk_ref, sems,
):
    place = info_ref[0]
    numbers = iter(range(15))
    copies = []

    def copy(source, target):
        copies.append(pltpu.make_async_copy(source, target, sems.at[next(numbers)]))

    for target, head in ((sent_ref, info_ref[2]), (own_ref, info_ref[1])):
        lanes = pl.ds(pl.multiple_of(head * 2 * HD, 2 * HD), 2 * HD)
        copy(query_ref.at[:, lanes], target.at[:, pl.ds(0, 2 * HD)])
        lanes = pl.ds(pl.multiple_of(head * HD, HD), HD)
        copy(key_ref.at[:, lanes], target.at[:, pl.ds(2 * HD, HD)])
        copy(value_ref.at[:, lanes], target.at[:, pl.ds(3 * HD, HD)])
    copy(out_ref.at[place], chunk_ref.at[pl.ds(0, OUT_ROWS)])
    copy(down_ref.at[place], chunk_ref.at[pl.ds(DOWN_AT, DOWN_ROWS)])
    copy(gain_ref, chunk_ref.at[pl.ds(CHUNK_ROWS, 16)])
    for ref, start in ((gate_ref, GATE_AT), (up_ref, UP_AT)):
        for block in range(BLOCKS):
            copy(
                ref.at[place, :, pl.ds(block * D, D)],
                chunk_ref.at[pl.ds(start + block * GATE_ROWS, GATE_ROWS)],
            )
    run_copies(copies)


def collect(info, projections, shards, gains):
    gain_rows = jnp.pad(gains, (0, 16 * D - gains.shape[0])).reshape(16, D)
    return pl.pallas_call(
        collect_kernel,
        name="collect_chunk",
        out_shape=(
            jax.ShapeDtypeStruct((D // 2, 4 * HD), bf16),
            jax.ShapeDtypeStruct((D // 2, 4 * HD), bf16),
            jax.ShapeDtypeStruct((CHUNK_ROWS + 16, D), bf16),
        ),
        in_specs=[smem] + [hbm] * 8,
        out_specs=[vmem] * 3,
        scratch_shapes=[pltpu.SemaphoreType.DMA((15,))],
        compiler_params=pltpu.CompilerParams(vmem_limit_bytes=60 << 20),
    )(info, *in_hbm(*projections, *shards, gain_rows))


ROWS = 2 * group_rows


def as_lanes(column):
    return jnp.broadcast_to(column, (ROWS, HD)).T[0:1]


def as_rows(row):
    return jnp.broadcast_to(row, (HD, ROWS)).T


def turn(tensor, cosine, sine):
    return tensor * cosine + pltpu.roll(tensor, HD // 2, 1) * sine


def token_loads(left_hbm, right_hbm, tokens_ref, sems):
    columns = pl.ds(0, D // 2), pl.ds(D // 2, D // 2)
    loads = [
        pltpu.make_async_copy(left_hbm.at[zl], tokens_ref.at[:, zl, :, columns[0]], sems.at[zl])
        for zl in range(2)
    ]
    return loads + [
        pltpu.make_async_copy(right_hbm, tokens_ref.at[:, :, :, columns[1]], sems.at[2])
    ]


def project_kernel(
    info_ref, left_hbm, right_hbm, own_ref, got_ref, raw_ref, weight_ref, squares_ref,
    tokens_ref, sems,
):
    zh = info_ref[0]
    loads = token_loads(left_hbm, right_hbm, tokens_ref, sems)
    for load in loads:
        load.start()
    weight_ref[pl.ds(pl.multiple_of(zh * (D // 2), D // 2), D // 2)] = own_ref[...]
    weight_ref[pl.ds(pl.multiple_of((1 - zh) * (D // 2), D // 2), D // 2)] = got_ref[...]
    for load in loads:
        load.wait()
    for owner in range(8):
        raw = dot_plain(tokens_ref[owner // 2, owner % 2], weight_ref[...])
        for half in range(2):
            start = half * group_rows + owner * half_blk
            raw_ref[start : start + half_blk] = raw[half * half_blk : (half + 1) * half_blk]
    raw = raw_ref[:, : 3 * HD]
    squares = raw * raw
    query = jnp.sum(squares[:, :HD] + squares[:, HD : 2 * HD], axis=1, keepdims=True)
    key = jnp.sum(squares[:, 2 * HD :], axis=1, keepdims=True)
    sums = jnp.concatenate([as_lanes(query), as_lanes(key)])
    for owner in range(8):
        squares_ref[owner] = sums


def project(info, left, right, own_slice, got_slice):
    return pl.pallas_call(
        project_kernel,
        name="project",
        out_shape=(
            jax.ShapeDtypeStruct((ROWS, 4 * HD), f32),
            jax.ShapeDtypeStruct((D, 4 * HD), bf16),
            jax.ShapeDtypeStruct((8, 2, ROWS), f32),
        ),
        in_specs=[smem, hbm, hbm, vmem, vmem],
        out_specs=[vmem] * 3,
        scratch_shapes=[pltpu.VMEM((4, 2, BLK, D), bf16), pltpu.SemaphoreType.DMA((3,))],
        compiler_params=pltpu.CompilerParams(vmem_limit_bytes=32 << 20),
        cost_estimate=pl.CostEstimate(
            flops=2 * ROWS * D * 4 * HD, bytes_accessed=6 << 20, transcendentals=0
        ),
    )(info, *in_hbm(left, right), own_slice, got_slice)


def inverses(squares_ref):
    total = jnp.sum(squares_ref[...], axis=0)
    return (
        as_rows(lax.rsqrt(total[0:1] / HQ + epsilon)),
        as_rows(lax.rsqrt(total[1:2] / HK + epsilon)),
    )


def prepare_kernel(raw_ref, squares_ref, cos_ref, sin_ref, gain_ref, query_ref, kv_ref):
    query_inverse, key_inverse = inverses(squares_ref)
    cosine, sine = cos_ref[...], sin_ref[...]
    for head in range(3):
        lanes = slice(head * HD, (head + 1) * HD)
        inverse = query_inverse if head < 2 else key_inverse
        turned = turn(raw_ref[:, lanes] * inverse * gain_ref[:, lanes], cosine, sine)
        if head < 2:
            turned = (turned * log2_scale).astype(bf16)
            query_ref[0, :, lanes] = turned[:group_rows]
            query_ref[1, :, lanes] = turned[group_rows:]
        else:
            turned = turned.astype(bf16)
            values = raw_ref[:, 3 * HD :].astype(bf16)
            for half in range(2):
                rows = slice(half * group_rows, (half + 1) * group_rows)
                kv_ref[half, :, :HD] = turned[rows]
                kv_ref[half, :, HD:] = values[rows]


def prepare(raw, squares, tables, gain):
    return pl.pallas_call(
        prepare_kernel,
        name="prepare",
        out_shape=(
            jax.ShapeDtypeStruct((2, group_rows, 2 * HD), bf16),
            jax.ShapeDtypeStruct((2, group_rows, 2 * HD), bf16),
        ),
        in_specs=[vmem] * 5,
        out_specs=[vmem] * 2,
        compiler_params=pltpu.CompilerParams(vmem_limit_bytes=32 << 20),
        cost_estimate=pl.CostEstimate(flops=8 << 20, bytes_accessed=6 << 20, transcendentals=0),
    )(raw, squares, *tables, gain)


def turned_back(raw_ref, squares_ref, cos_ref, sin_ref, dq_ref, dkv_ref):
    query_inverse, key_inverse = inverses(squares_ref)
    cosine, sine = cos_ref[...], -sin_ref[...]
    for head in range(3):
        lanes = slice(head * HD, (head + 1) * HD)
        inverse = query_inverse if head < 2 else key_inverse
        grad = dq_ref[:, lanes] if head < 2 else dkv_ref[:, :HD]
        yield head, lanes, turn(grad, cosine, sine), raw_ref[:, lanes] * inverse, inverse


def means_kernel(raw_ref, squares_ref, cos_ref, sin_ref, gain_ref, dq_ref, dkv_ref, means_ref):
    products = []
    for _, lanes, upstream, normed, _ in turned_back(
        raw_ref, squares_ref, cos_ref, sin_ref, dq_ref, dkv_ref
    ):
        products.append(upstream * gain_ref[:, lanes] * normed)
    query = jnp.sum(products[0] + products[1], axis=1, keepdims=True)
    key = jnp.sum(products[2], axis=1, keepdims=True)
    means_ref[...] = jnp.concatenate([as_lanes(query), as_lanes(key)])


def raw_grad_kernel(
    info_ref, squares_ref, gain_ref, dkv_ref, means_ref, norm_gains_ref,
    raw_hbm, cos_hbm, sin_hbm, dq_hbm, weight_hbm, left_hbm, right_hbm,
    gains_ref, *refs,
):
    outs, held, (raw_ref, cos_ref, sin_ref, dq_ref, weight_ref, tokens_ref, low_ref, sems) = (
        refs[:6],
        refs[6:12],
        refs[12:],
    )
    loads = [
        pltpu.make_async_copy(source, target, sems.at[number])
        for number, (source, target) in enumerate(
            (
                (raw_hbm, raw_ref),
                (cos_hbm, cos_ref),
                (sin_hbm, sin_ref),
                (dq_hbm, dq_ref),
                (weight_hbm, weight_ref),
            )
        )
    ]
    loads += token_loads(left_hbm, right_hbm, tokens_ref, sems.at[pl.ds(12, 3)])
    for load in loads:
        load.start()
    stores = [
        pltpu.make_async_copy(source, target, sems.at[6 + number])
        for number, (source, target) in enumerate(zip(held, outs))
    ]
    heads_sent_ref, heads_kept_ref = held[:2]
    left_sent_ref, left_kept_ref, right_sent_ref, right_kept_ref = held[2:]
    for load in loads[:4]:
        load.wait()
    co, x_high, zl = info_ref[0], info_ref[1], info_ref[2]
    means = (as_rows(means_ref[0:1]) / HQ, as_rows(means_ref[1:2]) / HK)

    def place(lanes, low):
        for owner in range(8):
            for half in range(2):
                start = half * group_rows + owner * half_blk
                low_ref[owner, half * half_blk : (half + 1) * half_blk, lanes] = low[
                    start : start + half_blk
                ]

    gains_ref[...] = jnp.zeros((8, 4 * HD), f32)
    for head, lanes, upstream, normed, inverse in turned_back(
        raw_ref, squares_ref, cos_ref, sin_ref, dq_ref, dkv_ref
    ):
        mean = means[0] if head < 2 else means[1]
        place(lanes, (inverse * (upstream * gain_ref[:, lanes] - normed * mean)).astype(bf16))
        gains_ref[0:1, lanes] = jnp.sum(upstream * normed, axis=0, keepdims=True)
    place(slice(3 * HD, 4 * HD), dkv_ref[:, HD:].astype(bf16))
    for row in range(4):
        part = slice((row % 2) * 4 * HD, (row % 2 + 1) * 4 * HD)
        gains_ref[1 + row : 2 + row] = norm_gains_ref[row // 2 : row // 2 + 1, part]
    gains = gains_ref[...]
    high = gains.astype(bf16)
    heads_sent_ref[512:] = jnp.concatenate([high, (gains - high.astype(f32)).astype(bf16)])

    for load in loads[4:]:
        load.wait()
    low = low_ref[...].reshape(ROWS, 4 * HD)
    for part in range(2):
        rows = slice(part * 256, (part + 1) * 256)
        for ref, side in ((heads_sent_ref, 1 - co), (heads_kept_ref, co)):
            lanes = pl.ds(pl.multiple_of(part * 512 + side * 256, 256), 256)
            tokens = tokens_ref[:, :, :, lanes].reshape(ROWS, 256)
            ref[rows] = dot_first(tokens, low).astype(ref.dtype)
    stores[0].start()
    stores[1].start()

    for number in range(4):
        for ref, side in ((left_sent_ref, 1 - x_high), (left_kept_ref, x_high)):
            rows = low_ref[side * 4 + number]
            ref[number] = dot_second(rows, weight_ref[: D // 2]).astype(bf16)
        for ref, side in ((right_sent_ref, 1 - zl), (right_kept_ref, zl)):
            rows = low_ref[2 * number + side]
            ref[number] = dot_second(rows, weight_ref[D // 2 :]).astype(bf16)
    for store in stores[2:]:
        store.start()
    for store in stores:
        store.wait()


def projection_means(*operands):
    return pl.pallas_call(
        means_kernel,
        name="projection_means",
        out_shape=jax.ShapeDtypeStruct((2, ROWS), f32),
        in_specs=[vmem] * 7,
        out_specs=vmem,
        compiler_params=pltpu.CompilerParams(vmem_limit_bytes=32 << 20),
        cost_estimate=pl.CostEstimate(flops=8 << 20, bytes_accessed=6 << 20, transcendentals=0),
    )(*operands)


def projection_grads(
    info, raw, squares, cosine, sine, gain, dq, dkv, means, left, right, weight, norm_gains
):
    shapes = [((512 + 16, 4 * HD), bf16), ((512, 4 * HD), f32)] + [((4, BLK, D // 2), bf16)] * 4
    large = (raw, cosine, sine, dq, weight)
    return pl.pallas_call(
        raw_grad_kernel,
        name="projection_grads",
        out_shape=[jax.ShapeDtypeStruct((8, 4 * HD), f32)]
        + [pltpu.HBM(shape, dtype) for shape, dtype in shapes],
        in_specs=[smem] + [vmem] * 5 + [hbm] * 7,
        out_specs=[vmem] + [hbm] * 6,
        scratch_shapes=[pltpu.VMEM(shape, dtype) for shape, dtype in shapes]
        + [pltpu.VMEM(array.shape, array.dtype) for array in large]
        + [
            pltpu.VMEM((4, 2, BLK, D), bf16),
            pltpu.VMEM((8, BLK, 4 * HD), bf16),
            pltpu.SemaphoreType.DMA((15,)),
        ],
        compiler_params=pltpu.CompilerParams(vmem_limit_bytes=40 << 20),
        cost_estimate=pl.CostEstimate(flops=4 << 30, bytes_accessed=16 << 20, transcendentals=0),
    )(info, squares, gain, dkv, means, norm_gains, *in_hbm(*large, left, right))


INNER_AT = 0
DOWN_LOW_AT = INNER_AT + FF // 2
ATT_AT = DOWN_LOW_AT + D
HIDDEN_AT = ATT_AT + HQ // 2
GATE_LOW_AT = HIDDEN_AT + D
UP_LOW_AT = GATE_LOW_AT + FF // 2
MIXED_LOW_AT = UP_LOW_AT + FF // 2
PACK = MIXED_LOW_AT + D


def rows_kernel(
    info_ref, att_ref, tokens_ref, cot_ref, attn_gain_ref, ffn_gain_ref,
    out_own, gate_own, up_own, down_own, mine, other,
    output_ref, own_hbm, sent_hbm, att_grad_ref, hidden_grad_ref, gain_grad_ref,
    own_ref, sent_ref, out_v, gate_v, up_v, down_v, gate_act, up_act, inner_ref, up_low_ref, hidden_ref, sems,
):
    zh, co = info_ref[0], info_ref[1]
    numbers = iter(range(22))

    def copy(source, target):
        return pltpu.make_async_copy(source, target, sems.at[next(numbers)])

    def pieces(own, rows_at, rows, scratch, blocks):
        copies = [copy(own, scratch.at[pl.ds(zh * 32, 32)])]
        for half, core in ((mine, co), (other, 1 - co)):
            at = (1 - zh) * 32 + core * 16
            for block in range(blocks):
                target = scratch.at[pl.ds(at, 16)]
                if blocks > 1:
                    target = scratch.at[pl.ds(at, 16), :, pl.ds(block * D, D)]
                copies.append(
                    copy(half.at[:, pl.ds(rows_at + block * rows, rows), :], target)
                )
        return copies

    out_copies = pieces(out_own, 0, OUT_ROWS, out_v, 1)
    gate_copies = pieces(gate_own, GATE_AT, GATE_ROWS, gate_v, BLOCKS)
    up_copies = pieces(up_own, UP_AT, GATE_ROWS, up_v, BLOCKS)
    down_copies = pieces(down_own, DOWN_AT, DOWN_ROWS, down_v, 1)
    for item in out_copies:
        item.start()

    def put(core, lanes, value):
        @pl.when(core == co)
        def _():
            own_ref[:, lanes] = value

        @pl.when(core != co)
        def _():
            sent_ref[:, lanes] = value

    def put_both(start, value):
        own_ref[:, start : start + D] = value
        sent_ref[:, start : start + D] = value

    for head in range(8):
        rows = att_ref[head].reshape(BLK, 2 * HD)
        inner_ref[:, head * 2 * HD : (head + 1) * 2 * HD] = rows
        start = ATT_AT + ((head // 4) * 2 + head % 2) * 2 * HD
        put((head // 2) % 2, slice(start, start + 2 * HD), rows)
    for item in out_copies:
        item.wait()
    for item in gate_copies + up_copies:
        item.start()
    attn_gain = attn_gain_ref[...]
    mixed = dot_plain(inner_ref[:, :HQ], out_v[...].reshape(HQ, D))
    hidden_grad_ref[...] = mixed
    attn_inverse = lax.rsqrt(jnp.mean(mixed * mixed, axis=-1, keepdims=True) + epsilon)
    hidden = tokens_ref[...].astype(f32) + mixed * attn_inverse * attn_gain
    hidden_ref[...] = hidden
    put_both(HIDDEN_AT, hidden.astype(bf16))
    for item in gate_copies + up_copies:
        item.wait()
    for item in down_copies:
        item.start()
    tile = 8 * DOWN_ROWS

    def act_body(step, carry):
        lanes = pl.ds(step * tile, tile)
        low = own_ref[:, HIDDEN_AT : HIDDEN_AT + D]
        gate = dot_plain(low, gate_v[:, :, lanes].reshape(D, tile))
        up = dot_plain(low, up_v[:, :, lanes].reshape(D, tile))
        gate_act[:, lanes] = gate
        up_act[:, lanes] = up
        inner = (gate * (1.0 / (1.0 + jnp.exp(-gate))) * up).astype(bf16)
        inner_ref[:, lanes] = inner
        column = (step // 4) * 2 + step % 2
        put((step // 2) % 2, pl.ds(pl.multiple_of(INNER_AT + column * tile, HD), tile), inner)
        return carry

    lax.fori_loop(0, FF // tile, act_body, 0)
    for item in down_copies:
        item.wait()
    ffn_gain = ffn_gain_ref[...]
    down = dot_plain(inner_ref[...], down_v[...].reshape(FF, D))
    ffn_inverse = lax.rsqrt(jnp.mean(down * down, axis=-1, keepdims=True) + epsilon)
    normed = down * ffn_inverse
    output_ref[...] = (hidden_ref[...] + normed * ffn_gain).astype(bf16)
    upstream = cot_ref[...].astype(f32)
    scaled = upstream * ffn_gain
    gain_grad_ref[1:2, :] = jnp.sum(upstream * normed, axis=0, keepdims=True)
    down_low = ffn_inverse * (scaled - normed * jnp.mean(scaled * normed, axis=-1, keepdims=True))
    put_both(DOWN_LOW_AT, down_low.astype(bf16))
    def back_body(step, carry):
        lanes = pl.ds(step * tile, tile)
        rows = down_v[pl.ds(step * 8, 8)].reshape(tile, D)
        inner_grad = dot_second(own_ref[:, DOWN_LOW_AT : DOWN_LOW_AT + D], rows)
        gate, up = gate_act[:, lanes], up_act[:, lanes]
        sigmoid = 1.0 / (1.0 + jnp.exp(-gate))
        gate_low = (inner_grad * up * sigmoid * (1.0 + gate * (1.0 - sigmoid))).astype(bf16)
        up_low = (inner_grad * (gate * sigmoid)).astype(bf16)
        column = (step % 4) * tile
        put(step // 4, pl.ds(pl.multiple_of(GATE_LOW_AT + column, HD), tile), gate_low)
        put(step // 4, pl.ds(pl.multiple_of(UP_LOW_AT + column, HD), tile), up_low)
        inner_ref[:, lanes] = gate_low
        up_low_ref[:, lanes] = up_low
        return carry

    lax.fori_loop(0, FF // tile, back_body, 0)
    mixed = hidden_grad_ref[...]
    attn_inverse = lax.rsqrt(jnp.mean(mixed * mixed, axis=-1, keepdims=True) + epsilon)
    normed = mixed * attn_inverse
    hidden_grad = (
        cot_ref[...].astype(f32)
        + dot_second(inner_ref[...], gate_v[...].reshape(D, FF))
        + dot_second(up_low_ref[...], up_v[...].reshape(D, FF))
    )
    scaled = hidden_grad * attn_gain_ref[...]
    gain_grad_ref[0:1, :] = jnp.sum(hidden_grad * normed, axis=0, keepdims=True)
    mixed_low = (
        attn_inverse * (scaled - normed * jnp.mean(scaled * normed, axis=-1, keepdims=True))
    ).astype(bf16)
    put_both(MIXED_LOW_AT, mixed_low)
    packs = [copy(sent_ref, sent_hbm), copy(own_ref, own_hbm)]
    for item in packs:
        item.start()
    hidden_grad_ref[...] = hidden_grad

    def grad_body(head, carry):
        rows = out_v[pl.ds(head * 8, 8)].reshape(2 * HD, D)
        mixed_low = own_ref[:, MIXED_LOW_AT : MIXED_LOW_AT + D]
        grad = dot_second(mixed_low, rows).astype(bf16)
        att_grad_ref[head] = grad.reshape(2, half_blk, 2 * HD)
        return carry

    lax.fori_loop(0, 8, grad_body, 0)
    for item in packs:
        item.wait()


def own_rows(info, attended, tokens, cotangent, attn_gain, ffn_gain, shards, mine, other):
    def shape(*dims, dtype=bf16):
        return jax.ShapeDtypeStruct(dims, dtype)

    return pl.pallas_call(
        rows_kernel,
        name="own_rows",
        out_shape=(
            shape(BLK, D),
            pltpu.HBM((BLK, PACK), bf16),
            pltpu.HBM((BLK, PACK), bf16),
            shape(8, 2, half_blk, 2 * HD),
            shape(BLK, D, dtype=f32),
            shape(2, D, dtype=f32),
        ),
        in_specs=[smem] + [vmem] * 5 + [hbm] * 6,
        out_specs=[vmem, hbm, hbm, vmem, vmem, vmem],
        scratch_shapes=[
            pltpu.VMEM((BLK, PACK), bf16),
            pltpu.VMEM((BLK, PACK), bf16),
            pltpu.VMEM((64, OUT_ROWS, D), bf16),
            pltpu.VMEM((64, GATE_ROWS, FF), bf16),
            pltpu.VMEM((64, GATE_ROWS, FF), bf16),
            pltpu.VMEM((64, DOWN_ROWS, D), bf16),
            pltpu.VMEM((BLK, FF), f32),
            pltpu.VMEM((BLK, FF), f32),
            pltpu.VMEM((BLK, FF), bf16),
            pltpu.VMEM((BLK, FF), bf16),
            pltpu.VMEM((BLK, D), f32),
            pltpu.SemaphoreType.DMA((22,)),
        ],
        compiler_params=pltpu.CompilerParams(vmem_limit_bytes=44 << 20),
        cost_estimate=pl.CostEstimate(
            flops=4 * BLK * (3 * D * FF + HQ * D),
            bytes_accessed=26 << 20,
            transcendentals=2 * BLK * FF,
        ),
    )(info, attended, tokens, cotangent, attn_gain, ffn_gain, *in_hbm(*shards, mine, other))


def wide_rows(array):
    return jnp.concatenate(
        [array[:, start : start + D] for start in range(0, array.shape[1], D)]
    )


def ring_place(bits):
    return bits[0] * 2 + (bits[0] ^ bits[1])


PRODUCTS = (
    (FF // 2, INNER_AT, D, DOWN_LOW_AT, "zB", "zA"),
    (D, HIDDEN_AT, FF // 2, GATE_LOW_AT, "x0", "x1"),
    (D, HIDDEN_AT, FF // 2, UP_LOW_AT, "x1", "x0"),
    (HQ // 2, ATT_AT, D, MIXED_LOW_AT, "zA", "zB"),
)


def product_places():
    places = []
    for *_, first_link, second_link in PRODUCTS:
        for first, second in ((1, 0), (1, 1), (0, 0), (0, 1)):
            bits = {
                first_link: link_bit(first_link) ^ first,
                second_link: link_bit(second_link) ^ second,
            }
            for part in range(2):
                if "zA" in bits:
                    places.append((bits["zB"] * 2 + bits["zA"]) * 2 + part)
                else:
                    places.append(part * 4 + ring_place((bits["x1"], bits["x0"])))
    return jnp.stack(places).astype(jnp.int32)


def products_kernel(places_ref, own_ref, got_ref, *refs):
    outs, (both, sems), lefts, scratch = refs[:8], refs[8:10], refs[10:13], refs[13:]
    lefts = dict(zip((INNER_AT, HIDDEN_AT, ATT_AT), lefts))
    run_copies(
        [
            pltpu.make_async_copy(ref, both.at[pl.ds(core * BLK, BLK)], sems.at[8 + core])
            for core, ref in enumerate((own_ref, got_ref))
        ]
    )
    copies = [
        pltpu.make_async_copy(held, out, sems.at[number])
        for number, (held, out) in enumerate(zip(scratch, outs))
    ]
    for left_at, left in lefts.items():
        columns = slice(left_at, left_at + left.shape[0])
        left[...] = both[:, columns].astype(f32).T.astype(bf16)
    for number, (rows, left_at, width, right_at, *_) in enumerate(PRODUCTS):
        left = lefts[left_at]
        eighth = rows // 8
        for part in range(2):
            out = scratch[2 * number + part]

            starts = [
                pl.multiple_of(places_ref[number * 8 + part * 4 + step] * eighth, eighth)
                for step in range(4)
            ]
            picked = jnp.concatenate([left[pl.ds(start, eighth)] for start in starts])
            out[...] = dot_plain(picked, both[:, right_at : right_at + width]).astype(bf16)
            copies[2 * number + part].start()
    for copy in copies:
        copy.wait()


def weight_products(own, got):
    flops = sum(2 * 2 * BLK * rows * width for rows, _, width, *_ in PRODUCTS)
    return pl.pallas_call(
        products_kernel,
        name="weight_products",
        out_shape=[
            pltpu.HBM((rows // 2, width), bf16)
            for rows, _, width, *_ in PRODUCTS
            for _ in range(2)
        ],
        in_specs=[smem, hbm, hbm],
        out_specs=[hbm] * 8,
        scratch_shapes=[
            pltpu.VMEM((2 * BLK, PACK), bf16),
            pltpu.SemaphoreType.DMA((10,)),
            pltpu.VMEM((FF // 2, 2 * BLK), bf16),
            pltpu.VMEM((D, 2 * BLK), bf16),
            pltpu.VMEM((HQ // 2, 2 * BLK), bf16),
        ]
        + [
            pltpu.VMEM((rows // 2, width), bf16)
            for rows, _, width, *_ in PRODUCTS
            for _ in range(2)
        ],
        compiler_params=pltpu.CompilerParams(vmem_limit_bytes=40 << 20),
        cost_estimate=pl.CostEstimate(flops=flops, bytes_accessed=16 << 20, transcendentals=0),
    )(product_places(), *in_hbm(own, got))


def place_kernel(core_ref, chunk_ref, *refs):
    gate_ref, up_ref, down_ref, out_ref = refs[-4:]
    for y in range(4):
        for part in range(2):
            chunk = chunk_ref[y, 0, part]
            start = (2 * y + part) * GATE_ROWS
            rows = slice(start, start + GATE_ROWS)
            gate_ref[rows, :D] = chunk[:16].astype(f32)
            gate_ref[rows, D:] = chunk[16:32, : D // 2].astype(f32)
            up_ref[rows, : D // 2] = chunk[16:32, D // 2 :].astype(f32)
            up_ref[rows, D // 2 :] = chunk[32:48].astype(f32)
            down_ref[part, y] = chunk[48:72].astype(f32)
            out_ref[part, y] = chunk[72:].astype(f32)


def place_rows(core, chunks, earlier):
    def columns(x, core):
        return (x, core[0])

    def rows(x, core):
        return (core[0], 0, x, 0)

    return pl.pallas_call(
        place_kernel,
        name="place_rows",
        out_shape=(
            jax.ShapeDtypeStruct((D // 2, FF), f32),
            jax.ShapeDtypeStruct((D // 2, FF), f32),
            jax.ShapeDtypeStruct((4, 4, 4 * 24, D), f32),
            jax.ShapeDtypeStruct((4, 4, 4 * 16, D), f32),
        ),
        grid_spec=pltpu.PrefetchScalarGridSpec(
            num_scalar_prefetch=1,
            grid=(4,),
            in_specs=[pl.BlockSpec((4, 1, 2, 88, D), lambda x, core: (0, x, 0, 0, 0))]
            + [hbm] * len(earlier),
            out_specs=[
                pl.BlockSpec((D // 8, FF // 2), columns),
                pl.BlockSpec((D // 8, FF // 2), columns),
                pl.BlockSpec((2, 4, 24, D), rows),
                pl.BlockSpec((2, 4, 16, D), rows),
            ],
        ),
        input_output_aliases={2 + number: number for number in range(len(earlier))},
        compiler_params=pltpu.CompilerParams(vmem_limit_bytes=32 << 20),
        cost_estimate=pl.CostEstimate(flops=3 << 20, bytes_accessed=18 << 20, transcendentals=0),
    )(core, *in_hbm(chunks), *earlier)


def place_heads_kernel(core_ref, query_chunk_ref, rest_chunk_ref, *refs):
    query_ref, key_ref, value_ref = refs[-3:]
    for owner in range(8):
        query = query_chunk_ref[owner // 2, 0, owner % 2, :64].astype(f32)
        rest = rest_chunk_ref[0, owner // 2, owner % 2, :64].astype(f32)
        query_ref[:, owner * 2 * HD : (owner + 1) * 2 * HD] = query
        key_ref[:, owner * HD : (owner + 1) * HD] = rest[:, :HD]
        value_ref[:, owner * HD : (owner + 1) * HD] = rest[:, HD:]


def place_heads(core, query, rest, earlier):
    def rows(y, core):
        return (core[0] * 4 + y, 0)

    return pl.pallas_call(
        place_heads_kernel,
        name="place_heads",
        out_shape=(
            jax.ShapeDtypeStruct((D // 2, HQ), f32),
            jax.ShapeDtypeStruct((D // 2, HK), f32),
            jax.ShapeDtypeStruct((D // 2, HK), f32),
        ),
        grid_spec=pltpu.PrefetchScalarGridSpec(
            num_scalar_prefetch=1,
            grid=(4,),
            in_specs=[
                pl.BlockSpec((4, 1, 2, 80, 2 * HD), lambda y, core: (0, y, 0, 0, 0)),
                pl.BlockSpec((1, 4, 2, 80, 2 * HD), lambda y, core: (y, 0, 0, 0, 0)),
            ]
            + [hbm] * len(earlier),
            out_specs=[
                pl.BlockSpec((64, HQ), rows),
                pl.BlockSpec((64, HK), rows),
                pl.BlockSpec((64, HK), rows),
            ],
        ),
        input_output_aliases={3 + number: number for number in range(len(earlier))},
        compiler_params=pltpu.CompilerParams(vmem_limit_bytes=32 << 20),
        cost_estimate=pl.CostEstimate(flops=1 << 20, bytes_accessed=6 << 20, transcendentals=0),
    )(core, *in_hbm(query, rest), *earlier)


def per_device(
    tokens,
    doc_lengths,
    query_weight,
    key_weight,
    value_weight,
    out_weight,
    gate_weight,
    up_weight,
    down_weight,
    query_gain,
    key_gain,
    attn_gain,
    ffn_gain,
    cotangent,
):
    y, x, zl, co, zh = (lax.axis_index(name) for name in ("y", "x", "zl", "co", "zh"))
    head = x * 2 + zl
    lengths = doc_lengths[0]
    first_end = lengths[0]
    second_end = lengths[0] + lengths[1]
    info = jnp.stack([y, co, first_end, second_end]).astype(jnp.int32)
    source = tokens[0]

    gains = jnp.concatenate([query_gain, key_gain, attn_gain, ffn_gain])
    shards = (
        out_weight.reshape(32, OUT_ROWS, D),
        gate_weight.reshape(32, GATE_ROWS, FF),
        up_weight.reshape(32, GATE_ROWS, FF),
        down_weight.reshape(32, DOWN_ROWS, D),
    )
    places = jnp.stack([co * 16 + y * 4 + x, head, x * 2 + 1 - zl]).astype(jnp.int32)
    own_slice, sent_slice, weight_chunk = collect(
        places,
        (query_weight, key_weight, value_weight),
        shards,
        gains,
    )
    got_slice = across(sent_slice, "zB")
    weight_chunk = across(weight_chunk, "zB")
    left_tokens, right_tokens = source[None, :, : D // 2], source[None, :, D // 2 :]
    for left_link, right_link in (("x0", "zl"), ("x1", "x0"), ("zl", "x1")):
        left_tokens = double(left_tokens, left_link)
        right_tokens = double(right_tokens, right_link)
    left_tokens = left_tokens.reshape(2, 4, BLK, D // 2)
    right_tokens = right_tokens.reshape(4, 2, BLK, D // 2)
    mine_weights = lax.all_gather(weight_chunk[:CHUNK_ROWS], ("y", "x"), axis=0, tiled=False)
    other_gains = weight_chunk[CHUNK_ROWS:].reshape(-1)[: gains.shape[0]]

    def whole_gain(start, size):
        own = gains[start : start + size]
        got = other_gains[start : start + size]
        return jnp.where(zh == 0, jnp.concatenate([own, got]), jnp.concatenate([got, own]))

    query_scale = lax.dynamic_slice_in_dim(whole_gain(0, 1024), head * 2 * HD, 2 * HD).astype(f32)
    key_scale = lax.dynamic_slice_in_dim(whole_gain(1024, 512), head * HD, HD).astype(f32)
    attn_scale = whole_gain(1536, 512)
    ffn_scale = whole_gain(2048, 512)

    head_gain = jnp.concatenate([query_scale, key_scale])[None]

    index = jnp.arange(group_rows, dtype=jnp.int32)
    positions = jnp.concatenate(
        [half_positions(index, y, co, 0), half_positions(index, y, co, 1)]
    )
    doc_start = jnp.where(
        positions >= second_end, second_end, jnp.where(positions >= first_end, first_end, 0)
    )
    frequency = jnp.power(
        f32(rope_base), -jnp.arange(HD // 2, dtype=f32) * (2.0 / HD)
    )
    angles = (positions - doc_start).astype(f32)[:, None] * frequency[None, :]
    cosine, sine_table = jnp.cos(angles), jnp.sin(angles)
    tables = (
        jnp.concatenate([cosine, cosine], axis=1),
        jnp.concatenate([-sine_table, sine_table], axis=1),
    )

    raw, head_weight, squares = project(
        zh[None].astype(jnp.int32), left_tokens, right_tokens, own_slice, got_slice
    )
    squares = exchange(squares, HEAD_AXES)
    queries, kv = prepare(raw, squares, tables, head_gain)
    pairs = [
        jnp.stack([kv[half], across(kv[half], first)]) for half, first in enumerate(("y0", "y1"))
    ]
    pieces = [
        piece
        for pair, second in zip(pairs, ("y1", "y0"))
        for piece in (pair, across(pair, second))
    ]
    pieces += [across(piece, "co") for piece in pieces]
    pieces, mine_weights = lax.optimization_barrier((pieces, mine_weights))
    other_weights = across(mine_weights, "co")

    attended_low, attended_full, log_total = attention_forward(info, queries, pieces)
    attended_low = exchange(attended_low, HEAD_AXES)
    (
        output,
        own_pack,
        sent_pack,
        attended_grad,
        hidden_grad,
        norm_gain_grads,
    ) = own_rows(
        jnp.stack([zh, co]).astype(jnp.int32),
        attended_low,
        source,
        cotangent[0],
        attn_scale.astype(f32)[None],
        ffn_scale.astype(f32)[None],
        shards,
        mine_weights,
        other_weights,
    )

    grads = exchange(attended_grad, HEAD_AXES)

    products = weight_products(own_pack, across(sent_pack, "co"))
    sent_parts, rest_parts = products[0::2], products[1::2]
    grads, sent_parts = lax.optimization_barrier((grads, sent_parts))
    got_parts = [
        across(sent, first_link)
        for sent, (*_, first_link, _) in zip(sent_parts, PRODUCTS)
    ]

    query_grad, sent, kept = attention_backward(
        info, queries, pieces, grads, attended_full, log_total
    )
    stage = lax.optimization_barrier
    own_core, other_core = co[None].astype(jnp.int32), (1 - co)[None].astype(jnp.int32)

    sent, got_parts = stage((sent, got_parts))
    got = across(sent, "co")
    second_sent = [
        (rest[rest.shape[0] // 2 :].astype(f32) + part[rest.shape[0] // 2 :].astype(f32)).astype(
            bf16
        )
        for rest, part in zip(rest_parts, got_parts)
    ]
    got, second_sent = stage((got, second_sent))
    orders = (("y1", "y0"), ("y0", "y1"))
    kv_got = [
        across((kept[half, 2:].astype(f32) + got[half, 2:].astype(f32)).astype(bf16), first)
        for half, (first, _) in enumerate(orders)
    ]
    second_got = [
        across(part, second_link) for part, (*_, second_link) in zip(second_sent, PRODUCTS)
    ]

    def second_sum(number, arrived):
        rest, part = rest_parts[number], got_parts[number]
        middle = rest.shape[0] // 2
        kept_part = rest[:middle].astype(f32) + part[:middle].astype(f32)
        return (kept_part + arrived.astype(f32)).astype(bf16)

    kv_got = stage(kv_got)
    kv_both = [
        kept[half, :2].astype(f32) + got[half, :2].astype(f32) + kv_got[half].astype(f32)
        for half in range(2)
    ]
    kv_got = [
        across(kv_both[half][1].astype(bf16), second) for half, (_, second) in enumerate(orders)
    ]
    kv_grad = jnp.concatenate(
        [both[0] + more.astype(f32) for both, more in zip(kv_both, kv_got)]
    )
    operands = (
        raw, squares, *tables, head_gain, query_grad.reshape(ROWS, 2 * HD), kv_grad,
    )
    means = projection_means(*operands)
    second_got, _ = stage((second_got, means))
    down_got, gate_got, up_got, out_got = second_got
    act_part = exchange(
        jnp.concatenate([second_sum(1, gate_got), second_sum(2, up_got)], axis=1).reshape(
            16, 16, FF
        ),
        ("zh", "y", "zl"),
    )
    for link in ("x0", "x1", "zA"):
        means = means + across(means, link)
    means, act_part, down_got, out_got = stage((means, act_part, down_got, out_got))
    rest_part = exchange(
        jnp.concatenate(
            [second_sum(0, down_got).reshape(16, 24, D), second_sum(3, out_got).reshape(16, 16, D)],
            axis=1,
        ),
        ("y", "x"),
    )

    x_high, x_low = x // 2, x % 2
    gain_sums, heads_sent, heads_kept, left_sent, left, right_sent, right = projection_grads(
        jnp.stack([co, x_high, zl]).astype(jnp.int32),
        *operands,
        means,
        left_tokens,
        right_tokens,
        head_weight,
        norm_gain_grads,
    )

    def pick(array, number):
        return lax.dynamic_index_in_dim(array, number, 0, keepdims=False)

    def pass_on(both, link, number):
        return pick(both, number).astype(f32), across(pick(both, 1 - number), link)

    def halves(both):
        return both.astype(bf16).reshape(2, both.shape[0] // 2, *both.shape[1:])

    def take_gains(got, kept, sums):
        more = got[-16:].astype(f32)
        return (kept + got[:-16].astype(f32)).astype(bf16), sums + more[:8] + more[8:]

    def with_gains(array, sums):
        return jnp.concatenate([array, high_low(sums).reshape(16, 4 * HD)])

    def halve_heads(chunk, sums, link):
        bit = link_bit(link)
        chunk = chunk.reshape(2, chunk.shape[0] // 2, 4 * HD)
        kept = pick(chunk, bit).astype(f32)
        return kept, across(with_gains(pick(chunk, 1 - bit), sums), link)

    heads_got = across(heads_sent, "co")
    left_got = across(left_sent, "x1")
    right_got = across(right_sent, "zA")
    rest_part, heads_got = stage((rest_part, heads_got))
    chunk = jnp.concatenate(
        [
            wide_rows(jnp.sum(act_part.astype(f32), axis=0).astype(bf16)),
            jnp.sum(rest_part.astype(f32), axis=0).astype(bf16),
        ]
    )
    chunk_got = across(chunk, "zA")
    def beside(start, stop, bit):
        mine, other = chunk[start:stop], chunk_got[start:stop]
        return jnp.where(bit == 0, jnp.stack([mine, other]), jnp.stack([other, mine]))

    chunks = lax.all_gather(
        jnp.concatenate([beside(0, 48, zl), beside(48, 88, link_bit("zA"))], axis=1),
        ("y", "x"),
        axis=0,
        tiled=False,
    ).reshape(4, 4, 2, 88, D)
    heads, gain_sums = take_gains(heads_got, heads_kept, gain_sums)
    heads = jnp.concatenate(
        [
            heads.reshape(8, 64, 4 * HD),
            jnp.broadcast_to(high_low(gain_sums).reshape(1, 16, 4 * HD), (8, 16, 4 * HD)),
        ],
        axis=1,
    )
    heads = exchange(heads, ("zh", "y"))
    left, left_got = pass_on(halves(left.astype(f32) + left_got.astype(f32)), "x0", x_low)
    right, right_got = pass_on(halves(right.astype(f32) + right_got.astype(f32)), "x1", x_high)
    heads, left_got, right_got = stage((heads, left_got, right_got))
    heads = jnp.sum(heads.astype(f32), axis=0)
    gain_sums = heads[64:72] + heads[72:]
    heads = jnp.concatenate([heads[:64].astype(bf16), high_low(gain_sums).reshape(16, 4 * HD)])
    heads = double(heads[None], "zl")
    head_query, head_rest = heads[:, :, : 2 * HD], heads[:, :, 2 * HD :]
    for query_link, rest_link in (("y0", "x0"), ("y1", "x1"), ("x0", "y0"), ("x1", "y1")):
        head_query, head_rest = double(head_query, query_link), double(head_rest, rest_link)
    head_query = head_query.reshape(4, 4, 2, 80, 2 * HD)
    head_rest = head_rest.reshape(4, 4, 2, 80, 2 * HD)
    left, left_got = pass_on(halves(left + left_got.astype(f32)), "zA", zl)
    right, right_got = pass_on(halves(right + right_got.astype(f32)), "x0", x_low)
    tokens_grad = hidden_grad + jnp.concatenate(
        [
            (left + left_got.astype(f32)).reshape(BLK, D // 2),
            (right + right_got.astype(f32)).reshape(BLK, D // 2),
        ],
        axis=1,
    )
    head_query, head_rest, tokens_grad, chunks = stage(
        (head_query, head_rest, tokens_grad, chunks)
    )
    other_chunks = across(chunks, "co")
    other_heads = across(head_query, "co"), across(head_rest, "co")
    placed = place_rows(own_core, chunks, ())
    placed_heads = place_heads(own_core, head_query, head_rest, ())
    gate_weight_grad, up_weight_grad, down_weight_grad, out_weight_grad = place_rows(
        other_core, other_chunks, placed
    )
    query_weight_grad, key_weight_grad, value_weight_grad = place_heads(
        other_core, *other_heads, placed_heads
    )
    down_weight_grad = down_weight_grad.reshape(FF // 2, D)
    out_weight_grad = out_weight_grad.reshape(HQ // 2, D)
    def gain_of(rows):
        return rows[..., 64, :].astype(f32) + rows[..., 72, :].astype(f32)

    query_gain_grad = gain_of(head_query[:, 0]).reshape(HQ)
    key_gain_grad = gain_of(head_rest[0])[..., :HD].reshape(HK)

    def norm_gains(rows):
        return jnp.sum(
            rows[:, :, 65:69].astype(f32) + rows[:, :, 73:77].astype(f32), axis=(0, 1)
        )

    norm_gain_grads = jnp.concatenate(
        [norm_gains(head_query[:, 0]), norm_gains(head_rest[0])], axis=1
    ).reshape(2, D)

    def own_gain(gain_grad):
        size = gain_grad.shape[0] // 2
        return lax.dynamic_slice_in_dim(gain_grad, zh * size, size)

    return (
        output[None],
        tokens_grad[None],
        query_weight_grad,
        key_weight_grad,
        value_weight_grad,
        out_weight_grad,
        gate_weight_grad,
        up_weight_grad,
        down_weight_grad,
        own_gain(query_gain_grad.reshape(HQ)),
        own_gain(key_gain_grad.reshape(HK)),
        own_gain(norm_gain_grads[0]),
        own_gain(norm_gain_grads[1]),
    )


def solution(mesh):
    fine = Mesh(mesh.devices.reshape(4, 4, 2, 2, 2), ("y", "x", "zl", "co", "zh"))
    rows = P("zh", TOKEN_AXES, None)
    weight = P("zh", None)
    gain = P("zh")
    return jax.shard_map(
        per_device,
        mesh=fine,
        in_specs=(rows, weight) + (weight,) * 7 + (gain,) * 4 + (rows,),
        out_specs=(rows, rows) + (weight,) * 7 + (gain,) * 4,
        check_vma=False,
    )
```

```python
import functools
import math

import jax
import jax.numpy as jnp
from jax import lax
from jax.experimental import pallas as pl
from jax.experimental.pallas import tpu as pltpu
from jax.sharding import Mesh
from jax.sharding import PartitionSpec as P

D = 1024
HEADS = 16
KVH = 8
HD = 128
FF = 3072
BLK = 128
HQ = 2048
HK = 1024
SEQ = 8192

epsilon = 1e-06
rope_base = 1000000.0
masked_score = -1e30
score_scale = HD**-0.5
log2_scale = score_scale * math.log2(math.e)
half_blk = BLK // 2
group_rows = 8 * half_blk

bf16 = jnp.bfloat16
f32 = jnp.float32

TOKEN_AXES = ("y", "x", "zl", "co")
HEAD_AXES = ("x", "zl")

edge_a = [(0, 1), (1, 0), (2, 3), (3, 2)]
edge_b = [(1, 2), (2, 1), (3, 0), (0, 3)]
swap = [(0, 1), (1, 0)]
LINKS = {
    "x0": ("x", edge_a),
    "x1": ("x", edge_b),
    "y0": ("y", edge_a),
    "y1": ("y", edge_b),
    "zA": ("zl", swap),
    "zB": (("zl", "zh"), [(0, 3), (3, 0), (1, 2), (2, 1)]),
    "zl": ("zl", swap),
    "co": ("co", swap),
    "zh": ("zh", swap),
}


def link_bit(link):
    if link in ("x0", "y0"):
        place = lax.axis_index(link[0])
        return ((place == 1) | (place == 2)).astype(jnp.int32)
    if link in ("x1", "y1"):
        return (lax.axis_index(link[0]) >= 2).astype(jnp.int32)
    if link == "zA":
        return lax.axis_index("zl") ^ lax.axis_index("zh")
    if link == "zB":
        return lax.axis_index("zh")
    return lax.axis_index(link)


def across(array, link):
    axis, pairs = LINKS[link]
    return lax.ppermute(array, axis, pairs)


def dot_plain(left_op, right_op):
    return jnp.dot(left_op, right_op, preferred_element_type=f32)


def dot_second(left_op, right_op):
    return lax.dot_general(
        left_op, right_op, (((1,), (1,)), ((), ())), preferred_element_type=f32
    )


def dot_first(left_op, right_op):
    return lax.dot_general(
        left_op, right_op, (((0,), (0,)), ((), ())), preferred_element_type=f32
    )


def exchange(array, axes):
    return lax.all_to_all(array, axes, 0, 0, tiled=True)


def gather_all(array, axes, count):
    return exchange(jnp.broadcast_to(array[None], (count, *array.shape)), axes)


def double(array, link):
    if link == "zA":
        bit = link_bit(link)
    else:
        place = lax.axis_index(LINKS[link][0])
        bit = place // 2 if link in ("x1", "y1") else place % 2
    got = across(array, link)
    return jnp.where(bit == 0, jnp.concatenate([array, got]), jnp.concatenate([got, array]))


def high_low(values):
    high = values.astype(bf16)
    return jnp.stack([high, (values - high.astype(f32)).astype(bf16)])


def half_positions(index, y, co, half):
    block = 16 * y + 2 * (index // half_blk) + co
    inner = index % half_blk
    return jnp.where(half == 0, block * half_blk + inner, SEQ - (block + 1) * half_blk + inner)


def query_masks(info_ref, half):
    y, co, first_end, second_end = info_ref[0], info_ref[1], info_ref[2], info_ref[3]
    index = lax.broadcasted_iota(jnp.int32, (1, group_rows), 1)
    position = half_positions(index, y, co, half)
    start = jnp.where(position >= second_end, second_end, 0)
    start = jnp.where((position >= first_end) & (position < second_end), first_end, start)
    return position, start, position >= second_end


def pair_mask(group, key_half, query_pos, query_start):
    index = lax.broadcasted_iota(jnp.int32, (group_rows, 1), 0)
    key_pos = half_positions(index, group // 2, group % 2, key_half)
    return (key_pos >= query_start) & (key_pos <= query_pos)


def open_steps(y, half):
    count = jnp.where(half == 0, jnp.maximum(2 * y - 2, 0), 6 + 6 - 2 * y)

    def chunk(step):
        late = step >= 6
        group = jnp.where(late, step - 6 + 2 * y + 2, step + 2)
        return group, jnp.where(late, 1, 0)

    return count, chunk


def masked_steps(y, half):
    count = jnp.where((half == 0) & (y == 0), 2, 4)

    def chunk(step):
        own = step >= 2
        group = jnp.where(own, 2 * y + step - 2, step)
        return group, jnp.where(own, half, 0)

    return count, chunk


def slot_of(group, key_half, y, co):
    other_y = group // 2
    beside, over = other_y == (y ^ 1), other_y == 3 - y
    first = jnp.where(key_half == 0, beside, over)
    second = jnp.where(key_half == 0, over, beside)
    ring = jnp.where(other_y == y, 0, jnp.where(first, 1, jnp.where(second, 2, 3)))
    return (group % 2) ^ co, key_half, ring


def load_chunks(pieces, kvs, sems):
    copies = []
    for number, piece in enumerate(pieces):
        core, half, pair = number // 4, number // 2 % 2, number % 2
        target = kvs.at[core, half, pl.ds(2 * pair, 2)]
        copies.append(pltpu.make_async_copy(piece, target, sems.at[number]))
    for copy in copies:
        copy.start()
    return copies


def forward_kernel(info_ref, query_ref, *refs):
    pieces, (low_ref, full_ref, total_ref), (kvs, sems, qt, top, denom, acc) = (
        refs[:8],
        refs[8:11],
        refs[11:],
    )
    y, co = info_ref[0], info_ref[1]
    for copy in load_chunks(pieces, kvs, sems):
        copy.wait()

    def half_body(half, carry):
        query_pos, query_start, last_doc = query_masks(info_ref, half)
        for head in range(2):
            lanes = slice(head * HD, (head + 1) * HD)
            qt[head] = query_ref[half, :, lanes].astype(f32).T.astype(bf16)
            top[head] = jnp.full((1, group_rows), masked_score, f32)
            denom[head] = jnp.zeros((1, group_rows), f32)
            acc[head] = jnp.zeros((HD, group_rows), f32)

        def step(chunks, masked):
            slots = [slot_of(*chunk, y, co) for chunk in chunks]
            keys = [kvs[(*slot, slice(None), slice(0, HD))] for slot in slots]
            values = [kvs[(*slot, slice(None), slice(HD, 2 * HD))] for slot in slots]
            if masked:
                masks = [pair_mask(*chunk, query_pos, query_start) for chunk in chunks]
            for head in range(2):
                scores = [dot_plain(part, qt[head]) for part in keys]
                if masked:
                    scores = [
                        jnp.where(mask, part, masked_score) for mask, part in zip(masks, scores)
                    ]
                old_top = top[head]
                new_top = old_top
                for part in scores:
                    new_top = jnp.maximum(new_top, jnp.max(part, axis=0, keepdims=True))
                weights = [jnp.exp2(part - new_top) for part in scores]
                rescale = jnp.exp2(old_top - new_top)
                total = denom[head] * rescale
                for part in weights:
                    total += jnp.sum(part, axis=0, keepdims=True)
                denom[head] = total
                acc[head] = (
                    acc[head] * rescale
                    + dot_first(values[0], weights[0].astype(bf16))
                    + dot_first(values[1], weights[1].astype(bf16))
                )
                top[head] = new_top

        count, chunk = open_steps(y, half)

        def open_body(number, inner):
            step((chunk(2 * number), chunk(2 * number + 1)), False)
            return inner

        lax.fori_loop(0, count // 2, open_body, 0)
        for head in range(2):
            top[head] = jnp.where(last_doc, masked_score, top[head])
            denom[head] = jnp.where(last_doc, 0.0, denom[head])
            acc[head] = jnp.where(last_doc, 0.0, acc[head])
        masked_count, masked_chunk = masked_steps(y, half)

        def masked_body(number, inner):
            step((masked_chunk(2 * number), masked_chunk(2 * number + 1)), True)
            return inner

        lax.fori_loop(0, masked_count // 2, masked_body, 0)
        for head in range(2):
            lanes = slice(head * HD, (head + 1) * HD)
            attended = acc[head] / denom[head]
            full_ref[half, head] = attended
            total_ref[half, head] = top[head] + jnp.log2(denom[head])
            rows = attended.T.astype(bf16)
            for owner in range(8):
                low_ref[owner, half, :, lanes] = rows[owner * half_blk : (owner + 1) * half_blk]
        return carry

    lax.fori_loop(0, 2, half_body, 0)


def backward_kernel(info_ref, query_ref, grad_ref, full_ref, total_ref, *refs):
    pieces, (dq_ref, sent_hbm, kept_hbm), (kvs, sems, qt, gt, delta, dqt, dkv) = (
        refs[:8],
        refs[8:11],
        refs[11:],
    )
    y, co = info_ref[0], info_ref[1]

    def grads_of(half, lanes):
        return grad_ref[:, half, :, lanes].reshape(group_rows, HD)

    copies = load_chunks(pieces, kvs, sems)
    dkv[...] = jnp.zeros_like(dkv)
    for copy in copies:
        copy.wait()

    def half_body(half, carry):
        query_pos, query_start, last_doc = query_masks(info_ref, half)
        for head in range(2):
            lanes = slice(head * HD, (head + 1) * HD)
            qt[head] = query_ref[half, :, lanes].astype(f32).T.astype(bf16)
            grad_t = grads_of(half, lanes).astype(f32).T
            gt[head] = grad_t.astype(bf16)
            delta[head] = jnp.sum(grad_t * full_ref[half, head], axis=0, keepdims=True)
            dqt[head] = jnp.zeros((HD, group_rows), f32)

        def step(chunks, masked):
            masks = [pair_mask(*chunk, query_pos, query_start) if masked else None for chunk in chunks]
            for head in range(2):
                lanes = slice(head * HD, (head + 1) * HD)
                total = total_ref[half, head]
                if not masked:
                    total = jnp.where(last_doc, -masked_score, total)
                query_total = dqt[head]
                for chunk, mask in zip(chunks, masks):
                    slot = slot_of(*chunk, y, co)
                    key_lanes = (*slot, slice(None), slice(0, HD))
                    value_lanes = (*slot, slice(None), slice(HD, 2 * HD))
                    keys = kvs[key_lanes]
                    scores = dot_plain(keys, qt[head])
                    if masked:
                        scores = jnp.where(mask, scores, masked_score)
                    probs = jnp.exp2(scores - total)
                    dkv[value_lanes] += dot_plain(probs.astype(bf16), grads_of(half, lanes))
                    prob_grad = dot_plain(kvs[value_lanes], gt[head])
                    low = (probs * (prob_grad - delta[head])).astype(bf16)
                    dkv[key_lanes] += dot_plain(low, query_ref[half, :, lanes])
                    query_total += dot_first(keys, low)
                dqt[head] = query_total

        count, chunk = open_steps(y, half)

        def open_body(number, inner):
            step((chunk(2 * number), chunk(2 * number + 1)), False)
            return inner

        lax.fori_loop(0, count // 2, open_body, 0)
        masked_count, masked_chunk = masked_steps(y, half)

        def masked_body(number, inner):
            step((masked_chunk(2 * number), masked_chunk(2 * number + 1)), True)
            return inner

        lax.fori_loop(0, masked_count // 2, masked_body, 0)
        for head in range(2):
            lanes = slice(head * HD, (head + 1) * HD)
            dq_ref[half, :, lanes] = dqt[head].T * score_scale
        return carry

    lax.fori_loop(0, 2, half_body, 0)

    def store(core):
        def store_body(number, carry):
            half, ring = number // 4, number % 4
            rows = (core, half, ring)
            kvs[(*rows, slice(None), slice(0, HD))] = (
                dkv[(*rows, slice(None), slice(0, HD))] * math.log(2.0)
            ).astype(bf16)
            kvs[(*rows, slice(None), slice(HD, 2 * HD))] = dkv[
                (*rows, slice(None), slice(HD, 2 * HD))
            ].astype(bf16)
            return carry

        lax.fori_loop(0, 8, store_body, 0)

    stores = [
        pltpu.make_async_copy(kvs.at[1], sent_hbm, sems.at[0]),
        pltpu.make_async_copy(kvs.at[0], kept_hbm, sems.at[1]),
    ]
    store(1)
    stores[0].start()
    store(0)
    stores[1].start()
    for copy in stores:
        copy.wait()


smem = pl.BlockSpec(memory_space=pltpu.SMEM)
vmem = pl.BlockSpec(memory_space=pltpu.VMEM)
hbm = pl.BlockSpec(memory_space=pltpu.HBM)


def in_hbm(*arrays):
    return [pltpu.with_memory_space_constraint(array, pltpu.HBM) for array in arrays]


PAIRS = 4 * 2 * group_rows * 9 * group_rows
CHUNKS = (2, 2, 4, group_rows, 2 * HD)


def attention_forward(info, queries, pieces):
    return pl.pallas_call(
        forward_kernel,
        name="attention_forward",
        out_shape=(
            jax.ShapeDtypeStruct((8, 2, half_blk, 2 * HD), bf16),
            jax.ShapeDtypeStruct((2, 2, HD, group_rows), f32),
            jax.ShapeDtypeStruct((2, 2, 1, group_rows), f32),
        ),
        in_specs=[smem, vmem] + [hbm] * 8,
        out_specs=[vmem] * 3,
        scratch_shapes=[
            pltpu.VMEM(CHUNKS, bf16),
            pltpu.SemaphoreType.DMA((8,)),
            pltpu.VMEM((2, HD, group_rows), bf16),
            pltpu.VMEM((2, 1, group_rows), f32),
            pltpu.VMEM((2, 1, group_rows), f32),
            pltpu.VMEM((2, HD, group_rows), f32),
        ],
        compiler_params=pltpu.CompilerParams(vmem_limit_bytes=24 << 20),
        cost_estimate=pl.CostEstimate(
            flops=2 * 2 * HD * PAIRS, bytes_accessed=8 << 20, transcendentals=PAIRS
        ),
    )(info, queries, *in_hbm(*pieces))


def attention_backward(info, queries, pieces, grads, full, total):
    return pl.pallas_call(
        backward_kernel,
        name="attention_backward",
        out_shape=(
            jax.ShapeDtypeStruct((2, group_rows, 2 * HD), f32),
            pltpu.HBM((2, 4, group_rows, 2 * HD), bf16),
            pltpu.HBM((2, 4, group_rows, 2 * HD), bf16),
        ),
        in_specs=[smem] + [vmem] * 4 + [hbm] * 8,
        out_specs=[vmem, hbm, hbm],
        scratch_shapes=[
            pltpu.VMEM(CHUNKS, bf16),
            pltpu.SemaphoreType.DMA((8,)),
            pltpu.VMEM((2, HD, group_rows), bf16),
            pltpu.VMEM((2, HD, group_rows), bf16),
            pltpu.VMEM((2, 1, group_rows), f32),
            pltpu.VMEM((2, HD, group_rows), f32),
            pltpu.VMEM(CHUNKS, f32),
        ],
        compiler_params=pltpu.CompilerParams(vmem_limit_bytes=36 << 20),
        cost_estimate=pl.CostEstimate(
            flops=5 * 2 * HD * PAIRS, bytes_accessed=12 << 20, transcendentals=PAIRS
        ),
    )(info, queries, grads, full, total, *in_hbm(*pieces))


OUT_ROWS, GATE_ROWS, DOWN_ROWS = HQ // 64, D // 64, FF // 64
BLOCKS = FF // D
GATE_AT = OUT_ROWS
UP_AT = GATE_AT + BLOCKS * GATE_ROWS
DOWN_AT = UP_AT + BLOCKS * GATE_ROWS
CHUNK_ROWS = DOWN_AT + DOWN_ROWS


def run_copies(copies):
    for copy in copies:
        copy.start()
    for copy in copies:
        copy.wait()


def collect_kernel(
    info_ref, query_ref, key_ref, value_ref, out_ref, gate_ref, up_ref, down_ref, gain_ref,
    own_ref, sent_ref, chunk_ref, sems,
):
    place = info_ref[0]
    numbers = iter(range(15))
    copies = []

    def copy(source, target):
        copies.append(pltpu.make_async_copy(source, target, sems.at[next(numbers)]))

    for target, head in ((sent_ref, info_ref[2]), (own_ref, info_ref[1])):
        lanes = pl.ds(pl.multiple_of(head * 2 * HD, 2 * HD), 2 * HD)
        copy(query_ref.at[:, lanes], target.at[:, pl.ds(0, 2 * HD)])
        lanes = pl.ds(pl.multiple_of(head * HD, HD), HD)
        copy(key_ref.at[:, lanes], target.at[:, pl.ds(2 * HD, HD)])
        copy(value_ref.at[:, lanes], target.at[:, pl.ds(3 * HD, HD)])
    copy(out_ref.at[place], chunk_ref.at[pl.ds(0, OUT_ROWS)])
    copy(down_ref.at[place], chunk_ref.at[pl.ds(DOWN_AT, DOWN_ROWS)])
    copy(gain_ref, chunk_ref.at[pl.ds(CHUNK_ROWS, 16)])
    for ref, start in ((gate_ref, GATE_AT), (up_ref, UP_AT)):
        for block in range(BLOCKS):
            copy(
                ref.at[place, :, pl.ds(block * D, D)],
                chunk_ref.at[pl.ds(start + block * GATE_ROWS, GATE_ROWS)],
            )
    run_copies(copies)


def collect(info, projections, shards, gains):
    gain_rows = jnp.pad(gains, (0, 16 * D - gains.shape[0])).reshape(16, D)
    return pl.pallas_call(
        collect_kernel,
        name="collect_chunk",
        out_shape=(
            jax.ShapeDtypeStruct((D // 2, 4 * HD), bf16),
            jax.ShapeDtypeStruct((D // 2, 4 * HD), bf16),
            jax.ShapeDtypeStruct((CHUNK_ROWS + 16, D), bf16),
        ),
        in_specs=[smem] + [hbm] * 8,
        out_specs=[vmem] * 3,
        scratch_shapes=[pltpu.SemaphoreType.DMA((15,))],
        compiler_params=pltpu.CompilerParams(vmem_limit_bytes=60 << 20),
    )(info, *in_hbm(*projections, *shards, gain_rows))


ROWS = 2 * group_rows


def as_lanes(column):
    return jnp.broadcast_to(column, (ROWS, HD)).T[0:1]


def as_rows(row):
    return jnp.broadcast_to(row, (HD, ROWS)).T


def turn(tensor, cosine, sine):
    return tensor * cosine + pltpu.roll(tensor, HD // 2, 1) * sine


def token_loads(left_hbm, right_hbm, tokens_ref, sems):
    columns = pl.ds(0, D // 2), pl.ds(D // 2, D // 2)
    loads = [
        pltpu.make_async_copy(left_hbm.at[zl], tokens_ref.at[:, zl, :, columns[0]], sems.at[zl])
        for zl in range(2)
    ]
    return loads + [
        pltpu.make_async_copy(right_hbm, tokens_ref.at[:, :, :, columns[1]], sems.at[2])
    ]


def project_kernel(
    info_ref, left_hbm, right_hbm, own_ref, got_ref, raw_ref, weight_ref, squares_ref,
    tokens_ref, sems,
):
    zh = info_ref[0]
    loads = token_loads(left_hbm, right_hbm, tokens_ref, sems)
    for load in loads:
        load.start()
    weight_ref[pl.ds(pl.multiple_of(zh * (D // 2), D // 2), D // 2)] = own_ref[...]
    weight_ref[pl.ds(pl.multiple_of((1 - zh) * (D // 2), D // 2), D // 2)] = got_ref[...]
    for load in loads:
        load.wait()
    for owner in range(8):
        raw = dot_plain(tokens_ref[owner // 2, owner % 2], weight_ref[...])
        for half in range(2):
            start = half * group_rows + owner * half_blk
            raw_ref[start : start + half_blk] = raw[half * half_blk : (half + 1) * half_blk]
    raw = raw_ref[:, : 3 * HD]
    squares = raw * raw
    query = jnp.sum(squares[:, :HD] + squares[:, HD : 2 * HD], axis=1, keepdims=True)
    key = jnp.sum(squares[:, 2 * HD :], axis=1, keepdims=True)
    sums = jnp.concatenate([as_lanes(query), as_lanes(key)])
    for owner in range(8):
        squares_ref[owner] = sums


def project(info, left, right, own_slice, got_slice):
    return pl.pallas_call(
        project_kernel,
        name="project",
        out_shape=(
            jax.ShapeDtypeStruct((ROWS, 4 * HD), f32),
            jax.ShapeDtypeStruct((D, 4 * HD), bf16),
            jax.ShapeDtypeStruct((8, 2, ROWS), f32),
        ),
        in_specs=[smem, hbm, hbm, vmem, vmem],
        out_specs=[vmem] * 3,
        scratch_shapes=[pltpu.VMEM((4, 2, BLK, D), bf16), pltpu.SemaphoreType.DMA((3,))],
        compiler_params=pltpu.CompilerParams(vmem_limit_bytes=32 << 20),
        cost_estimate=pl.CostEstimate(
            flops=2 * ROWS * D * 4 * HD, bytes_accessed=6 << 20, transcendentals=0
        ),
    )(info, *in_hbm(left, right), own_slice, got_slice)


def inverses(squares_ref):
    total = jnp.sum(squares_ref[...], axis=0)
    return (
        as_rows(lax.rsqrt(total[0:1] / HQ + epsilon)),
        as_rows(lax.rsqrt(total[1:2] / HK + epsilon)),
    )


def prepare_kernel(raw_ref, squares_ref, cos_ref, sin_ref, gain_ref, query_ref, kv_ref):
    query_inverse, key_inverse = inverses(squares_ref)
    cosine, sine = cos_ref[...], sin_ref[...]
    for head in range(3):
        lanes = slice(head * HD, (head + 1) * HD)
        inverse = query_inverse if head < 2 else key_inverse
        turned = turn(raw_ref[:, lanes] * inverse * gain_ref[:, lanes], cosine, sine)
        if head < 2:
            turned = (turned * log2_scale).astype(bf16)
            query_ref[0, :, lanes] = turned[:group_rows]
            query_ref[1, :, lanes] = turned[group_rows:]
        else:
            turned = turned.astype(bf16)
            values = raw_ref[:, 3 * HD :].astype(bf16)
            for half in range(2):
                rows = slice(half * group_rows, (half + 1) * group_rows)
                kv_ref[half, :, :HD] = turned[rows]
                kv_ref[half, :, HD:] = values[rows]


def prepare(raw, squares, tables, gain):
    return pl.pallas_call(
        prepare_kernel,
        name="prepare",
        out_shape=(
            jax.ShapeDtypeStruct((2, group_rows, 2 * HD), bf16),
            jax.ShapeDtypeStruct((2, group_rows, 2 * HD), bf16),
        ),
        in_specs=[vmem] * 5,
        out_specs=[vmem] * 2,
        compiler_params=pltpu.CompilerParams(vmem_limit_bytes=32 << 20),
        cost_estimate=pl.CostEstimate(flops=8 << 20, bytes_accessed=6 << 20, transcendentals=0),
    )(raw, squares, *tables, gain)


def turned_back(raw_ref, squares_ref, cos_ref, sin_ref, dq_ref, dkv_ref):
    query_inverse, key_inverse = inverses(squares_ref)
    cosine, sine = cos_ref[...], -sin_ref[...]
    for head in range(3):
        lanes = slice(head * HD, (head + 1) * HD)
        inverse = query_inverse if head < 2 else key_inverse
        grad = dq_ref[:, lanes] if head < 2 else dkv_ref[:, :HD]
        yield head, lanes, turn(grad, cosine, sine), raw_ref[:, lanes] * inverse, inverse


def means_kernel(raw_ref, squares_ref, cos_ref, sin_ref, gain_ref, dq_ref, dkv_ref, means_ref):
    products = []
    for _, lanes, upstream, normed, _ in turned_back(
        raw_ref, squares_ref, cos_ref, sin_ref, dq_ref, dkv_ref
    ):
        products.append(upstream * gain_ref[:, lanes] * normed)
    query = jnp.sum(products[0] + products[1], axis=1, keepdims=True)
    key = jnp.sum(products[2], axis=1, keepdims=True)
    means_ref[...] = jnp.concatenate([as_lanes(query), as_lanes(key)])


def raw_grad_kernel(
    info_ref, squares_ref, gain_ref, dkv_ref, means_ref, norm_gains_ref,
    raw_hbm, cos_hbm, sin_hbm, dq_hbm, weight_hbm, left_hbm, right_hbm,
    gains_ref, *refs,
):
    outs, held, (raw_ref, cos_ref, sin_ref, dq_ref, weight_ref, tokens_ref, low_ref, sems) = (
        refs[:6],
        refs[6:12],
        refs[12:],
    )
    loads = [
        pltpu.make_async_copy(source, target, sems.at[number])
        for number, (source, target) in enumerate(
            (
                (raw_hbm, raw_ref),
                (cos_hbm, cos_ref),
                (sin_hbm, sin_ref),
                (dq_hbm, dq_ref),
                (weight_hbm, weight_ref),
            )
        )
    ]
    loads += token_loads(left_hbm, right_hbm, tokens_ref, sems.at[pl.ds(12, 3)])
    for load in loads:
        load.start()
    stores = [
        pltpu.make_async_copy(source, target, sems.at[6 + number])
        for number, (source, target) in enumerate(zip(held, outs))
    ]
    heads_sent_ref, heads_kept_ref = held[:2]
    left_sent_ref, left_kept_ref, right_sent_ref, right_kept_ref = held[2:]
    for load in loads[:4]:
        load.wait()
    co, x_high, zl = info_ref[0], info_ref[1], info_ref[2]
    means = (as_rows(means_ref[0:1]) / HQ, as_rows(means_ref[1:2]) / HK)

    def place(lanes, low):
        for owner in range(8):
            for half in range(2):
                start = half * group_rows + owner * half_blk
                low_ref[owner, half * half_blk : (half + 1) * half_blk, lanes] = low[
                    start : start + half_blk
                ]

    gains_ref[...] = jnp.zeros((8, 4 * HD), f32)
    for head, lanes, upstream, normed, inverse in turned_back(
        raw_ref, squares_ref, cos_ref, sin_ref, dq_ref, dkv_ref
    ):
        mean = means[0] if head < 2 else means[1]
        place(lanes, (inverse * (upstream * gain_ref[:, lanes] - normed * mean)).astype(bf16))
        gains_ref[0:1, lanes] = jnp.sum(upstream * normed, axis=0, keepdims=True)
    place(slice(3 * HD, 4 * HD), dkv_ref[:, HD:].astype(bf16))
    for row in range(4):
        part = slice((row % 2) * 4 * HD, (row % 2 + 1) * 4 * HD)
        gains_ref[1 + row : 2 + row] = norm_gains_ref[row // 2 : row // 2 + 1, part]
    gains = gains_ref[...]
    high = gains.astype(bf16)
    heads_sent_ref[512:] = jnp.concatenate([high, (gains - high.astype(f32)).astype(bf16)])

    for load in loads[4:]:
        load.wait()
    low = low_ref[...].reshape(ROWS, 4 * HD)
    for part in range(2):
        rows = slice(part * 256, (part + 1) * 256)
        for ref, side in ((heads_sent_ref, 1 - co), (heads_kept_ref, co)):
            lanes = pl.ds(pl.multiple_of(part * 512 + side * 256, 256), 256)
            tokens = tokens_ref[:, :, :, lanes].reshape(ROWS, 256)
            ref[rows] = dot_first(tokens, low).astype(ref.dtype)
    stores[0].start()
    stores[1].start()

    for number in range(4):
        for ref, side in ((left_sent_ref, 1 - x_high), (left_kept_ref, x_high)):
            rows = low_ref[side * 4 + number]
            ref[number] = dot_second(rows, weight_ref[: D // 2]).astype(bf16)
        for ref, side in ((right_sent_ref, 1 - zl), (right_kept_ref, zl)):
            rows = low_ref[2 * number + side]
            ref[number] = dot_second(rows, weight_ref[D // 2 :]).astype(bf16)
    for store in stores[2:]:
        store.start()
    for store in stores:
        store.wait()


def projection_means(*operands):
    return pl.pallas_call(
        means_kernel,
        name="projection_means",
        out_shape=jax.ShapeDtypeStruct((2, ROWS), f32),
        in_specs=[vmem] * 7,
        out_specs=vmem,
        compiler_params=pltpu.CompilerParams(vmem_limit_bytes=32 << 20),
        cost_estimate=pl.CostEstimate(flops=8 << 20, bytes_accessed=6 << 20, transcendentals=0),
    )(*operands)


def projection_grads(
    info, raw, squares, cosine, sine, gain, dq, dkv, means, left, right, weight, norm_gains
):
    shapes = [((512 + 16, 4 * HD), bf16), ((512, 4 * HD), f32)] + [((4, BLK, D // 2), bf16)] * 4
    large = (raw, cosine, sine, dq, weight)
    return pl.pallas_call(
        raw_grad_kernel,
        name="projection_grads",
        out_shape=[jax.ShapeDtypeStruct((8, 4 * HD), f32)]
        + [pltpu.HBM(shape, dtype) for shape, dtype in shapes],
        in_specs=[smem] + [vmem] * 5 + [hbm] * 7,
        out_specs=[vmem] + [hbm] * 6,
        scratch_shapes=[pltpu.VMEM(shape, dtype) for shape, dtype in shapes]
        + [pltpu.VMEM(array.shape, array.dtype) for array in large]
        + [
            pltpu.VMEM((4, 2, BLK, D), bf16),
            pltpu.VMEM((8, BLK, 4 * HD), bf16),
            pltpu.SemaphoreType.DMA((15,)),
        ],
        compiler_params=pltpu.CompilerParams(vmem_limit_bytes=40 << 20),
        cost_estimate=pl.CostEstimate(flops=4 << 30, bytes_accessed=16 << 20, transcendentals=0),
    )(info, squares, gain, dkv, means, norm_gains, *in_hbm(*large, left, right))


INNER_AT = 0
DOWN_LOW_AT = INNER_AT + FF // 2
ATT_AT = DOWN_LOW_AT + D
HIDDEN_AT = ATT_AT + HQ // 2
GATE_LOW_AT = HIDDEN_AT + D
UP_LOW_AT = GATE_LOW_AT + FF // 2
MIXED_LOW_AT = UP_LOW_AT + FF // 2
PACK = MIXED_LOW_AT + D


def rows_kernel(
    info_ref, att_ref, tokens_ref, cot_ref, attn_gain_ref, ffn_gain_ref,
    out_own, gate_own, up_own, down_own, mine, other,
    output_ref, own_hbm, sent_hbm, att_grad_ref, hidden_grad_ref, gain_grad_ref,
    own_ref, sent_ref, out_v, gate_v, up_v, down_v, gate_act, up_act, inner_ref, up_low_ref, hidden_ref, sems,
):
    zh, co = info_ref[0], info_ref[1]
    numbers = iter(range(22))

    def copy(source, target):
        return pltpu.make_async_copy(source, target, sems.at[next(numbers)])

    def pieces(own, rows_at, rows, scratch, blocks):
        copies = [copy(own, scratch.at[pl.ds(zh * 32, 32)])]
        for half, core in ((mine, co), (other, 1 - co)):
            at = (1 - zh) * 32 + core * 16
            for block in range(blocks):
                target = scratch.at[pl.ds(at, 16)]
                if blocks > 1:
                    target = scratch.at[pl.ds(at, 16), :, pl.ds(block * D, D)]
                copies.append(
                    copy(half.at[:, pl.ds(rows_at + block * rows, rows), :], target)
                )
        return copies

    out_copies = pieces(out_own, 0, OUT_ROWS, out_v, 1)
    gate_copies = pieces(gate_own, GATE_AT, GATE_ROWS, gate_v, BLOCKS)
    up_copies = pieces(up_own, UP_AT, GATE_ROWS, up_v, BLOCKS)
    down_copies = pieces(down_own, DOWN_AT, DOWN_ROWS, down_v, 1)
    for item in out_copies:
        item.start()

    def put(core, lanes, value):
        @pl.when(core == co)
        def _():
            own_ref[:, lanes] = value

        @pl.when(core != co)
        def _():
            sent_ref[:, lanes] = value

    def put_both(start, value):
        own_ref[:, start : start + D] = value
        sent_ref[:, start : start + D] = value

    for head in range(8):
        rows = att_ref[head].reshape(BLK, 2 * HD)
        inner_ref[:, head * 2 * HD : (head + 1) * 2 * HD] = rows
        start = ATT_AT + ((head // 4) * 2 + head % 2) * 2 * HD
        put((head // 2) % 2, slice(start, start + 2 * HD), rows)
    for item in out_copies:
        item.wait()
    for item in gate_copies + up_copies:
        item.start()
    attn_gain = attn_gain_ref[...]
    mixed = dot_plain(inner_ref[:, :HQ], out_v[...].reshape(HQ, D))
    hidden_grad_ref[...] = mixed
    attn_inverse = lax.rsqrt(jnp.mean(mixed * mixed, axis=-1, keepdims=True) + epsilon)
    hidden = tokens_ref[...].astype(f32) + mixed * attn_inverse * attn_gain
    hidden_ref[...] = hidden
    put_both(HIDDEN_AT, hidden.astype(bf16))
    for item in gate_copies + up_copies:
        item.wait()
    for item in down_copies:
        item.start()
    tile = 8 * DOWN_ROWS

    def act_body(step, carry):
        lanes = pl.ds(step * tile, tile)
        low = own_ref[:, HIDDEN_AT : HIDDEN_AT + D]
        gate = dot_plain(low, gate_v[:, :, lanes].reshape(D, tile))
        up = dot_plain(low, up_v[:, :, lanes].reshape(D, tile))
        gate_act[:, lanes] = gate
        up_act[:, lanes] = up
        inner = (gate * (1.0 / (1.0 + jnp.exp(-gate))) * up).astype(bf16)
        inner_ref[:, lanes] = inner
        column = (step // 4) * 2 + step % 2
        put((step // 2) % 2, pl.ds(pl.multiple_of(INNER_AT + column * tile, HD), tile), inner)
        return carry

    lax.fori_loop(0, FF // tile, act_body, 0)
    for item in down_copies:
        item.wait()
    ffn_gain = ffn_gain_ref[...]
    down = dot_plain(inner_ref[...], down_v[...].reshape(FF, D))
    ffn_inverse = lax.rsqrt(jnp.mean(down * down, axis=-1, keepdims=True) + epsilon)
    normed = down * ffn_inverse
    output_ref[...] = (hidden_ref[...] + normed * ffn_gain).astype(bf16)
    upstream = cot_ref[...].astype(f32)
    scaled = upstream * ffn_gain
    gain_grad_ref[1:2, :] = jnp.sum(upstream * normed, axis=0, keepdims=True)
    down_low = ffn_inverse * (scaled - normed * jnp.mean(scaled * normed, axis=-1, keepdims=True))
    put_both(DOWN_LOW_AT, down_low.astype(bf16))
    def back_body(step, carry):
        lanes = pl.ds(step * tile, tile)
        rows = down_v[pl.ds(step * 8, 8)].reshape(tile, D)
        inner_grad = dot_second(own_ref[:, DOWN_LOW_AT : DOWN_LOW_AT + D], rows)
        gate, up = gate_act[:, lanes], up_act[:, lanes]
        sigmoid = 1.0 / (1.0 + jnp.exp(-gate))
        gate_low = (inner_grad * up * sigmoid * (1.0 + gate * (1.0 - sigmoid))).astype(bf16)
        up_low = (inner_grad * (gate * sigmoid)).astype(bf16)
        column = (step % 4) * tile
        put(step // 4, pl.ds(pl.multiple_of(GATE_LOW_AT + column, HD), tile), gate_low)
        put(step // 4, pl.ds(pl.multiple_of(UP_LOW_AT + column, HD), tile), up_low)
        inner_ref[:, lanes] = gate_low
        up_low_ref[:, lanes] = up_low
        return carry

    lax.fori_loop(0, FF // tile, back_body, 0)
    mixed = hidden_grad_ref[...]
    attn_inverse = lax.rsqrt(jnp.mean(mixed * mixed, axis=-1, keepdims=True) + epsilon)
    normed = mixed * attn_inverse
    hidden_grad = (
        cot_ref[...].astype(f32)
        + dot_second(inner_ref[...], gate_v[...].reshape(D, FF))
        + dot_second(up_low_ref[...], up_v[...].reshape(D, FF))
    )
    scaled = hidden_grad * attn_gain_ref[...]
    gain_grad_ref[0:1, :] = jnp.sum(hidden_grad * normed, axis=0, keepdims=True)
    mixed_low = (
        attn_inverse * (scaled - normed * jnp.mean(scaled * normed, axis=-1, keepdims=True))
    ).astype(bf16)
    put_both(MIXED_LOW_AT, mixed_low)
    packs = [copy(sent_ref, sent_hbm), copy(own_ref, own_hbm)]
    for item in packs:
        item.start()
    hidden_grad_ref[...] = hidden_grad

    def grad_body(head, carry):
        rows = out_v[pl.ds(head * 8, 8)].reshape(2 * HD, D)
        mixed_low = own_ref[:, MIXED_LOW_AT : MIXED_LOW_AT + D]
        grad = dot_second(mixed_low, rows).astype(bf16)
        att_grad_ref[head] = grad.reshape(2, half_blk, 2 * HD)
        return carry

    lax.fori_loop(0, 8, grad_body, 0)
    for item in packs:
        item.wait()


def own_rows(info, attended, tokens, cotangent, attn_gain, ffn_gain, shards, mine, other):
    def shape(*dims, dtype=bf16):
        return jax.ShapeDtypeStruct(dims, dtype)

    return pl.pallas_call(
        rows_kernel,
        name="own_rows",
        out_shape=(
            shape(BLK, D),
            pltpu.HBM((BLK, PACK), bf16),
            pltpu.HBM((BLK, PACK), bf16),
            shape(8, 2, half_blk, 2 * HD),
            shape(BLK, D, dtype=f32),
            shape(2, D, dtype=f32),
        ),
        in_specs=[smem] + [vmem] * 5 + [hbm] * 6,
        out_specs=[vmem, hbm, hbm, vmem, vmem, vmem],
        scratch_shapes=[
            pltpu.VMEM((BLK, PACK), bf16),
            pltpu.VMEM((BLK, PACK), bf16),
            pltpu.VMEM((64, OUT_ROWS, D), bf16),
            pltpu.VMEM((64, GATE_ROWS, FF), bf16),
            pltpu.VMEM((64, GATE_ROWS, FF), bf16),
            pltpu.VMEM((64, DOWN_ROWS, D), bf16),
            pltpu.VMEM((BLK, FF), f32),
            pltpu.VMEM((BLK, FF), f32),
            pltpu.VMEM((BLK, FF), bf16),
            pltpu.VMEM((BLK, FF), bf16),
            pltpu.VMEM((BLK, D), f32),
            pltpu.SemaphoreType.DMA((22,)),
        ],
        compiler_params=pltpu.CompilerParams(vmem_limit_bytes=44 << 20),
        cost_estimate=pl.CostEstimate(
            flops=4 * BLK * (3 * D * FF + HQ * D),
            bytes_accessed=26 << 20,
            transcendentals=2 * BLK * FF,
        ),
    )(info, attended, tokens, cotangent, attn_gain, ffn_gain, *in_hbm(*shards, mine, other))


def wide_rows(array):
    return jnp.concatenate(
        [array[:, start : start + D] for start in range(0, array.shape[1], D)]
    )


def ring_place(bits):
    return bits[0] * 2 + (bits[0] ^ bits[1])


PRODUCTS = (
    (FF // 2, INNER_AT, D, DOWN_LOW_AT, "zB", "zA"),
    (D, HIDDEN_AT, FF // 2, GATE_LOW_AT, "x0", "x1"),
    (D, HIDDEN_AT, FF // 2, UP_LOW_AT, "x1", "x0"),
    (HQ // 2, ATT_AT, D, MIXED_LOW_AT, "zA", "zB"),
)


def product_places():
    places = []
    for *_, first_link, second_link in PRODUCTS:
        for first, second in ((1, 0), (1, 1), (0, 0), (0, 1)):
            bits = {
                first_link: link_bit(first_link) ^ first,
                second_link: link_bit(second_link) ^ second,
            }
            for part in range(2):
                if "zA" in bits:
                    places.append((bits["zB"] * 2 + bits["zA"]) * 2 + part)
                else:
                    places.append(part * 4 + ring_place((bits["x1"], bits["x0"])))
    return jnp.stack(places).astype(jnp.int32)


def products_kernel(places_ref, own_ref, got_ref, *refs):
    outs, (both, sems), lefts, scratch = refs[:8], refs[8:10], refs[10:13], refs[13:]
    lefts = dict(zip((INNER_AT, HIDDEN_AT, ATT_AT), lefts))
    run_copies(
        [
            pltpu.make_async_copy(ref, both.at[pl.ds(core * BLK, BLK)], sems.at[8 + core])
            for core, ref in enumerate((own_ref, got_ref))
        ]
    )
    copies = [
        pltpu.make_async_copy(held, out, sems.at[number])
        for number, (held, out) in enumerate(zip(scratch, outs))
    ]
    for left_at, left in lefts.items():
        columns = slice(left_at, left_at + left.shape[0])
        left[...] = both[:, columns].astype(f32).T.astype(bf16)
    for number, (rows, left_at, width, right_at, *_) in enumerate(PRODUCTS):
        left = lefts[left_at]
        eighth = rows // 8
        for part in range(2):
            out = scratch[2 * number + part]

            starts = [
                pl.multiple_of(places_ref[number * 8 + part * 4 + step] * eighth, eighth)
                for step in range(4)
            ]
            picked = jnp.concatenate([left[pl.ds(start, eighth)] for start in starts])
            out[...] = dot_plain(picked, both[:, right_at : right_at + width]).astype(bf16)
            copies[2 * number + part].start()
    for copy in copies:
        copy.wait()


def weight_products(own, got):
    flops = sum(2 * 2 * BLK * rows * width for rows, _, width, *_ in PRODUCTS)
    return pl.pallas_call(
        products_kernel,
        name="weight_products",
        out_shape=[
            pltpu.HBM((rows // 2, width), bf16)
            for rows, _, width, *_ in PRODUCTS
            for _ in range(2)
        ],
        in_specs=[smem, hbm, hbm],
        out_specs=[hbm] * 8,
        scratch_shapes=[
            pltpu.VMEM((2 * BLK, PACK), bf16),
            pltpu.SemaphoreType.DMA((10,)),
            pltpu.VMEM((FF // 2, 2 * BLK), bf16),
            pltpu.VMEM((D, 2 * BLK), bf16),
            pltpu.VMEM((HQ // 2, 2 * BLK), bf16),
        ]
        + [
            pltpu.VMEM((rows // 2, width), bf16)
            for rows, _, width, *_ in PRODUCTS
            for _ in range(2)
        ],
        compiler_params=pltpu.CompilerParams(vmem_limit_bytes=40 << 20),
        cost_estimate=pl.CostEstimate(flops=flops, bytes_accessed=16 << 20, transcendentals=0),
    )(product_places(), *in_hbm(own, got))


def place_kernel(core_ref, chunk_ref, *refs):
    gate_ref, up_ref, down_ref, out_ref = refs[-4:]
    for y in range(4):
        for part in range(2):
            chunk = chunk_ref[y, 0, part]
            start = (2 * y + part) * GATE_ROWS
            rows = slice(start, start + GATE_ROWS)
            gate_ref[rows, :D] = chunk[:16].astype(f32)
            gate_ref[rows, D:] = chunk[16:32, : D // 2].astype(f32)
            up_ref[rows, : D // 2] = chunk[16:32, D // 2 :].astype(f32)
            up_ref[rows, D // 2 :] = chunk[32:48].astype(f32)
            down_ref[part, y] = chunk[48:72].astype(f32)
            out_ref[part, y] = chunk[72:].astype(f32)


def place_rows(core, chunks, earlier):
    def columns(x, core):
        return (x, core[0])

    def rows(x, core):
        return (core[0], 0, x, 0)

    return pl.pallas_call(
        place_kernel,
        name="place_rows",
        out_shape=(
            jax.ShapeDtypeStruct((D // 2, FF), f32),
            jax.ShapeDtypeStruct((D // 2, FF), f32),
            jax.ShapeDtypeStruct((4, 4, 4 * 24, D), f32),
            jax.ShapeDtypeStruct((4, 4, 4 * 16, D), f32),
        ),
        grid_spec=pltpu.PrefetchScalarGridSpec(
            num_scalar_prefetch=1,
            grid=(4,),
            in_specs=[pl.BlockSpec((4, 1, 2, 88, D), lambda x, core: (0, x, 0, 0, 0))]
            + [hbm] * len(earlier),
            out_specs=[
                pl.BlockSpec((D // 8, FF // 2), columns),
                pl.BlockSpec((D // 8, FF // 2), columns),
                pl.BlockSpec((2, 4, 24, D), rows),
                pl.BlockSpec((2, 4, 16, D), rows),
            ],
        ),
        input_output_aliases={2 + number: number for number in range(len(earlier))},
        compiler_params=pltpu.CompilerParams(vmem_limit_bytes=32 << 20),
        cost_estimate=pl.CostEstimate(flops=3 << 20, bytes_accessed=18 << 20, transcendentals=0),
    )(core, chunks, *earlier)


def place_heads_kernel(core_ref, query_chunk_ref, rest_chunk_ref, *refs):
    query_ref, key_ref, value_ref = refs[-3:]
    for owner in range(8):
        query = query_chunk_ref[owner // 2, 0, owner % 2, :64].astype(f32)
        rest = rest_chunk_ref[0, owner // 2, owner % 2, :64].astype(f32)
        query_ref[:, owner * 2 * HD : (owner + 1) * 2 * HD] = query
        key_ref[:, owner * HD : (owner + 1) * HD] = rest[:, :HD]
        value_ref[:, owner * HD : (owner + 1) * HD] = rest[:, HD:]


def place_heads(core, query, rest, earlier):
    def rows(y, core):
        return (core[0] * 4 + y, 0)

    return pl.pallas_call(
        place_heads_kernel,
        name="place_heads",
        out_shape=(
            jax.ShapeDtypeStruct((D // 2, HQ), f32),
            jax.ShapeDtypeStruct((D // 2, HK), f32),
            jax.ShapeDtypeStruct((D // 2, HK), f32),
        ),
        grid_spec=pltpu.PrefetchScalarGridSpec(
            num_scalar_prefetch=1,
            grid=(4,),
            in_specs=[
                pl.BlockSpec((4, 1, 2, 80, 2 * HD), lambda y, core: (0, y, 0, 0, 0)),
                pl.BlockSpec((1, 4, 2, 80, 2 * HD), lambda y, core: (y, 0, 0, 0, 0)),
            ]
            + [hbm] * len(earlier),
            out_specs=[
                pl.BlockSpec((64, HQ), rows),
                pl.BlockSpec((64, HK), rows),
                pl.BlockSpec((64, HK), rows),
            ],
        ),
        input_output_aliases={3 + number: number for number in range(len(earlier))},
        compiler_params=pltpu.CompilerParams(vmem_limit_bytes=32 << 20),
        cost_estimate=pl.CostEstimate(flops=1 << 20, bytes_accessed=6 << 20, transcendentals=0),
    )(core, query, rest, *earlier)


def per_device(
    tokens,
    doc_lengths,
    query_weight,
    key_weight,
    value_weight,
    out_weight,
    gate_weight,
    up_weight,
    down_weight,
    query_gain,
    key_gain,
    attn_gain,
    ffn_gain,
    cotangent,
):
    y, x, zl, co, zh = (lax.axis_index(name) for name in ("y", "x", "zl", "co", "zh"))
    head = x * 2 + zl
    lengths = doc_lengths[0]
    first_end = lengths[0]
    second_end = lengths[0] + lengths[1]
    info = jnp.stack([y, co, first_end, second_end]).astype(jnp.int32)
    source = tokens[0]

    gains = jnp.concatenate([query_gain, key_gain, attn_gain, ffn_gain])
    shards = (
        out_weight.reshape(32, OUT_ROWS, D),
        gate_weight.reshape(32, GATE_ROWS, FF),
        up_weight.reshape(32, GATE_ROWS, FF),
        down_weight.reshape(32, DOWN_ROWS, D),
    )
    places = jnp.stack([co * 16 + y * 4 + x, head, x * 2 + 1 - zl]).astype(jnp.int32)
    own_slice, sent_slice, weight_chunk = collect(
        places,
        (query_weight, key_weight, value_weight),
        shards,
        gains,
    )
    got_slice = across(sent_slice, "zB")
    weight_chunk = across(weight_chunk, "zB")
    left_tokens, right_tokens = source[None, :, : D // 2], source[None, :, D // 2 :]
    for left_link, right_link in (("x0", "zl"), ("x1", "x0"), ("zl", "x1")):
        left_tokens = double(left_tokens, left_link)
        right_tokens = double(right_tokens, right_link)
    left_tokens = left_tokens.reshape(2, 4, BLK, D // 2)
    right_tokens = right_tokens.reshape(4, 2, BLK, D // 2)
    mine_weights = lax.all_gather(weight_chunk[:CHUNK_ROWS], ("y", "x"), axis=0, tiled=False)
    other_gains = weight_chunk[CHUNK_ROWS:].reshape(-1)[: gains.shape[0]]

    def whole_gain(start, size):
        own = gains[start : start + size]
        got = other_gains[start : start + size]
        return jnp.where(zh == 0, jnp.concatenate([own, got]), jnp.concatenate([got, own]))

    query_scale = lax.dynamic_slice_in_dim(whole_gain(0, 1024), head * 2 * HD, 2 * HD).astype(f32)
    key_scale = lax.dynamic_slice_in_dim(whole_gain(1024, 512), head * HD, HD).astype(f32)
    attn_scale = whole_gain(1536, 512)
    ffn_scale = whole_gain(2048, 512)

    head_gain = jnp.concatenate([query_scale, key_scale])[None]

    index = jnp.arange(group_rows, dtype=jnp.int32)
    positions = jnp.concatenate(
        [half_positions(index, y, co, 0), half_positions(index, y, co, 1)]
    )
    doc_start = jnp.where(
        positions >= second_end, second_end, jnp.where(positions >= first_end, first_end, 0)
    )
    frequency = jnp.power(
        f32(rope_base), -jnp.arange(HD // 2, dtype=f32) * (2.0 / HD)
    )
    angles = (positions - doc_start).astype(f32)[:, None] * frequency[None, :]
    cosine, sine_table = jnp.cos(angles), jnp.sin(angles)
    tables = (
        jnp.concatenate([cosine, cosine], axis=1),
        jnp.concatenate([-sine_table, sine_table], axis=1),
    )

    raw, head_weight, squares = project(
        zh[None].astype(jnp.int32), left_tokens, right_tokens, own_slice, got_slice
    )
    squares = exchange(squares, HEAD_AXES)
    queries, kv = prepare(raw, squares, tables, head_gain)
    pairs = [
        jnp.stack([kv[half], across(kv[half], first)]) for half, first in enumerate(("y0", "y1"))
    ]
    pieces = [
        piece
        for pair, second in zip(pairs, ("y1", "y0"))
        for piece in (pair, across(pair, second))
    ]
    pieces += [across(piece, "co") for piece in pieces]
    pieces, mine_weights = lax.optimization_barrier((pieces, mine_weights))
    other_weights = across(mine_weights, "co")

    attended_low, attended_full, log_total = attention_forward(info, queries, pieces)
    attended_low = exchange(attended_low, HEAD_AXES)
    (
        output,
        own_pack,
        sent_pack,
        attended_grad,
        hidden_grad,
        norm_gain_grads,
    ) = own_rows(
        jnp.stack([zh, co]).astype(jnp.int32),
        attended_low,
        source,
        cotangent[0],
        attn_scale.astype(f32)[None],
        ffn_scale.astype(f32)[None],
        shards,
        mine_weights,
        other_weights,
    )

    grads = exchange(attended_grad, HEAD_AXES)

    products = weight_products(own_pack, across(sent_pack, "co"))
    sent_parts, rest_parts = products[0::2], products[1::2]
    grads, sent_parts = lax.optimization_barrier((grads, sent_parts))
    got_parts = [
        across(sent, first_link)
        for sent, (*_, first_link, _) in zip(sent_parts, PRODUCTS)
    ]

    query_grad, sent, kept = attention_backward(
        info, queries, pieces, grads, attended_full, log_total
    )
    stage = lax.optimization_barrier
    own_core, other_core = co[None].astype(jnp.int32), (1 - co)[None].astype(jnp.int32)

    sent, got_parts = stage((sent, got_parts))
    got = across(sent, "co")
    second_sent = [
        (rest[rest.shape[0] // 2 :].astype(f32) + part[rest.shape[0] // 2 :].astype(f32)).astype(
            bf16
        )
        for rest, part in zip(rest_parts, got_parts)
    ]
    got, second_sent = stage((got, second_sent))
    orders = (("y1", "y0"), ("y0", "y1"))
    kv_got = [
        across((kept[half, 2:].astype(f32) + got[half, 2:].astype(f32)).astype(bf16), first)
        for half, (first, _) in enumerate(orders)
    ]
    second_got = [
        across(part, second_link) for part, (*_, second_link) in zip(second_sent, PRODUCTS)
    ]

    def second_sum(number, arrived):
        rest, part = rest_parts[number], got_parts[number]
        middle = rest.shape[0] // 2
        kept_part = rest[:middle].astype(f32) + part[:middle].astype(f32)
        return (kept_part + arrived.astype(f32)).astype(bf16)

    kv_got = stage(kv_got)
    kv_both = [
        kept[half, :2].astype(f32) + got[half, :2].astype(f32) + kv_got[half].astype(f32)
        for half in range(2)
    ]
    kv_got = [
        across(kv_both[half][1].astype(bf16), second) for half, (_, second) in enumerate(orders)
    ]
    kv_grad = jnp.concatenate(
        [both[0] + more.astype(f32) for both, more in zip(kv_both, kv_got)]
    )
    operands = (
        raw, squares, *tables, head_gain, query_grad.reshape(ROWS, 2 * HD), kv_grad,
    )
    means = projection_means(*operands)
    second_got, _ = stage((second_got, means))
    down_got, gate_got, up_got, out_got = second_got
    act_part = exchange(
        jnp.concatenate([second_sum(1, gate_got), second_sum(2, up_got)], axis=1).reshape(
            16, 16, FF
        ),
        ("zh", "y", "zl"),
    )
    for link in ("x0", "x1", "zA"):
        means = means + across(means, link)
    means, act_part, down_got, out_got = stage((means, act_part, down_got, out_got))
    rest_part = exchange(
        jnp.concatenate(
            [second_sum(0, down_got).reshape(16, 24, D), second_sum(3, out_got).reshape(16, 16, D)],
            axis=1,
        ),
        ("y", "x"),
    )

    x_high, x_low = x // 2, x % 2
    gain_sums, heads_sent, heads_kept, left_sent, left, right_sent, right = projection_grads(
        jnp.stack([co, x_high, zl]).astype(jnp.int32),
        *operands,
        means,
        left_tokens,
        right_tokens,
        head_weight,
        norm_gain_grads,
    )

    def pick(array, number):
        return lax.dynamic_index_in_dim(array, number, 0, keepdims=False)

    def pass_on(both, link, number):
        return pick(both, number).astype(f32), across(pick(both, 1 - number), link)

    def halves(both):
        return both.astype(bf16).reshape(2, both.shape[0] // 2, *both.shape[1:])

    def take_gains(got, kept, sums):
        more = got[-16:].astype(f32)
        return (kept + got[:-16].astype(f32)).astype(bf16), sums + more[:8] + more[8:]

    def with_gains(array, sums):
        return jnp.concatenate([array, high_low(sums).reshape(16, 4 * HD)])

    def halve_heads(chunk, sums, link):
        bit = link_bit(link)
        chunk = chunk.reshape(2, chunk.shape[0] // 2, 4 * HD)
        kept = pick(chunk, bit).astype(f32)
        return kept, across(with_gains(pick(chunk, 1 - bit), sums), link)

    heads_got = across(heads_sent, "co")
    left_got = across(left_sent, "x1")
    right_got = across(right_sent, "zA")
    rest_part, heads_got = stage((rest_part, heads_got))
    chunk = jnp.concatenate(
        [
            wide_rows(jnp.sum(act_part.astype(f32), axis=0).astype(bf16)),
            jnp.sum(rest_part.astype(f32), axis=0).astype(bf16),
        ]
    )
    chunk_got = across(chunk, "zA")
    def beside(start, stop, bit):
        mine, other = chunk[start:stop], chunk_got[start:stop]
        return jnp.where(bit == 0, jnp.stack([mine, other]), jnp.stack([other, mine]))

    chunks = lax.all_gather(
        jnp.concatenate([beside(0, 48, zl), beside(48, 88, link_bit("zA"))], axis=1),
        ("y", "x"),
        axis=0,
        tiled=False,
    ).reshape(4, 4, 2, 88, D)
    heads, gain_sums = take_gains(heads_got, heads_kept, gain_sums)
    heads = jnp.concatenate(
        [
            heads.reshape(8, 64, 4 * HD),
            jnp.broadcast_to(high_low(gain_sums).reshape(1, 16, 4 * HD), (8, 16, 4 * HD)),
        ],
        axis=1,
    )
    heads = exchange(heads, ("zh", "y"))
    left, left_got = pass_on(halves(left.astype(f32) + left_got.astype(f32)), "x0", x_low)
    right, right_got = pass_on(halves(right.astype(f32) + right_got.astype(f32)), "x1", x_high)
    heads, left_got, right_got = stage((heads, left_got, right_got))
    heads = jnp.sum(heads.astype(f32), axis=0)
    gain_sums = heads[64:72] + heads[72:]
    heads = jnp.concatenate([heads[:64].astype(bf16), high_low(gain_sums).reshape(16, 4 * HD)])
    heads = double(heads[None], "zl")
    head_query, head_rest = heads[:, :, : 2 * HD], heads[:, :, 2 * HD :]
    for query_link, rest_link in (("y0", "x0"), ("y1", "x1"), ("x0", "y0"), ("x1", "y1")):
        head_query, head_rest = double(head_query, query_link), double(head_rest, rest_link)
    head_query = head_query.reshape(4, 4, 2, 80, 2 * HD)
    head_rest = head_rest.reshape(4, 4, 2, 80, 2 * HD)
    left, left_got = pass_on(halves(left + left_got.astype(f32)), "zA", zl)
    right, right_got = pass_on(halves(right + right_got.astype(f32)), "x0", x_low)
    tokens_grad = hidden_grad + jnp.concatenate(
        [
            (left + left_got.astype(f32)).reshape(BLK, D // 2),
            (right + right_got.astype(f32)).reshape(BLK, D // 2),
        ],
        axis=1,
    )
    head_query, head_rest, tokens_grad, chunks = stage(
        (head_query, head_rest, tokens_grad, chunks)
    )
    other_chunks = across(chunks, "co")
    other_heads = across(head_query, "co"), across(head_rest, "co")
    placed = place_rows(own_core, chunks, ())
    placed_heads = place_heads(own_core, head_query, head_rest, ())
    gate_weight_grad, up_weight_grad, down_weight_grad, out_weight_grad = place_rows(
        other_core, other_chunks, placed
    )
    query_weight_grad, key_weight_grad, value_weight_grad = place_heads(
        other_core, *other_heads, placed_heads
    )
    down_weight_grad = down_weight_grad.reshape(FF // 2, D)
    out_weight_grad = out_weight_grad.reshape(HQ // 2, D)
    def gain_of(rows):
        return rows[..., 64, :].astype(f32) + rows[..., 72, :].astype(f32)

    query_gain_grad = gain_of(head_query[:, 0]).reshape(HQ)
    key_gain_grad = gain_of(head_rest[0])[..., :HD].reshape(HK)

    def norm_gains(rows):
        return jnp.sum(
            rows[:, :, 65:69].astype(f32) + rows[:, :, 73:77].astype(f32), axis=(0, 1)
        )

    norm_gain_grads = jnp.concatenate(
        [norm_gains(head_query[:, 0]), norm_gains(head_rest[0])], axis=1
    ).reshape(2, D)

    def own_gain(gain_grad):
        size = gain_grad.shape[0] // 2
        return lax.dynamic_slice_in_dim(gain_grad, zh * size, size)

    return (
        output[None],
        tokens_grad[None],
        query_weight_grad,
        key_weight_grad,
        value_weight_grad,
        out_weight_grad,
        gate_weight_grad,
        up_weight_grad,
        down_weight_grad,
        own_gain(query_gain_grad.reshape(HQ)),
        own_gain(key_gain_grad.reshape(HK)),
        own_gain(norm_gain_grads[0]),
        own_gain(norm_gain_grads[1]),
    )


def solution(mesh):
    fine = Mesh(mesh.devices.reshape(4, 4, 2, 2, 2), ("y", "x", "zl", "co", "zh"))
    rows = P("zh", TOKEN_AXES, None)
    weight = P("zh", None)
    gain = P("zh")
    return jax.shard_map(
        per_device,
        mesh=fine,
        in_specs=(rows, weight) + (weight,) * 7 + (gain,) * 4 + (rows,),
        out_specs=(rows, rows) + (weight,) * 7 + (gain,) * 4,
        check_vma=False,
    )
```
